32 devices in a mesh: fluid: 4 (over z), solid: 8 (over y, x, core).
Axes of the slice: x: 2, y: 2, z: 4, core: 2. Of those that a mesh axis runs over, the one named last changes fastest.
Arguments:
- pressure: float32 [32768, 128], P(('fluid', 'solid')), may hold values from -24 to 24
- face_owner: int32 [32768, 1], P(('fluid', 'solid')), may hold values from 0 to 31; in each aligned block of 1024 rows (0 to 1023, 1024 to 2047, ...) at most 80 rows name the same one
- face_element: int32 [32768], P(('fluid', 'solid')), may hold values from 0 to 1023
- shape_table: float32 [24, 128], replicated, may hold values from -0.5 to 0.5
- stiffness: float32 [24, 24, 32768], P(None, None, ('fluid', 'solid')), as said below
- connectivity: int32 [8, 32768], P(None, ('fluid', 'solid')), may hold values from 0 to 1151, as said below
- support: float32 [3, 32768], P(None, ('fluid', 'solid')), may hold values from 0.5 to 5
Outputs:
- displacement: float32 [3, 32768], P(None, ('fluid', 'solid'))
- face_motion: float32 [32768, 128], P(('fluid', 'solid'))
The draws below stay inside these ranges and needn't reach their ends.
Inputs may be any that keep to these rules, and one draw needn't show every extreme that they name: `face_owner`: in the rows of one device no owner is named by more than 80 faces, a bound that some block reaches. `connectivity`: an entry below 1024 names a node of the element's own partition; an entry j of 1024 or more names node j - 1024 of the next partition in the order of the index over fluid and solid together; elements of the last partition name their own nodes only. `stiffness`: each element's matrix is symmetric with a positive diagonal that exceeds the sum of magnitudes of the rest of its row.
All inputs are finite; a program needn't handle non-finite values.
Results may differ from the reference program's by a relative error of at most 0.0001.
Values sent between devices are 32-bit elements; how exact they have to be, the bound alone decides.
No kernel may reach another device: no remote copies, remote signals or barrier semaphores. Data moves between devices by JAX's collectives and lax.ppermute only.
A program may use at most 64 MiB of HBM per device.

```python
import math
import jax
import jax.numpy as jnp
import numpy as np
from jax import lax

QP = 128
DOF = 24
ITERS = 3
F_DEV = 1024
E_DEV = 1024
NODE_DEV = 1024
SHARED = 128
CAP = 80
FACES = 32768
ELEMS = 32768
NODES = 32768
DEVICES = 32


def draw_stiffness(key, part):
    key = jax.random.fold_in(key, 23)
    first, second, third = jax.random.split(key, 3)
    rough = jax.random.uniform(first, (24, 24, ELEMS), jnp.float32, -1.0, 1.0)
    off_diagonal = 0.175 * (rough + jnp.transpose(rough, (1, 0, 2)))
    diagonal = jax.random.uniform(second, (24, 1, ELEMS), jnp.float32, 8.1, 8.6)
    lower, upper = (0.05, 0.5)
    scales = jnp.exp(jax.random.uniform(third, (ELEMS,), jnp.float32, math.log(lower), math.log(upper)))
    identity = jnp.arange(24)[:, None] == jnp.arange(24)[None, :]
    matrices = jnp.where(identity[:, :, None], diagonal, off_diagonal)
    return (scales[None, None, :] * matrices).astype(jnp.float32)


def draw_connectivity(key, part):
    key = jax.random.fold_in(key, 11)
    owner_of = jnp.arange(ELEMS, dtype=jnp.int32) // E_DEV
    final_owner = ELEMS // E_DEV - 1
    upper = jnp.where(owner_of == final_owner, NODE_DEV, NODE_DEV + SHARED).astype(jnp.int32)
    return jax.random.randint(key, (8, ELEMS), 0, upper[None, :]).astype(jnp.int32)


def plant(drawn, stream_key, least, top_value):
    longest = drawn.shape.index(max(drawn.shape))
    spots = []
    for shift in (0, 1):
        where = [jax.random.randint(jax.random.fold_in(stream_key, axis), (), 0, length) for axis, length in enumerate(drawn.shape)]
        where[longest] = (where[longest] + shift) % drawn.shape[longest]
        spots.append(tuple(where))
    return drawn.at[spots[0]].set(least).at[spots[1]].set(top_value)


def block_scale(rng, extent, shards, low, largest):
    factor_of = 1.0
    for dim, parts in shards:
        heights = jax.random.uniform(jax.random.fold_in(jax.random.fold_in(rng, 6), dim), (parts,), jnp.float32, low / len(shards), largest / len(shards))
        factor_of = factor_of * jnp.repeat(jnp.exp(heights), extent[dim] // parts).reshape((-1,) + (1,) * (len(extent) - 1 - dim))
    return factor_of


def assign_block(stream_key, own, number, rows, count, top, limit, skew):
    ranking = jax.random.permutation(stream_key, count)
    heavy_load, ordinary = shares(count, rows * top, limit, skew, True), shares(count, rows * top, limit, skew, False)
    places = jnp.arange(count)

    def named(lengths, turn):
        used = int((lengths > 0).sum())
        fixed = max(1, used // 4)
        moved = fixed + (places - fixed + turn * (used - fixed)) % max(1, count - fixed)
        return jnp.zeros((count,), jnp.int32).at[ranking[jnp.where(places < fixed, places, moved)]].set(jnp.asarray(lengths, jnp.int32))

    lengths = jnp.where(number % 4 == 0, named(heavy_load, number // 4), named(ordinary, number - number // 4 - 1))
    mixed = jax.random.permutation(jax.random.fold_in(own, 3), count)
    donor, receiver = mixed[0:count // 2 * 2:2], mixed[1:count // 2 * 2:2]
    margin = jnp.minimum(lengths[donor] - 1, limit - lengths[receiver]) // 2
    margin = jnp.where((donor == ranking[0]) | (receiver == ranking[0]) | (lengths[receiver] == 0), 0, jnp.maximum(margin, 0))
    moved = jax.random.randint(jax.random.fold_in(own, 4), (count // 2,), 0, 1 << 20) % (margin + 1)
    lengths = lengths.at[donor].add(-moved).at[receiver].add(moved)
    items = jnp.searchsorted(jnp.cumsum(lengths), jnp.arange(rows * top), side="right").astype(jnp.int32)
    listing = items.reshape(top, rows).T
    listing = listing[jax.random.permutation(jax.random.fold_in(own, 1), rows)]
    turn = jax.random.randint(jax.random.fold_in(own, 2), (rows, 1), 0, top)
    return jnp.take_along_axis(listing, (jnp.arange(top)[None, :] + turn) % top, axis=1)


def shares(number_of, total, limit, lean, full):
    weights = [(1 << 20) // math.isqrt(rank ** lean) + 1 for rank in range(1, number_of + 1)]
    largest = limit if full else min(limit, max(-(-total // number_of), total * weights[0] // sum(weights)))
    least = 1 if total - largest >= number_of - 1 else 0
    counts, rest = [largest] + [least] * (number_of - 1), total - largest - least * (number_of - 1)
    while rest > 0:
        free = [i for i in range(1, number_of) if counts[i] < largest] or [i for i in range(1, number_of) if counts[i] < limit]
        pool, budget = sum([weights[i] for i in free]), rest
        for i in free:
            more = min(limit - counts[i], max(1, budget * weights[i] // pool), rest)
            counts[i] = counts[i] + more
            rest = rest - more
    return np.array(counts)


def noise(key, extent, width, bound, shards=(), kind=jnp.bfloat16):
    gain = block_scale(key, extent, shards, -0.22, 0.18) if shards else 1.0
    values = jax.random.normal(key, extent, jnp.float32) * width * gain
    return jnp.minimum(jnp.maximum(values, -bound), bound).astype(kind)


def setup_inputs(seed: int = 0) -> dict:
    streams_of = jax.random.split(jax.random.key(seed), 8)
    pressure = noise(streams_of[0], (FACES, QP), 4.0, 24.0, ((0, 32),), jnp.float32)
    face_owner_keys = jax.random.split(jax.random.fold_in(streams_of[1], 1), FACES // F_DEV)
    face_owner_turns = jax.random.permutation(jax.random.fold_in(streams_of[1], 3), FACES // F_DEV)
    face_owner = jax.vmap(lambda own, number: assign_block(jax.random.fold_in(streams_of[1], 2), own, number, F_DEV, DEVICES, 1, CAP, 2))(face_owner_keys, face_owner_turns).reshape((FACES, 1))
    face_element = plant(jax.random.randint(streams_of[2], (FACES,), 0, E_DEV), jax.random.fold_in(streams_of[2], 1), 0, E_DEV - 1).astype(jnp.int32)
    shape_table = noise(streams_of[3], (DOF, QP), QP ** -0.5, 0.5, (), jnp.float32)
    stiffness = draw_stiffness(jax.random.fold_in(streams_of[7], 71), 0)
    connectivity = draw_connectivity(jax.random.fold_in(streams_of[7], 71), 0)
    support = jnp.clip(jnp.exp(math.log(5.0) - 2.3025851 * jax.random.uniform(streams_of[6], (3, NODES), jnp.float32) ** block_scale(streams_of[6], (3, NODES), ((1, 32),), -0.2, 0.2)), 0.5, 5.0)
    return dict(pressure=pressure, face_owner=face_owner, face_element=face_element, shape_table=shape_table, stiffness=stiffness, connectivity=connectivity, support=support)


def gather_values(field, node_ids):
    return field[:, node_ids].reshape(24, node_ids.shape[1])


def assemble_terms(terms, node_ids):
    totals = jnp.zeros((3, NODES), jnp.float32)
    return totals.at[:, node_ids.reshape(-1)].add(terms.reshape(3, -1))


def apply_operator(field, stiffness, node_ids, support):
    element_disp = gather_values(field, node_ids)
    forces = jnp.einsum("abe,be->ae", stiffness, element_disp, precision=lax.Precision.HIGHEST)
    return assemble_terms(forces, node_ids) + support * field


def reference(pressure, face_owner, face_element, shape_table, stiffness, connectivity, support):
    owner_of = jnp.arange(ELEMS, dtype=jnp.int32) // E_DEV
    node_ids = owner_of[None, :] * NODE_DEV + connectivity
    element_of = face_owner[:, 0] * E_DEV + face_element
    projected = lax.dot_general(pressure, shape_table, (((1,), (1,)), ((), ())),
                                precision=lax.Precision.HIGHEST, preferred_element_type=jnp.float32)
    element_loads = jax.ops.segment_sum(projected, element_of, num_segments=ELEMS).T
    nodal_loads = assemble_terms(element_loads, node_ids)
    displacement = jnp.zeros((3, NODES), jnp.float32)
    residual = nodal_loads
    direction = nodal_loads
    norm_now = jnp.sum(residual * residual)
    for iteration in range(ITERS):
        image = apply_operator(direction, stiffness, node_ids, support)
        step_size = norm_now / jnp.sum(direction * image)
        displacement = displacement + step_size * direction
        residual = residual - step_size * image
        if iteration + 1 < ITERS:
            norm_next = jnp.sum(residual * residual)
            direction = residual + (norm_next / norm_now) * direction
            norm_now = norm_next
    final_values = gather_values(displacement, node_ids)
    picked = final_values[:, element_of]
    face_motion = lax.dot_general(picked, shape_table, (((0,), (0,)), ((), ())),
                                  precision=lax.Precision.HIGHEST, preferred_element_type=jnp.float32)
    return displacement, face_motion
```

```python
import functools

import jax
import jax.numpy as jnp
from jax import lax
from jax.experimental import pallas as pl
from jax.experimental.pallas import tpu as pltpu
from jax.sharding import PartitionSpec as P

AXES = ("fluid", "solid")
DOF = 24
CORNERS = 8
GROUPS = 5
ROWS_PER_FIELD = 8
WIDE = 256
VMEM_BYTES = 24 * 1024 * 1024
F32 = jnp.float32
BF16 = jnp.bfloat16


def iota(shape, axis):
    return lax.broadcasted_iota(jnp.int32, shape, axis)


def onehot(mask):
    return jnp.where(mask, 1.0, 0.0).astype(BF16)


def split(value):
    high = value.astype(BF16)
    return high, (value - high.astype(F32)).astype(BF16)


def dot_nt(left, right):
    return lax.dot_general(left, right, (((1,), (1,)), ((), ())), preferred_element_type=F32)


def dot_nn(left, right):
    return lax.dot_general(left, right, (((1,), (0,)), ((), ())), preferred_element_type=F32)


def take_lanes(table, index):
    return jnp.take_along_axis(table, index, axis=1, mode="promise_in_bounds")


def group_rows(group, sections, tail):
    kept = [jnp.where(group == i, section, 0.0) for i, section in enumerate(sections)]
    return jnp.concatenate(kept + [tail], axis=0)


def gather_corners(field, connectivity):
    elements = connectivity.shape[1]
    rows = {}
    for c in range(3):
        for h in range(9):
            row = field[c * ROWS_PER_FIELD + h // 2:c * ROWS_PER_FIELD + h // 2 + 1, (h % 2) * 128:(h % 2) * 128 + 128]
            rows[c, h] = jnp.broadcast_to(row, (CORNERS, 128))
    parts = [[], [], []]
    for start in range(0, elements, 128):
        index = connectivity[:, start:start + 128]
        low, high = index & 127, index >> 7
        masks = [high == h for h in range(9)]
        for c in range(3):
            total = jnp.zeros((CORNERS, 128), F32)
            for h in range(9):
                total = jnp.where(masks[h], take_lanes(rows[c, h], low), total)
            parts[c].append(total)
    return [jnp.concatenate(part, axis=1) for part in parts]


def assemble(terms, connectivity):
    elements = connectivity.shape[1]
    high, low = connectivity >> 8, connectivity & 255
    upper = terms.astype(BF16).astype(F32)
    lower = terms - upper
    total = jnp.zeros((2 * DOF, WIDE), F32)
    for k in range(CORNERS):
        mask = iota((ROWS_PER_FIELD, elements), 0) == high[k:k + 1]
        pieces = [
            jnp.where(mask, part[c * CORNERS + k:c * CORNERS + k + 1], 0.0)
            for part in (upper, lower)
            for c in range(3)
        ]
        left = jnp.concatenate(pieces, axis=0).astype(BF16)
        right = onehot(iota((WIDE, elements), 0) == low[k:k + 1])
        total = total + dot_nt(left, right)
    return total[:DOF] + total[DOF:]


def matvec(stiffness, values):
    elements = stiffness.shape[2]
    parts = []
    for start in range(0, elements, 128):
        total = jnp.zeros((DOF, 128), F32)
        for b in range(DOF):
            total = total + stiffness[b, :, start:start + 128] * values[b // 8][b % 8:b % 8 + 1, start:start + 128]
        parts.append(total)
    return jnp.concatenate(parts, axis=1)


def rim_rows(field, h):
    return [field[c * ROWS_PER_FIELD + h:c * ROWS_PER_FIELD + h + 1, :128] for c in range(3)]


def put_ends(partial, odd, own_rows, swap_a_ref, swap_b_ref):
    first = jnp.concatenate(rim_rows(partial, 0) + [jnp.zeros((5, 128), F32)], axis=0)
    over = jnp.concatenate(rim_rows(partial, own_rows) + [jnp.zeros((5, 128), F32)], axis=0)
    swap_a_ref[...] = jnp.where(odd, first, over)
    swap_b_ref[...] = jnp.where(odd, over, first)


def add_ends(partial, odd, own_rows, swap_a, swap_b):
    before = jnp.where(odd, swap_a, swap_b)
    after = jnp.where(odd, swap_b, swap_a)
    pad = jnp.zeros((1, WIDE - 128), F32)
    none = jnp.zeros((1, WIDE), F32)
    rows = []
    for c in range(3):
        for h in range(ROWS_PER_FIELD):
            if h == 0:
                rows.append(jnp.concatenate([before[c:c + 1], pad], axis=1))
            elif h == own_rows:
                rows.append(jnp.concatenate([after[c:c + 1], pad], axis=1))
            else:
                rows.append(none)
    return partial + jnp.concatenate(rows, axis=0)


def own_mask(own_rows):
    return (iota((DOF, WIDE), 0) % ROWS_PER_FIELD) < own_rows


def as_field(rows, own_rows):
    pieces = []
    for c in range(3):
        pieces += [rows[c:c + 1, h * WIDE:(h + 1) * WIDE] for h in range(own_rows)]
        pieces.append(jnp.zeros((ROWS_PER_FIELD - own_rows, WIDE), F32))
    return jnp.concatenate(pieces, axis=0)


def send_kernel(devices, per, pressure_ref, owner_ref, element_ref, table_ref, support_ref, stiffness_ref,
                out_ref, place_ref, diagonal_ref, sems):
    copies = [
        pltpu.make_async_copy(
            stiffness_ref.at[pl.ds(8 * i, 8), pl.ds(8 * i, 8)], diagonal_ref.at[i], sems.at[i])
        for i in range(3)
    ]
    for copy in copies:
        copy.start()
    faces = pressure_ref.shape[0]
    target, element = owner_ref[...], element_ref[...]
    named = iota((devices, faces), 0) == target
    named16 = onehot(named)
    upto = onehot(iota((WIDE, WIDE), 0) <= iota((WIDE, WIDE), 1))
    before = jnp.zeros((devices, 1), F32)
    ranks = []
    for start in range(0, faces, WIDE):
        counts = dot_nn(named16[:, start:start + WIDE], upto) + before
        ranks.append(jnp.sum(jnp.where(named[:, start:start + WIDE], counts, 0.0), axis=0, keepdims=True))
        before = counts[:, WIDE - 1:]
    rank = jnp.concatenate(ranks, axis=1).astype(jnp.int32) - 1
    group = jnp.zeros_like(rank)
    for i in range(1, GROUPS):
        group = group + (rank >= i * per).astype(jnp.int32)
    place = target * per + rank - group * per
    place_ref[...] = jnp.concatenate([place, group, jnp.zeros((6, faces), jnp.int32)], axis=0)

    table = jnp.concatenate([table_ref[...]] * GROUPS + [jnp.zeros((8, table_ref.shape[1]), F32)], axis=0)
    table_high, table_low = split(table)
    rows_high, rows_low = split(pressure_ref[...])
    projected = dot_nt(
        jnp.concatenate([table_high, table_low, table_high], axis=1),
        jnp.concatenate([rows_high, rows_high, rows_low], axis=1),
    )
    codes = jnp.where(iota((8, faces), 0) == group, element.astype(F32), 0.0)
    spread = group_rows(group, [projected[i * DOF:(i + 1) * DOF] for i in range(GROUPS)], codes)
    spread_high, spread_low = split(spread)
    chosen = onehot(iota((devices * per, faces), 0) == place)
    sent = dot_nt(chosen, jnp.concatenate([spread_high, spread_low], axis=0))

    for copy in copies:
        copy.wait()
    trace = jnp.zeros((8, faces), F32)
    for i in range(3):
        for j in range(8):
            trace = trace + jnp.where(iota((8, faces), 0) == j, diagonal_ref[i, j], 0.0)
    trace = jnp.sum(trace) + jnp.sum(support_ref[...])
    out_ref[...] = jnp.where(iota((devices * per, 128), 1) == 125, trace, sent[:, :128] + sent[:, 128:])


def load_kernel(devices, per, odd_ref, rows_ref, connectivity_ref, support_ref,
                partial_ref, swap_a_ref, swap_b_ref, weight_ref, scale_ref, code_ref):
    nodes = support_ref.shape[1]
    own_rows = nodes // WIDE
    rows = rows_ref[...]
    arrived = rows.T
    codes = arrived[GROUPS * DOF:].astype(jnp.int32)
    code_ref[...] = codes
    slots = rows.shape[0]
    total = jnp.zeros((4 * 2 * DOF, WIDE), F32)
    for g in range(GROUPS):
        terms = arrived[g * DOF:(g + 1) * DOF]
        upper = terms.astype(BF16).astype(F32)
        both = jnp.concatenate([upper, terms - upper], axis=0)
        code = codes[g:g + 1]
        left = jnp.concatenate([jnp.where((code >> 8) == i, both, 0.0) for i in range(4)], axis=0).astype(BF16)
        right = onehot(iota((WIDE, slots), 0) == (code & 255))
        total = total + dot_nt(left, right)
    loads = jnp.concatenate(
        [total[i * 2 * DOF:i * 2 * DOF + DOF] + total[i * 2 * DOF + DOF:(i + 1) * 2 * DOF] for i in range(4)], axis=1)
    partial = assemble(loads, connectivity_ref[...])
    partial_ref[...] = partial
    put_ends(partial, odd_ref[0] == 1, own_rows, swap_a_ref, swap_b_ref)
    trace = jnp.sum(rows[:, 125:126]) * (1.0 / per)
    inverse = jnp.full((8, 128), 3.0 * nodes * devices, F32) / jnp.full((8, 128), trace, F32)
    scale_ref[...] = inverse
    weight = as_field(support_ref[...], own_rows) * inverse[:1, :1] - 1.0
    weight_ref[...] = jnp.where(own_mask(own_rows), weight, 0.0)


def product_kernel(own_rows, odd_ref, partial_ref, swap_a_in, swap_b_in, weight_ref, scale_ref, connectivity_ref,
                   stiffness_ref, field_ref, next_ref, swap_a_ref, swap_b_ref):
    odd = odd_ref[0] == 1
    field = add_ends(partial_ref[...], odd, own_rows, swap_a_in[...], swap_b_in[...])
    field_ref[...] = field
    connectivity = connectivity_ref[...]
    forces = matvec(stiffness_ref, gather_corners(field, connectivity))
    partial = assemble(forces, connectivity) * scale_ref[:1, :1] + weight_ref[...] * field
    next_ref[...] = partial
    put_ends(partial, odd, own_rows, swap_a_ref, swap_b_ref)


def moment_kernel(own_rows, devices, odd_ref, partial_ref, swap_a_in, swap_b_in, weight_ref, scale_ref,
                  connectivity_ref, stiffness_ref, first_ref, second_ref, field_ref, moments_ref):
    odd = odd_ref[0] == 1
    third = add_ends(partial_ref[...], odd, own_rows, swap_a_in[...], swap_b_in[...])
    field_ref[...] = third
    values = gather_corners(third, connectivity_ref[...])
    forces = matvec(stiffness_ref, values)
    energy = jnp.sum(forces * jnp.concatenate(values, axis=0), axis=0, keepdims=True)
    own = own_mask(own_rows)
    first, second = jnp.where(own, first_ref[...], 0.0), jnp.where(own, second_ref[...], 0.0)
    owned = jnp.where(own, third, 0.0)
    moments = [
        jnp.sum(first * first),
        jnp.sum(first * second),
        jnp.sum(second * second),
        jnp.sum(second * owned),
        jnp.sum(owned * owned),
        jnp.sum(energy) * scale_ref[:1, :1] + jnp.sum(weight_ref[...] * owned * owned),
    ]
    lane = iota((devices, 128), 1)
    row = jnp.zeros((devices, 128), F32)
    for i, moment in enumerate(moments):
        row = jnp.where(lane == i, moment, row)
    moments_ref[...] = row


def step_weights(m):
    def dot(p, q):
        terms = [p[i] * q[j] * m[i + j] for i in range(3) for j in range(3) if p[i] is not None and q[j] is not None]
        return functools.reduce(lambda a, b: a + b, terms)

    def energy(p):
        terms = [p[i] * p[j] * (m[i + j + 1] + m[i + j]) for i in range(3) for j in range(3)
                 if p[i] is not None and p[j] is not None]
        return functools.reduce(lambda a, b: a + b, terms)

    norm0 = m[0]
    curve0 = m[0] + m[1]
    step0 = norm0 / curve0
    residual = [m[1] / curve0, -step0, None]
    norm1 = dot(residual, residual)
    turn0 = norm1 / norm0
    direction = [residual[0] + turn0, residual[1], None]
    step1 = norm1 / energy(direction)
    result = [step0 + step1 * direction[0], step1 * direction[1]]
    residual = [
        residual[0] - step1 * direction[0],
        residual[1] - step1 * (direction[0] + direction[1]),
        -step1 * direction[1],
    ]
    norm2 = dot(residual, residual)
    turn1 = norm2 / norm1
    direction = [residual[0] + turn1 * direction[0], residual[1] + turn1 * direction[1], residual[2]]
    step2 = norm2 / energy(direction)
    return [result[0] + step2 * direction[0], result[1] + step2 * direction[1], step2 * direction[2]]


def pick_kernel(own_rows, moments_ref, scale_ref, first_ref, second_ref, third_ref, connectivity_ref, code_ref,
                displacement_ref, out_ref):
    sums = jnp.sum(moments_ref[...], axis=0, keepdims=True)
    weights = step_weights([sums[:, i:i + 1] for i in range(6)])
    scale = scale_ref[:1, :1]
    field = (
        (weights[0] * scale) * first_ref[...]
        + (weights[1] * scale) * second_ref[...]
        + (weights[2] * scale) * third_ref[...]
    )
    for c in range(3):
        for h in range(own_rows):
            displacement_ref[c:c + 1, h * WIDE:(h + 1) * WIDE] = (
                field[c * ROWS_PER_FIELD + h:c * ROWS_PER_FIELD + h + 1])
    values = gather_corners(field, connectivity_ref[...])
    slots = code_ref.shape[1]
    tiles = []
    for start in range(0, slots, 128):
        sections = []
        for g in range(GROUPS):
            code = jnp.broadcast_to(code_ref[g:g + 1, start:start + 128], (8, 128))
            low, high = code & 127, code >> 7
            masks = [high == i for i in range(8)]
            for c in range(3):
                total = jnp.zeros((8, 128), F32)
                for i in range(8):
                    total = jnp.where(masks[i], take_lanes(values[c][:, i * 128:(i + 1) * 128], low), total)
                sections.append(total)
        sections.append(jnp.zeros((8, 128), F32))
        tiles.append(jnp.concatenate(sections, axis=0).T)
    out_ref[...] = jnp.concatenate(tiles, axis=0)


def motion_kernel(rows_ref, place_ref, table_ref, out_ref):
    returned = rows_ref[...].T
    high, low = split(returned)
    slots = returned.shape[1]
    place, group = place_ref[0:1], place_ref[1:2]
    faces = place.shape[1]
    chosen = onehot(iota((slots, faces), 0) == place)
    found = dot_nn(jnp.concatenate([high, low], axis=0), chosen)
    found = found[:128] + found[128:]
    owned = jnp.zeros((DOF, faces), F32)
    for i in range(GROUPS):
        owned = jnp.where(group == i, found[i * DOF:(i + 1) * DOF], owned)
    upper = owned.astype(BF16).astype(F32)
    lower = owned - upper
    left = jnp.concatenate([upper, lower, upper], axis=0).T.astype(BF16)
    table_high, table_low = split(table_ref[...])
    out_ref[...] = dot_nn(left, jnp.concatenate([table_high, table_high, table_low], axis=0))


def call(kernel, outs, args, scalars=0, hbm=(), scratch=()):
    in_specs = []
    for i in range(len(args)):
        if i < scalars:
            in_specs.append(pl.BlockSpec(memory_space=pltpu.SMEM))
        elif i in hbm:
            in_specs.append(pl.BlockSpec(memory_space=pl.ANY))
        else:
            in_specs.append(pl.BlockSpec(memory_space=pltpu.VMEM))
    return pl.pallas_call(
        kernel,
        out_shape=[jax.ShapeDtypeStruct(shape, dtype) for shape, dtype in outs],
        in_specs=in_specs,
        out_specs=[pl.BlockSpec(memory_space=pltpu.VMEM)] * len(outs),
        scratch_shapes=list(scratch),
        compiler_params=pltpu.CompilerParams(vmem_limit_bytes=VMEM_BYTES),
    )(*args)


def shards(pressure, face_owner, face_element, shape_table, stiffness, connectivity, support):
    devices = lax.axis_size(AXES)
    faces = pressure.shape[0]
    elements = stiffness.shape[2]
    nodes = support.shape[1]
    own_rows = nodes // WIDE
    capacity = max(2, (5 * faces + 2 * devices - 1) // (2 * devices))
    per = (capacity + GROUPS - 1) // GROUPS
    slots = devices * per
    odd = (lax.axis_index(AXES) % 2).astype(jnp.int32).reshape(1)
    evens = [(i, i + 1) for i in range(0, devices - 1, 2)]
    odds = [(i, i + 1) for i in range(1, devices - 1, 2)]
    pairs_a = evens + [(j, i) for i, j in evens]
    pairs_b = odds + [(j, i) for i, j in odds]

    def swap(a, b):
        return lax.ppermute(a, AXES, pairs_a), lax.ppermute(b, AXES, pairs_b)

    def everywhere(rows):
        return lax.all_to_all(rows, AXES, split_axis=0, concat_axis=0, tiled=True)

    field = ((DOF, WIDE), F32)
    ends = ((8, 128), F32)
    sent, place = call(
        functools.partial(send_kernel, devices, per),
        [((slots, 128), F32), ((8, faces), jnp.int32)],
        (pressure, face_owner.reshape(1, faces), face_element.reshape(1, faces), shape_table, support, stiffness),
        hbm=(5,),
        scratch=(pltpu.VMEM((3, 8, 8, elements), F32), pltpu.SemaphoreType.DMA((3,))),
    )
    arrived = everywhere(sent)
    partial, end_a, end_b, weight, scale, codes = call(
        functools.partial(load_kernel, devices, per),
        [field, ends, ends, field, ends, ((8, slots), jnp.int32)],
        (odd, arrived, connectivity, support),
        scalars=1,
    )
    fields = []
    for _ in range(2):
        end_a, end_b = swap(end_a, end_b)
        full, partial, end_a, end_b = call(
            functools.partial(product_kernel, own_rows),
            [field, field, ends, ends],
            (odd, partial, end_a, end_b, weight, scale, connectivity, stiffness),
            scalars=1,
        )
        fields.append(full)
    end_a, end_b = swap(end_a, end_b)
    third, moments = call(
        functools.partial(moment_kernel, own_rows, devices),
        [field, ((devices, 128), F32)],
        (odd, partial, end_a, end_b, weight, scale, connectivity, stiffness, fields[0], fields[1]),
        scalars=1,
    )
    moments = everywhere(moments)
    displacement, leaving = call(
        functools.partial(pick_kernel, own_rows),
        [((3, nodes), F32), ((slots, 128), F32)],
        (moments, scale, fields[0], fields[1], third, connectivity, codes),
    )
    returned = everywhere(leaving)
    (face_motion,) = call(motion_kernel, [((faces, 128), F32)], (returned, place, shape_table))
    return displacement, face_motion


def solution(mesh):
    in_specs = (
        P(AXES, None),
        P(AXES, None),
        P(AXES),
        P(),
        P(None, None, AXES),
        P(None, AXES),
        P(None, AXES),
    )
    out_specs = (P(None, AXES), P(AXES, None))
    return jax.shard_map(shards, mesh=mesh, in_specs=in_specs, out_specs=out_specs, check_vma=False)
```

```python
import functools

import jax
import jax.numpy as jnp
from jax import lax
from jax.experimental import pallas as pl
from jax.experimental.pallas import tpu as pltpu
from jax.sharding import PartitionSpec as P

AXES = ("fluid", "solid")
DOF = 24
CORNERS = 8
GROUPS = 5
ROWS_PER_FIELD = 8
WIDE = 256
VMEM_BYTES = 24 * 1024 * 1024
F32 = jnp.float32
BF16 = jnp.bfloat16


def iota(shape, axis):
    return lax.broadcasted_iota(jnp.int32, shape, axis)


def onehot(mask):
    return jnp.where(mask, 1.0, 0.0).astype(BF16)


def split(value):
    high = value.astype(BF16)
    return high, (value - high.astype(F32)).astype(BF16)


def dot_nt(left, right):
    return lax.dot_general(left, right, (((1,), (1,)), ((), ())), preferred_element_type=F32)


def dot_nn(left, right):
    return lax.dot_general(left, right, (((1,), (0,)), ((), ())), preferred_element_type=F32)


def take_lanes(table, index):
    return jnp.take_along_axis(table, index, axis=1, mode="promise_in_bounds")


def group_rows(group, sections, tail):
    kept = [jnp.where(group == i, section, 0.0) for i, section in enumerate(sections)]
    return jnp.concatenate(kept + [tail], axis=0)


def gather_corners(field, connectivity):
    elements = connectivity.shape[1]
    rows = {}
    for c in range(3):
        for h in range(9):
            row = field[c * ROWS_PER_FIELD + h // 2:c * ROWS_PER_FIELD + h // 2 + 1, (h % 2) * 128:(h % 2) * 128 + 128]
            rows[c, h] = jnp.broadcast_to(row, (CORNERS, 128))
    parts = [[], [], []]
    for start in range(0, elements, 128):
        index = connectivity[:, start:start + 128]
        low, high = index & 127, index >> 7
        masks = [high == h for h in range(9)]
        for c in range(3):
            total = jnp.zeros((CORNERS, 128), F32)
            for h in range(9):
                total = jnp.where(masks[h], take_lanes(rows[c, h], low), total)
            parts[c].append(total)
    return [jnp.concatenate(part, axis=1) for part in parts]


def assemble(terms, connectivity):
    elements = connectivity.shape[1]
    high, low = connectivity >> 8, connectivity & 255
    upper = terms.astype(BF16).astype(F32)
    lower = terms - upper
    total = jnp.zeros((2 * DOF, WIDE), F32)
    for k in range(CORNERS):
        mask = iota((ROWS_PER_FIELD, elements), 0) == high[k:k + 1]
        pieces = [
            jnp.where(mask, part[c * CORNERS + k:c * CORNERS + k + 1], 0.0)
            for part in (upper, lower)
            for c in range(3)
        ]
        left = jnp.concatenate(pieces, axis=0).astype(BF16)
        right = onehot(iota((WIDE, elements), 0) == low[k:k + 1])
        total = total + dot_nt(left, right)
    return total[:DOF] + total[DOF:]


def matvec(stiffness, values):
    elements = stiffness.shape[2]
    parts = []
    for start in range(0, elements, 128):
        total = jnp.zeros((DOF, 128), F32)
        for b in range(DOF):
            total = total + stiffness[b, :, start:start + 128] * values[b // 8][b % 8:b % 8 + 1, start:start + 128]
        parts.append(total)
    return jnp.concatenate(parts, axis=1)


def rim_rows(field, h):
    return [field[c * ROWS_PER_FIELD + h:c * ROWS_PER_FIELD + h + 1, :128] for c in range(3)]


def put_ends(partial, odd, own_rows, swap_a_ref, swap_b_ref):
    first = jnp.concatenate(rim_rows(partial, 0) + [jnp.zeros((5, 128), F32)], axis=0)
    over = jnp.concatenate(rim_rows(partial, own_rows) + [jnp.zeros((5, 128), F32)], axis=0)
    swap_a_ref[...] = jnp.where(odd, first, over)
    swap_b_ref[...] = jnp.where(odd, over, first)


def add_ends(partial, odd, own_rows, swap_a, swap_b):
    before = jnp.where(odd, swap_a, swap_b)
    after = jnp.where(odd, swap_b, swap_a)
    pad = jnp.zeros((1, WIDE - 128), F32)
    none = jnp.zeros((1, WIDE), F32)
    rows = []
    for c in range(3):
        for h in range(ROWS_PER_FIELD):
            if h == 0:
                rows.append(jnp.concatenate([before[c:c + 1], pad], axis=1))
            elif h == own_rows:
                rows.append(jnp.concatenate([after[c:c + 1], pad], axis=1))
            else:
                rows.append(none)
    return partial + jnp.concatenate(rows, axis=0)


def own_mask(own_rows):
    return (iota((DOF, WIDE), 0) % ROWS_PER_FIELD) < own_rows


def as_field(rows, own_rows):
    pieces = []
    for c in range(3):
        pieces += [rows[c:c + 1, h * WIDE:(h + 1) * WIDE] for h in range(own_rows)]
        pieces.append(jnp.zeros((ROWS_PER_FIELD - own_rows, WIDE), F32))
    return jnp.concatenate(pieces, axis=0)


def send_kernel(devices, per, odd_ref, pressure_hbm, owner_hbm, element_hbm, table_hbm, support_hbm, stiffness_hbm,
                out_ref, place_ref, pressure_ref, owner_ref, element_ref, table_ref, support_ref, diagonal_ref, sems):
    del odd_ref
    moves = [(owner_hbm, owner_ref), (table_hbm, table_ref), (pressure_hbm, pressure_ref), (element_hbm, element_ref),
             (support_hbm, support_ref)]
    moves += [(stiffness_hbm.at[pl.ds(8 * i, 8), pl.ds(8 * i, 8)], diagonal_ref.at[i]) for i in range(3)]
    copies = [pltpu.make_async_copy(source, target, sems.at[i]) for i, (source, target) in enumerate(moves)]
    for copy in copies:
        copy.start()
    faces = pressure_ref.shape[0]
    copies[0].wait()
    target = owner_ref[...]
    named = iota((devices, faces), 0) == target
    named16 = onehot(named)
    upto = onehot(iota((WIDE, WIDE), 0) <= iota((WIDE, WIDE), 1))
    before = jnp.zeros((devices, 1), F32)
    ranks = []
    for start in range(0, faces, WIDE):
        counts = dot_nn(named16[:, start:start + WIDE], upto) + before
        ranks.append(jnp.sum(jnp.where(named[:, start:start + WIDE], counts, 0.0), axis=0, keepdims=True))
        before = counts[:, WIDE - 1:]
    rank = jnp.concatenate(ranks, axis=1).astype(jnp.int32) - 1
    group = jnp.zeros_like(rank)
    for i in range(1, GROUPS):
        group = group + (rank >= i * per).astype(jnp.int32)
    place = target * per + rank - group * per
    place_ref[...] = jnp.concatenate([place, group, jnp.zeros((6, faces), jnp.int32)], axis=0)

    for copy in copies[1:4]:
        copy.wait()
    element = element_ref[...]
    table = jnp.concatenate([table_ref[...]] * GROUPS + [jnp.zeros((8, table_ref.shape[1]), F32)], axis=0)
    table_high, table_low = split(table)
    rows_high, rows_low = split(pressure_ref[...])
    projected = dot_nt(
        jnp.concatenate([table_high, table_low, table_high], axis=1),
        jnp.concatenate([rows_high, rows_high, rows_low], axis=1),
    )
    codes = jnp.where(iota((8, faces), 0) == group, element.astype(F32), 0.0)
    spread = group_rows(group, [projected[i * DOF:(i + 1) * DOF] for i in range(GROUPS)], codes)
    spread_high, spread_low = split(spread)
    chosen = onehot(iota((devices * per, faces), 0) == place)
    sent = dot_nt(chosen, jnp.concatenate([spread_high, spread_low], axis=0))

    for copy in copies[4:]:
        copy.wait()
    trace = jnp.zeros((8, faces), F32)
    for i in range(3):
        for j in range(8):
            trace = trace + jnp.where(iota((8, faces), 0) == j, diagonal_ref[i, j], 0.0)
    trace = jnp.sum(trace) + jnp.sum(support_ref[...])
    out_ref[...] = jnp.where(iota((devices * per, 128), 1) == 125, trace, sent[:, :128] + sent[:, 128:])


def load_kernel(devices, per, odd_ref, rows_ref, connectivity_ref, support_ref,
                partial_ref, swap_a_ref, swap_b_ref, weight_ref, scale_ref, code_ref):
    nodes = support_ref.shape[1]
    own_rows = nodes // WIDE
    rows = rows_ref[...]
    arrived = rows.T
    codes = arrived[GROUPS * DOF:].astype(jnp.int32)
    code_ref[...] = codes
    slots = rows.shape[0]
    total = jnp.zeros((4 * 2 * DOF, WIDE), F32)
    for g in range(GROUPS):
        terms = arrived[g * DOF:(g + 1) * DOF]
        upper = terms.astype(BF16).astype(F32)
        both = jnp.concatenate([upper, terms - upper], axis=0)
        code = codes[g:g + 1]
        left = jnp.concatenate([jnp.where((code >> 8) == i, both, 0.0) for i in range(4)], axis=0).astype(BF16)
        right = onehot(iota((WIDE, slots), 0) == (code & 255))
        total = total + dot_nt(left, right)
    loads = jnp.concatenate(
        [total[i * 2 * DOF:i * 2 * DOF + DOF] + total[i * 2 * DOF + DOF:(i + 1) * 2 * DOF] for i in range(4)], axis=1)
    partial = assemble(loads, connectivity_ref[...])
    partial_ref[...] = partial
    put_ends(partial, odd_ref[0] == 1, own_rows, swap_a_ref, swap_b_ref)
    trace = jnp.sum(rows[:, 125:126]) * (1.0 / per)
    inverse = jnp.full((8, 128), 3.0 * nodes * devices, F32) / jnp.full((8, 128), trace, F32)
    scale_ref[...] = inverse
    weight = as_field(support_ref[...], own_rows) * inverse[:1, :1] - 1.0
    weight_ref[...] = jnp.where(own_mask(own_rows), weight, 0.0)


def product_kernel(own_rows, odd_ref, partial_ref, swap_a_in, swap_b_in, weight_ref, scale_ref, connectivity_ref,
                   stiffness_ref, field_ref, next_ref, swap_a_ref, swap_b_ref):
    odd = odd_ref[0] == 1
    field = add_ends(partial_ref[...], odd, own_rows, swap_a_in[...], swap_b_in[...])
    field_ref[...] = field
    connectivity = connectivity_ref[...]
    forces = matvec(stiffness_ref, gather_corners(field, connectivity))
    partial = assemble(forces, connectivity) * scale_ref[:1, :1] + weight_ref[...] * field
    next_ref[...] = partial
    put_ends(partial, odd, own_rows, swap_a_ref, swap_b_ref)


def moment_kernel(own_rows, devices, odd_ref, partial_ref, swap_a_in, swap_b_in, weight_ref, scale_ref,
                  connectivity_ref, stiffness_ref, first_ref, second_ref, field_ref, moments_ref):
    odd = odd_ref[0] == 1
    third = add_ends(partial_ref[...], odd, own_rows, swap_a_in[...], swap_b_in[...])
    field_ref[...] = third
    values = gather_corners(third, connectivity_ref[...])
    forces = matvec(stiffness_ref, values)
    energy = jnp.sum(forces * jnp.concatenate(values, axis=0), axis=0, keepdims=True)
    own = own_mask(own_rows)
    first, second = jnp.where(own, first_ref[...], 0.0), jnp.where(own, second_ref[...], 0.0)
    owned = jnp.where(own, third, 0.0)
    moments = [
        jnp.sum(first * first),
        jnp.sum(first * second),
        jnp.sum(second * second),
        jnp.sum(second * owned),
        jnp.sum(owned * owned),
        jnp.sum(energy) * scale_ref[:1, :1] + jnp.sum(weight_ref[...] * owned * owned),
    ]
    lane = iota((devices, 128), 1)
    row = jnp.zeros((devices, 128), F32)
    for i, moment in enumerate(moments):
        row = jnp.where(lane == i, moment, row)
    moments_ref[...] = row


def step_weights(m):
    def dot(p, q):
        terms = [p[i] * q[j] * m[i + j] for i in range(3) for j in range(3) if p[i] is not None and q[j] is not None]
        return functools.reduce(lambda a, b: a + b, terms)

    def energy(p):
        terms = [p[i] * p[j] * (m[i + j + 1] + m[i + j]) for i in range(3) for j in range(3)
                 if p[i] is not None and p[j] is not None]
        return functools.reduce(lambda a, b: a + b, terms)

    norm0 = m[0]
    curve0 = m[0] + m[1]
    step0 = norm0 / curve0
    residual = [m[1] / curve0, -step0, None]
    norm1 = dot(residual, residual)
    turn0 = norm1 / norm0
    direction = [residual[0] + turn0, residual[1], None]
    step1 = norm1 / energy(direction)
    result = [step0 + step1 * direction[0], step1 * direction[1]]
    residual = [
        residual[0] - step1 * direction[0],
        residual[1] - step1 * (direction[0] + direction[1]),
        -step1 * direction[1],
    ]
    norm2 = dot(residual, residual)
    turn1 = norm2 / norm1
    direction = [residual[0] + turn1 * direction[0], residual[1] + turn1 * direction[1], residual[2]]
    step2 = norm2 / energy(direction)
    return [result[0] + step2 * direction[0], result[1] + step2 * direction[1], step2 * direction[2]]


def pick_kernel(own_rows, moments_ref, scale_ref, first_ref, second_ref, third_ref, connectivity_ref, code_ref,
                displacement_ref, out_ref):
    sums = jnp.sum(moments_ref[...], axis=0, keepdims=True)
    weights = step_weights([sums[:, i:i + 1] for i in range(6)])
    scale = scale_ref[:1, :1]
    field = (
        (weights[0] * scale) * first_ref[...]
        + (weights[1] * scale) * second_ref[...]
        + (weights[2] * scale) * third_ref[...]
    )
    for c in range(3):
        for h in range(own_rows):
            displacement_ref[c:c + 1, h * WIDE:(h + 1) * WIDE] = (
                field[c * ROWS_PER_FIELD + h:c * ROWS_PER_FIELD + h + 1])
    values = gather_corners(field, connectivity_ref[...])
    slots = code_ref.shape[1]
    tiles = []
    for start in range(0, slots, 128):
        sections = []
        for g in range(GROUPS):
            code = jnp.broadcast_to(code_ref[g:g + 1, start:start + 128], (8, 128))
            low, high = code & 127, code >> 7
            masks = [high == i for i in range(8)]
            for c in range(3):
                total = jnp.zeros((8, 128), F32)
                for i in range(8):
                    total = jnp.where(masks[i], take_lanes(values[c][:, i * 128:(i + 1) * 128], low), total)
                sections.append(total)
        sections.append(jnp.zeros((8, 128), F32))
        tiles.append(jnp.concatenate(sections, axis=0).T)
    out_ref[...] = jnp.concatenate(tiles, axis=0)


def motion_kernel(rows_ref, place_ref, table_ref, out_ref):
    returned = rows_ref[...].T
    high, low = split(returned)
    slots = returned.shape[1]
    place, group = place_ref[0:1], place_ref[1:2]
    faces = place.shape[1]
    chosen = onehot(iota((slots, faces), 0) == place)
    found = dot_nn(jnp.concatenate([high, low], axis=0), chosen)
    found = found[:128] + found[128:]
    owned = jnp.zeros((DOF, faces), F32)
    for i in range(GROUPS):
        owned = jnp.where(group == i, found[i * DOF:(i + 1) * DOF], owned)
    upper = owned.astype(BF16).astype(F32)
    lower = owned - upper
    left = jnp.concatenate([upper, lower, upper], axis=0).T.astype(BF16)
    table_high, table_low = split(table_ref[...])
    out_ref[...] = dot_nn(left, jnp.concatenate([table_high, table_high, table_low], axis=0))


def call(kernel, outs, args, scalars=0, hbm=(), scratch=()):
    in_specs = []
    for i in range(len(args)):
        if i < scalars:
            in_specs.append(pl.BlockSpec(memory_space=pltpu.SMEM))
        elif i in hbm:
            in_specs.append(pl.BlockSpec(memory_space=pltpu.HBM))
        else:
            in_specs.append(pl.BlockSpec(memory_space=pltpu.VMEM))
    return pl.pallas_call(
        kernel,
        out_shape=[jax.ShapeDtypeStruct(shape, dtype) for shape, dtype in outs],
        in_specs=in_specs,
        out_specs=[pl.BlockSpec(memory_space=pltpu.VMEM)] * len(outs),
        scratch_shapes=list(scratch),
        compiler_params=pltpu.CompilerParams(vmem_limit_bytes=VMEM_BYTES),
    )(*[pltpu.with_memory_space_constraint(arg, pltpu.HBM) if i in hbm else arg for i, arg in enumerate(args)])


def shards(pressure, face_owner, face_element, shape_table, stiffness, connectivity, support):
    devices = lax.axis_size(AXES)
    faces = pressure.shape[0]
    elements = stiffness.shape[2]
    nodes = support.shape[1]
    own_rows = nodes // WIDE
    capacity = max(2, (5 * faces + 2 * devices - 1) // (2 * devices))
    per = (capacity + GROUPS - 1) // GROUPS
    slots = devices * per
    odd = (lax.axis_index(AXES) % 2).astype(jnp.int32).reshape(1)
    evens = [(i, i + 1) for i in range(0, devices - 1, 2)]
    odds = [(i, i + 1) for i in range(1, devices - 1, 2)]
    pairs_a = evens + [(j, i) for i, j in evens]
    pairs_b = odds + [(j, i) for i, j in odds]

    def swap(a, b):
        return lax.ppermute(a, AXES, pairs_a), lax.ppermute(b, AXES, pairs_b)

    def everywhere(rows):
        return lax.all_to_all(rows, AXES, split_axis=0, concat_axis=0, tiled=True)

    field = ((DOF, WIDE), F32)
    ends = ((8, 128), F32)
    sent, place = call(
        functools.partial(send_kernel, devices, per),
        [((slots, 128), F32), ((8, faces), jnp.int32)],
        (odd, pressure, face_owner.reshape(1, faces), face_element.reshape(1, faces), shape_table, support, stiffness),
        scalars=1,
        hbm=range(1, 7),
        scratch=(
            pltpu.VMEM(pressure.shape, F32),
            pltpu.VMEM((1, faces), jnp.int32),
            pltpu.VMEM((1, faces), jnp.int32),
            pltpu.VMEM(shape_table.shape, F32),
            pltpu.VMEM(support.shape, F32),
            pltpu.VMEM((3, 8, 8, elements), F32),
            pltpu.SemaphoreType.DMA((8,)),
        ),
    )
    arrived = everywhere(sent)
    partial, end_a, end_b, weight, scale, codes = call(
        functools.partial(load_kernel, devices, per),
        [field, ends, ends, field, ends, ((8, slots), jnp.int32)],
        (odd, arrived, connectivity, support),
        scalars=1,
    )
    fields = []
    for _ in range(2):
        end_a, end_b = swap(end_a, end_b)
        full, partial, end_a, end_b = call(
            functools.partial(product_kernel, own_rows),
            [field, field, ends, ends],
            (odd, partial, end_a, end_b, weight, scale, connectivity, stiffness),
            scalars=1,
        )
        fields.append(full)
    end_a, end_b = swap(end_a, end_b)
    third, moments = call(
        functools.partial(moment_kernel, own_rows, devices),
        [field, ((devices, 128), F32)],
        (odd, partial, end_a, end_b, weight, scale, connectivity, stiffness, fields[0], fields[1]),
        scalars=1,
    )
    moments = everywhere(moments)
    displacement, leaving = call(
        functools.partial(pick_kernel, own_rows),
        [((3, nodes), F32), ((slots, 128), F32)],
        (moments, scale, fields[0], fields[1], third, connectivity, codes),
    )
    returned = everywhere(leaving)
    (face_motion,) = call(motion_kernel, [((faces, 128), F32)], (returned, place, shape_table))
    return displacement, face_motion


def solution(mesh):
    in_specs = (
        P(AXES, None),
        P(AXES, None),
        P(AXES),
        P(),
        P(None, None, AXES),
        P(None, AXES),
        P(None, AXES),
    )
    out_specs = (P(None, AXES), P(AXES, None))
    return jax.shard_map(shards, mesh=mesh, in_specs=in_specs, out_specs=out_specs, check_vma=False)
```

```python
import functools

import jax
import jax.numpy as jnp
from jax import lax
from jax.experimental import pallas as pl
from jax.experimental.pallas import tpu as pltpu
from jax.sharding import PartitionSpec as P

AXES = ("fluid", "solid")
DOF = 24
CORNERS = 8
GROUPS = 5
FIELD_ROWS = 16
LANES = 128
WIDE = 256
VMEM_BYTES = 24 * 1024 * 1024
F32 = jnp.float32
BF16 = jnp.bfloat16


def iota(shape, axis):
    return lax.broadcasted_iota(jnp.int32, shape, axis)


def onehot(mask):
    return jnp.where(mask, 1.0, 0.0).astype(BF16)


def split(value):
    high = value.astype(BF16)
    return high, (value - high.astype(F32)).astype(BF16)


def dot_nt(left, right):
    return lax.dot_general(left, right, (((1,), (1,)), ((), ())), preferred_element_type=F32)


def dot_nn(left, right):
    return lax.dot_general(left, right, (((1,), (0,)), ((), ())), preferred_element_type=F32)


def take_lanes(table, index):
    return jnp.take_along_axis(table, index, axis=1, mode="promise_in_bounds")


def gather_corners(field, connectivity):
    elements = connectivity.shape[1]
    rows = {}
    for c in range(3):
        for h in range(9):
            rows[c, h] = jnp.broadcast_to(field[c * FIELD_ROWS + h:c * FIELD_ROWS + h + 1], (CORNERS, LANES))
    parts = [[], [], []]
    for start in range(0, elements, LANES):
        index = connectivity[:, start:start + LANES]
        low, high = index & 127, index >> 7
        masks = [high == h for h in range(9)]
        for c in range(3):
            total = jnp.zeros((CORNERS, LANES), F32)
            for h in range(9):
                total = jnp.where(masks[h], take_lanes(rows[c, h], low), total)
            parts[c].append(total)
    return [jnp.concatenate(part, axis=1) for part in parts]


def assemble(terms, connectivity):
    elements = connectivity.shape[1]
    high, low = connectivity >> 7, connectivity & 127
    upper = terms.astype(BF16).astype(F32)
    lower = terms - upper
    total = jnp.zeros((6 * FIELD_ROWS, LANES), F32)
    for k in range(CORNERS):
        mask = iota((FIELD_ROWS, elements), 0) == high[k:k + 1]
        pieces = [
            jnp.where(mask, part[c * CORNERS + k:c * CORNERS + k + 1], 0.0)
            for part in (upper, lower)
            for c in range(3)
        ]
        left = jnp.concatenate(pieces, axis=0).astype(BF16)
        total = total + dot_nt(left, onehot(iota((LANES, elements), 0) == low[k:k + 1]))
    return total[:3 * FIELD_ROWS] + total[3 * FIELD_ROWS:]


def matvec(stiffness, values):
    elements = stiffness.shape[2]
    parts = []
    for start in range(0, elements, 128):
        total = jnp.zeros((DOF, 128), F32)
        for b in range(DOF):
            total = total + stiffness[b, :, start:start + 128] * values[b // 8][b % 8:b % 8 + 1, start:start + 128]
        parts.append(total)
    return jnp.concatenate(parts, axis=1)


def put_ends(partial, odd, own_rows, swap_a_ref, swap_b_ref):
    pad = [jnp.zeros((5, LANES), F32)]
    first = jnp.concatenate([partial[c * FIELD_ROWS:c * FIELD_ROWS + 1] for c in range(3)] + pad, axis=0)
    over = jnp.concatenate(
        [partial[c * FIELD_ROWS + own_rows:c * FIELD_ROWS + own_rows + 1] for c in range(3)] + pad, axis=0)
    swap_a_ref[...] = jnp.where(odd, first, over)
    swap_b_ref[...] = jnp.where(odd, over, first)


def add_ends(partial, odd, own_rows, swap_a, swap_b):
    before = jnp.where(odd, swap_a, swap_b)
    after = jnp.where(odd, swap_b, swap_a)
    pieces = []
    for c in range(3):
        pieces += [
            before[c:c + 1],
            jnp.zeros((own_rows - 1, LANES), F32),
            after[c:c + 1],
            jnp.zeros((FIELD_ROWS - own_rows - 1, LANES), F32),
        ]
    return partial + jnp.concatenate(pieces, axis=0)


def own_mask(own_rows):
    return (iota((3 * FIELD_ROWS, LANES), 0) % FIELD_ROWS) < own_rows


def as_field(rows, own_rows):
    pieces = []
    for c in range(3):
        pieces += [rows[c:c + 1, h * LANES:(h + 1) * LANES] for h in range(own_rows)]
        pieces.append(jnp.zeros((FIELD_ROWS - own_rows, LANES), F32))
    return jnp.concatenate(pieces, axis=0)


def send_kernel(devices, per, odd_ref, pressure_hbm, owner_hbm, element_hbm, table_hbm, support_hbm, stiffness_hbm,
                out_ref, place_ref, pressure_ref, owner_ref, element_ref, table_ref, support_ref, diagonal_ref, sems):
    del odd_ref
    moves = [(owner_hbm, owner_ref), (element_hbm, element_ref), (table_hbm, table_ref), (pressure_hbm, pressure_ref),
             (support_hbm, support_ref)]
    moves += [(stiffness_hbm.at[i, pl.ds(i, 1)], diagonal_ref.at[pl.ds(i, 1)]) for i in range(DOF)]
    copies = [pltpu.make_async_copy(source, target, sems.at[i]) for i, (source, target) in enumerate(moves)]
    for copy in copies:
        copy.start()
    for copy in copies:
        copy.wait()
    faces = pressure_ref.shape[0]
    target = owner_ref[...]
    named = iota((devices, faces), 0) == target
    named16 = onehot(named)
    blocks = range(0, faces, WIDE)
    upto = onehot(iota((WIDE, WIDE), 0) <= iota((WIDE, WIDE), 1))
    counts = dot_nn(jnp.concatenate([named16[:, start:start + WIDE] for start in blocks], axis=0), upto)
    before = jnp.zeros((devices, 1), F32)
    ranks = []
    for i, start in enumerate(blocks):
        count = counts[i * devices:(i + 1) * devices]
        here = jnp.where(named[:, start:start + WIDE], count + before, 0.0)
        ranks.append(jnp.sum(here, axis=0, keepdims=True))
        before = before + count[:, WIDE - 1:]
    rank = jnp.concatenate(ranks, axis=1).astype(jnp.int32) - 1
    group = jnp.zeros_like(rank)
    for i in range(1, GROUPS):
        group = group + (rank >= i * per).astype(jnp.int32)
    place = target * per + rank - group * per
    place_ref[...] = jnp.concatenate([place, group, jnp.zeros((6, faces), jnp.int32)], axis=0)
    chosen = onehot(iota((devices * per, faces), 0) == place)

    pad = jnp.zeros((LANES - GROUPS * DOF, table_ref.shape[1]), F32)
    table_high, table_low = split(jnp.concatenate([table_ref[...]] * GROUPS + [pad], axis=0))
    rows_high, rows_low = split(pressure_ref[...])
    projected = dot_nt(
        jnp.concatenate([table_high, table_low, table_high], axis=1),
        jnp.concatenate([rows_high, rows_high, rows_low], axis=1),
    )
    spread = [jnp.where(group == i, projected[i * DOF:(i + 1) * DOF], 0.0) for i in range(GROUPS)]
    spread.append(jnp.where(iota((8, faces), 0) == group, element_ref[...].astype(F32), 0.0))
    spread_high, spread_low = split(jnp.concatenate(spread, axis=0))
    sent = dot_nt(chosen, jnp.concatenate([spread_high, spread_low], axis=0))

    trace = jnp.sum(diagonal_ref[...]) + jnp.sum(support_ref[...])
    out_ref[...] = jnp.where(iota((devices * per, LANES), 1) == 125, trace, sent[:, :LANES] + sent[:, LANES:])


def load_kernel(devices, per, odd_ref, rows_ref, connectivity_ref, support_ref,
                partial_ref, swap_a_ref, swap_b_ref, weight_ref, scale_ref, code_ref):
    nodes = support_ref.shape[1]
    own_rows = nodes // LANES
    rows = rows_ref[...]
    slots = rows.shape[0]
    arrived = rows.T
    codes = arrived[GROUPS * DOF:].astype(jnp.int32)
    code_ref[...] = codes
    total = jnp.zeros((4 * 2 * DOF, WIDE), F32)
    for g in range(GROUPS):
        terms = arrived[g * DOF:(g + 1) * DOF]
        upper = terms.astype(BF16).astype(F32)
        both = jnp.concatenate([upper, terms - upper], axis=0)
        code = codes[g:g + 1]
        left = jnp.concatenate([jnp.where((code >> 8) == i, both, 0.0) for i in range(4)], axis=0).astype(BF16)
        total = total + dot_nt(left, onehot(iota((WIDE, slots), 0) == (code & 255)))
    loads = jnp.concatenate(
        [total[i * 2 * DOF:i * 2 * DOF + DOF] + total[i * 2 * DOF + DOF:(i + 1) * 2 * DOF] for i in range(4)], axis=1)
    partial = assemble(loads, connectivity_ref[...])
    partial_ref[...] = partial
    put_ends(partial, odd_ref[0] == 1, own_rows, swap_a_ref, swap_b_ref)
    trace = jnp.sum(rows[:, 125:126]) * (1.0 / per)
    inverse = jnp.full((8, LANES), 3.0 * nodes * devices, F32) / jnp.full((8, LANES), trace, F32)
    scale_ref[...] = inverse
    weight = as_field(support_ref[...], own_rows) * inverse[:1, :1] - 1.0
    weight_ref[...] = jnp.where(own_mask(own_rows), weight, 0.0)


def product_kernel(own_rows, odd_ref, partial_ref, swap_a_in, swap_b_in, weight_ref, scale_ref, connectivity_ref,
                   stiffness_ref, field_ref, values_ref, next_ref, swap_a_ref, swap_b_ref):
    odd = odd_ref[0] == 1
    field = add_ends(partial_ref[...], odd, own_rows, swap_a_in[...], swap_b_in[...])
    field_ref[...] = field
    connectivity = connectivity_ref[...]
    values = gather_corners(field, connectivity)
    values_ref[...] = jnp.concatenate(values, axis=0)
    forces = matvec(stiffness_ref, values)
    partial = assemble(forces, connectivity) * scale_ref[:1, :1] + weight_ref[...] * field
    next_ref[...] = partial
    put_ends(partial, odd, own_rows, swap_a_ref, swap_b_ref)


def moment_kernel(own_rows, devices, odd_ref, partial_ref, swap_a_in, swap_b_in, weight_ref, scale_ref,
                  connectivity_ref, stiffness_ref, first_ref, second_ref, pick0_ref, pick1_ref,
                  field_ref, values_ref, moments_ref):
    del pick0_ref, pick1_ref
    odd = odd_ref[0] == 1
    third = add_ends(partial_ref[...], odd, own_rows, swap_a_in[...], swap_b_in[...])
    field_ref[...] = third
    values = gather_corners(third, connectivity_ref[...])
    forces = matvec(stiffness_ref, values)
    values = jnp.concatenate(values, axis=0)
    values_ref[...] = values
    energy = jnp.sum(forces * values, axis=0, keepdims=True)
    own = own_mask(own_rows)
    first, second = jnp.where(own, first_ref[...], 0.0), jnp.where(own, second_ref[...], 0.0)
    owned = jnp.where(own, third, 0.0)
    moments = [
        jnp.sum(first * first),
        jnp.sum(first * second),
        jnp.sum(second * second),
        jnp.sum(second * owned),
        jnp.sum(owned * owned),
        jnp.sum(energy) * scale_ref[:1, :1] + jnp.sum(weight_ref[...] * owned * owned),
    ]
    lane = iota((devices, LANES), 1)
    row = jnp.zeros((devices, LANES), F32)
    for i, moment in enumerate(moments):
        row = jnp.where(lane == i, moment, row)
    moments_ref[...] = row


def step_weights(m):
    def dot(p, q):
        terms = [p[i] * q[j] * m[i + j] for i in range(3) for j in range(3) if p[i] is not None and q[j] is not None]
        return functools.reduce(lambda a, b: a + b, terms)

    def energy(p):
        terms = [p[i] * p[j] * (m[i + j + 1] + m[i + j]) for i in range(3) for j in range(3)
                 if p[i] is not None and p[j] is not None]
        return functools.reduce(lambda a, b: a + b, terms)

    norm0 = m[0]
    curve0 = m[0] + m[1]
    step0 = norm0 / curve0
    residual = [m[1] / curve0, -step0, None]
    norm1 = dot(residual, residual)
    turn0 = norm1 / norm0
    direction = [residual[0] + turn0, residual[1], None]
    step1 = norm1 / energy(direction)
    result = [step0 + step1 * direction[0], step1 * direction[1]]
    residual = [
        residual[0] - step1 * direction[0],
        residual[1] - step1 * (direction[0] + direction[1]),
        -step1 * direction[1],
    ]
    norm2 = dot(residual, residual)
    turn1 = norm2 / norm1
    direction = [residual[0] + turn1 * direction[0], residual[1] + turn1 * direction[1], residual[2]]
    step2 = norm2 / energy(direction)
    return [result[0] + step2 * direction[0], result[1] + step2 * direction[1], step2 * direction[2]]


def pick(values, code_ref, out_ref, blend):
    for start in range(0, code_ref.shape[1], LANES):
        sections = []
        for g in range(GROUPS):
            code = jnp.broadcast_to(code_ref[g:g + 1, start:start + LANES], (CORNERS, LANES))
            low, high = code & 127, code >> 7
            masks = [high == i for i in range(8)]
            for c in range(3):
                total = jnp.zeros((CORNERS, LANES), F32)
                for i in range(8):
                    tile = values[c * CORNERS:(c + 1) * CORNERS, i * LANES:(i + 1) * LANES]
                    total = jnp.where(masks[i], take_lanes(tile, low), total)
                sections.append(total)
        sections.append(jnp.zeros((CORNERS, LANES), F32))
        rows = pl.ds(start, LANES)
        out_ref[rows, :] = blend(jnp.concatenate(sections, axis=0).T, rows)


def pick_kernel(values_ref, code_ref, after_ref, out_ref):
    del after_ref
    pick(values_ref[...], code_ref, out_ref, lambda tile, rows: tile)


def blend_kernel(moments_ref, scale_ref, code_ref, pick0_ref, pick1_ref, values_ref, weights_ref, out_ref):
    sums = jnp.sum(moments_ref[...], axis=0, keepdims=True)
    weights = step_weights([sums[:, i:i + 1] for i in range(6)])
    weights = [weight * scale_ref[:1, :1] for weight in weights]
    weights_ref[...] = jnp.concatenate([jnp.broadcast_to(weight, (8, LANES)) for weight in weights], axis=0)

    def blend(tile, rows):
        return weights[0] * pick0_ref[rows, :] + weights[1] * pick1_ref[rows, :] + weights[2] * tile

    pick(values_ref[...], code_ref, out_ref, blend)


def motion_kernel(own_rows, rows_ref, place_ref, table_ref, weights_ref, first_ref, second_ref, third_ref,
                  displacement_hbm, out_hbm, displacement_ref, out_ref, sems):
    field = weights_ref[:1] * first_ref[...] + weights_ref[8:9] * second_ref[...] + weights_ref[16:17] * third_ref[...]
    for c in range(3):
        for h in range(own_rows):
            displacement_ref[c:c + 1, h * LANES:(h + 1) * LANES] = field[c * FIELD_ROWS + h:c * FIELD_ROWS + h + 1]
    copies = [pltpu.make_async_copy(displacement_ref, displacement_hbm, sems.at[0])]
    copies[0].start()
    high, low = split(rows_ref[...].T)
    slots, faces = rows_ref.shape[0], place_ref.shape[1]
    place, group = place_ref[0:1], place_ref[1:2]
    found = dot_nn(jnp.concatenate([high, low], axis=0), onehot(iota((slots, faces), 0) == place))
    found = found[:LANES] + found[LANES:]
    owned = jnp.zeros((DOF, faces), F32)
    for g in range(GROUPS):
        owned = jnp.where(group == g, found[g * DOF:(g + 1) * DOF], owned)
    upper = owned.astype(BF16).astype(F32)
    lower = owned - upper
    parts = jnp.concatenate([upper, lower, upper], axis=0).T.astype(BF16)
    table_high, table_low = split(table_ref[...])
    right = jnp.concatenate([table_high, table_high, table_low], axis=0)
    for i, start in enumerate(range(0, faces, WIDE)):
        out_ref[start:start + WIDE, :] = dot_nn(parts[start:start + WIDE], right)
        copy = pltpu.make_async_copy(
            out_ref.at[pl.ds(start, WIDE)], out_hbm.at[pl.ds(start, WIDE)], sems.at[1 + i])
        copy.start()
        copies.append(copy)
    for copy in copies:
        copy.wait()


def call(kernel, outs, args, scalars=0, hbm=(), outs_hbm=(), scratch=(), time=1.0):
    in_specs = []
    for i in range(len(args)):
        if i < scalars:
            in_specs.append(pl.BlockSpec(memory_space=pltpu.SMEM))
        elif i in hbm:
            in_specs.append(pl.BlockSpec(memory_space=pltpu.HBM))
        else:
            in_specs.append(pl.BlockSpec(memory_space=pltpu.VMEM))
    return pl.pallas_call(
        kernel,
        name=getattr(kernel, "func", kernel).__name__,
        out_shape=[jax.ShapeDtypeStruct(shape, dtype) for shape, dtype in outs],
        in_specs=in_specs,
        out_specs=[
            pl.BlockSpec(memory_space=pltpu.HBM if i in outs_hbm else pltpu.VMEM) for i in range(len(outs))
        ],
        scratch_shapes=list(scratch),
        cost_estimate=pl.CostEstimate(flops=int(time * 1e9), transcendentals=0, bytes_accessed=int(time * 1e6)),
        compiler_params=pltpu.CompilerParams(vmem_limit_bytes=VMEM_BYTES),
    )(*[pltpu.with_memory_space_constraint(arg, pltpu.HBM) if i in hbm else arg for i, arg in enumerate(args)])


def shards(pressure, face_owner, face_element, shape_table, stiffness, connectivity, support):
    devices = lax.axis_size(AXES)
    faces = pressure.shape[0]
    elements = stiffness.shape[2]
    nodes = support.shape[1]
    own_rows = nodes // LANES
    capacity = max(2, (5 * faces + 2 * devices - 1) // (2 * devices))
    per = (capacity + GROUPS - 1) // GROUPS
    slots = devices * per
    odd = (lax.axis_index(AXES) % 2).astype(jnp.int32).reshape(1)
    evens = [(i, i + 1) for i in range(0, devices - 1, 2)]
    odds = [(i, i + 1) for i in range(1, devices - 1, 2)]
    pairs_a = evens + [(j, i) for i, j in evens]
    pairs_b = odds + [(j, i) for i, j in odds]

    def swap(a, b):
        return lax.ppermute(a, AXES, pairs_a), lax.ppermute(b, AXES, pairs_b)

    def everywhere(rows):
        return lax.all_to_all(rows, AXES, split_axis=0, concat_axis=0, tiled=True)

    field = ((3 * FIELD_ROWS, LANES), F32)
    values = ((DOF, elements), F32)
    ends = ((8, LANES), F32)
    block = ((slots, LANES), F32)
    sent, place = call(
        functools.partial(send_kernel, devices, per),
        [block, ((8, faces), jnp.int32)],
        (odd, pressure, face_owner.reshape(1, faces), face_element.reshape(1, faces), shape_table, support, stiffness),
        scalars=1,
        hbm=range(1, 7),
        scratch=(
            pltpu.VMEM(pressure.shape, F32),
            pltpu.VMEM((1, faces), jnp.int32),
            pltpu.VMEM((1, faces), jnp.int32),
            pltpu.VMEM(shape_table.shape, F32),
            pltpu.VMEM(support.shape, F32),
            pltpu.VMEM((DOF, elements), F32),
            pltpu.SemaphoreType.DMA((5 + DOF,)),
        ),
    )
    arrived = everywhere(sent)
    partial, end_a, end_b, weight, scale, codes = call(
        functools.partial(load_kernel, devices, per),
        [field, ends, ends, field, ends, ((8, slots), jnp.int32)],
        (odd, arrived, connectivity, support),
        scalars=1,
    )
    fields, picks = [], []
    end_a, end_b = swap(end_a, end_b)
    for _ in range(2):
        full, corners, partial, end_a, end_b = call(
            functools.partial(product_kernel, own_rows),
            [field, values, field, ends, ends],
            (odd, partial, end_a, end_b, weight, scale, connectivity, stiffness),
            scalars=1,
        )
        fields.append(full)
        end_a, end_b = swap(end_a, end_b)
        picks += call(pick_kernel, [block], (corners, codes, end_a), time=0.1)
    third, corners, moments = call(
        functools.partial(moment_kernel, own_rows, devices),
        [field, values, ((devices, LANES), F32)],
        (odd, partial, end_a, end_b, weight, scale, connectivity, stiffness, *fields, *picks),
        scalars=1,
    )
    moments = everywhere(moments)
    weights, leaving = call(
        blend_kernel,
        [((24, LANES), F32), block],
        (moments, scale, codes, *picks, corners),
    )
    returned = everywhere(leaving)
    return call(
        functools.partial(motion_kernel, own_rows),
        [((3, nodes), F32), ((faces, LANES), F32)],
        (returned, place, shape_table, weights, *fields, third),
        outs_hbm=(0, 1),
        scratch=(
            pltpu.VMEM((3, nodes), F32),
            pltpu.VMEM((faces, LANES), F32),
            pltpu.SemaphoreType.DMA((1 + faces // WIDE,)),
        ),
    )


def solution(mesh):
    in_specs = (
        P(AXES, None),
        P(AXES, None),
        P(AXES),
        P(),
        P(None, None, AXES),
        P(None, AXES),
        P(None, AXES),
    )
    out_specs = (P(None, AXES), P(AXES, None))
    return jax.shard_map(shards, mesh=mesh, in_specs=in_specs, out_specs=out_specs, check_vma=False)
```

```python
import functools

import jax
import jax.numpy as jnp
from jax import lax
from jax.experimental import pallas as pl
from jax.experimental.pallas import tpu as pltpu
from jax.sharding import PartitionSpec as P

AXES = ("fluid", "solid")
DOF = 24
CORNERS = 8
GROUPS = 5
FIELD_ROWS = 16
LANES = 128
WIDE = 256
VMEM_BYTES = 24 * 1024 * 1024
F32 = jnp.float32
BF16 = jnp.bfloat16


def iota(shape, axis):
    return lax.broadcasted_iota(jnp.int32, shape, axis)


def onehot(mask):
    return jnp.where(mask, 1.0, 0.0).astype(BF16)


def split(value):
    high = value.astype(BF16)
    return high, (value - high.astype(F32)).astype(BF16)


def dot_nt(left, right):
    return lax.dot_general(left, right, (((1,), (1,)), ((), ())), preferred_element_type=F32)


def dot_nn(left, right):
    return lax.dot_general(left, right, (((1,), (0,)), ((), ())), preferred_element_type=F32)


def take_lanes(table, index):
    return jnp.take_along_axis(table, index, axis=1, mode="promise_in_bounds")


def gather_corners(field, connectivity):
    elements = connectivity.shape[1]
    rows = {}
    for c in range(3):
        for h in range(9):
            rows[c, h] = jnp.broadcast_to(field[c * FIELD_ROWS + h:c * FIELD_ROWS + h + 1], (CORNERS, LANES))
    parts = [[], [], []]
    for start in range(0, elements, LANES):
        index = connectivity[:, start:start + LANES]
        low, high = index & 127, index >> 7
        masks = [high == h for h in range(9)]
        for c in range(3):
            total = jnp.zeros((CORNERS, LANES), F32)
            for h in range(9):
                total = jnp.where(masks[h], take_lanes(rows[c, h], low), total)
            parts[c].append(total)
    return [jnp.concatenate(part, axis=1) for part in parts]


def assemble(terms, connectivity):
    elements = connectivity.shape[1]
    high, low = connectivity >> 7, connectivity & 127
    upper = terms.astype(BF16).astype(F32)
    lower = terms - upper
    total = jnp.zeros((6 * FIELD_ROWS, LANES), F32)
    for k in range(CORNERS):
        mask = iota((FIELD_ROWS, elements), 0) == high[k:k + 1]
        pieces = [
            jnp.where(mask, part[c * CORNERS + k:c * CORNERS + k + 1], 0.0)
            for part in (upper, lower)
            for c in range(3)
        ]
        left = jnp.concatenate(pieces, axis=0).astype(BF16)
        total = total + dot_nt(left, onehot(iota((LANES, elements), 0) == low[k:k + 1]))
    return total[:3 * FIELD_ROWS] + total[3 * FIELD_ROWS:]


def matvec(stiffness, values):
    elements = stiffness.shape[2]
    parts = []
    for start in range(0, elements, 128):
        total = jnp.zeros((DOF, 128), F32)
        for b in range(DOF):
            total = total + stiffness[b, :, start:start + 128] * values[b // 8][b % 8:b % 8 + 1, start:start + 128]
        parts.append(total)
    return jnp.concatenate(parts, axis=1)


def put_ends(partial, odd, own_rows, swap_a_ref, swap_b_ref):
    pad = [jnp.zeros((5, LANES), F32)]
    first = jnp.concatenate([partial[c * FIELD_ROWS:c * FIELD_ROWS + 1] for c in range(3)] + pad, axis=0)
    over = jnp.concatenate(
        [partial[c * FIELD_ROWS + own_rows:c * FIELD_ROWS + own_rows + 1] for c in range(3)] + pad, axis=0)
    swap_a_ref[...] = jnp.where(odd, first, over)
    swap_b_ref[...] = jnp.where(odd, over, first)


def add_ends(partial, odd, own_rows, swap_a, swap_b):
    before = jnp.where(odd, swap_a, swap_b)
    after = jnp.where(odd, swap_b, swap_a)
    pieces = []
    for c in range(3):
        pieces += [
            before[c:c + 1],
            jnp.zeros((own_rows - 1, LANES), F32),
            after[c:c + 1],
            jnp.zeros((FIELD_ROWS - own_rows - 1, LANES), F32),
        ]
    return partial + jnp.concatenate(pieces, axis=0)


def own_mask(own_rows):
    return (iota((3 * FIELD_ROWS, LANES), 0) % FIELD_ROWS) < own_rows


def as_field(rows, own_rows):
    pieces = []
    for c in range(3):
        pieces += [rows[c:c + 1, h * LANES:(h + 1) * LANES] for h in range(own_rows)]
        pieces.append(jnp.zeros((FIELD_ROWS - own_rows, LANES), F32))
    return jnp.concatenate(pieces, axis=0)


def send_kernel(devices, per, odd_ref, pressure_hbm, owner_hbm, element_hbm, table_hbm, support_hbm, stiffness_hbm,
                out_ref, place_ref, pressure_ref, owner_ref, element_ref, table_ref, support_ref, diagonal_ref, sems):
    del odd_ref
    moves = [(owner_hbm, owner_ref), (element_hbm, element_ref), (table_hbm, table_ref), (pressure_hbm, pressure_ref),
             (support_hbm, support_ref)]
    moves += [(stiffness_hbm.at[i, pl.ds(i, 1)], diagonal_ref.at[pl.ds(i, 1)]) for i in range(DOF)]
    copies = [pltpu.make_async_copy(source, target, sems.at[i]) for i, (source, target) in enumerate(moves)]
    for copy in copies:
        copy.start()
    for copy in copies:
        copy.wait()
    faces = pressure_ref.shape[0]
    target = owner_ref[...]
    named = iota((devices, faces), 0) == target
    named16 = onehot(named)
    blocks = range(0, faces, WIDE)
    upto = onehot(iota((WIDE, WIDE), 0) <= iota((WIDE, WIDE), 1))
    counts = dot_nn(jnp.concatenate([named16[:, start:start + WIDE] for start in blocks], axis=0), upto)
    before = jnp.zeros((devices, 1), F32)
    ranks = []
    for i, start in enumerate(blocks):
        count = counts[i * devices:(i + 1) * devices]
        here = jnp.where(named[:, start:start + WIDE], count + before, 0.0)
        ranks.append(jnp.sum(here, axis=0, keepdims=True))
        before = before + count[:, WIDE - 1:]
    rank = jnp.concatenate(ranks, axis=1).astype(jnp.int32) - 1
    group = jnp.zeros_like(rank)
    for i in range(1, GROUPS):
        group = group + (rank >= i * per).astype(jnp.int32)
    place = target * per + rank - group * per
    place_ref[...] = jnp.concatenate([place, group, jnp.zeros((6, faces), jnp.int32)], axis=0)
    chosen = onehot(iota((devices * per, faces), 0) == place)

    pad = jnp.zeros((LANES - GROUPS * DOF, table_ref.shape[1]), F32)
    table_high, table_low = split(jnp.concatenate([table_ref[...]] * GROUPS + [pad], axis=0))
    rows_high, rows_low = split(pressure_ref[...])
    projected = dot_nt(
        jnp.concatenate([table_high, table_low, table_high], axis=1),
        jnp.concatenate([rows_high, rows_high, rows_low], axis=1),
    )
    spread = [jnp.where(group == i, projected[i * DOF:(i + 1) * DOF], 0.0) for i in range(GROUPS)]
    spread.append(jnp.where(iota((8, faces), 0) == group, element_ref[...].astype(F32), 0.0))
    spread_high, spread_low = split(jnp.concatenate(spread, axis=0))
    sent = dot_nt(chosen, jnp.concatenate([spread_high, spread_low], axis=0))

    trace = jnp.sum(diagonal_ref[...]) + jnp.sum(support_ref[...])
    out_ref[...] = jnp.where(iota((devices * per, LANES), 1) == 125, trace, sent[:, :LANES] + sent[:, LANES:])


def load_kernel(devices, per, odd_ref, rows_ref, connectivity_ref, support_ref,
                partial_ref, swap_a_ref, swap_b_ref, weight_ref, scale_ref, code_ref):
    nodes = support_ref.shape[1]
    own_rows = nodes // LANES
    rows = rows_ref[...]
    slots = rows.shape[0]
    arrived = rows.T
    codes = arrived[GROUPS * DOF:].astype(jnp.int32)
    code_ref[...] = codes
    total = jnp.zeros((4 * 2 * DOF, WIDE), F32)
    for g in range(GROUPS):
        terms = arrived[g * DOF:(g + 1) * DOF]
        upper = terms.astype(BF16).astype(F32)
        both = jnp.concatenate([upper, terms - upper], axis=0)
        code = codes[g:g + 1]
        left = jnp.concatenate([jnp.where((code >> 8) == i, both, 0.0) for i in range(4)], axis=0).astype(BF16)
        total = total + dot_nt(left, onehot(iota((WIDE, slots), 0) == (code & 255)))
    loads = jnp.concatenate(
        [total[i * 2 * DOF:i * 2 * DOF + DOF] + total[i * 2 * DOF + DOF:(i + 1) * 2 * DOF] for i in range(4)], axis=1)
    partial = assemble(loads, connectivity_ref[...])
    partial_ref[...] = partial
    put_ends(partial, odd_ref[0] == 1, own_rows, swap_a_ref, swap_b_ref)
    trace = jnp.sum(rows[:, 125:126]) * (1.0 / per)
    inverse = jnp.full((8, LANES), 3.0 * nodes * devices, F32) / jnp.full((8, LANES), trace, F32)
    scale_ref[...] = inverse
    weight_ref[...] = as_field(support_ref[...], own_rows) * inverse[:1, :1]


def product_kernel(own_rows, odd_ref, partial_ref, swap_a_in, swap_b_in, weight_ref, scale_ref, connectivity_ref,
                   stiffness_ref, field_ref, values_ref, forces_ref, next_ref, swap_a_ref, swap_b_ref):
    odd = odd_ref[0] == 1
    field = add_ends(partial_ref[...], odd, own_rows, swap_a_in[...], swap_b_in[...])
    field_ref[...] = field
    connectivity = connectivity_ref[...]
    values = gather_corners(field, connectivity)
    values_ref[...] = jnp.concatenate(values, axis=0)
    forces = matvec(stiffness_ref, values)
    forces_ref[...] = forces
    partial = assemble(forces, connectivity) * scale_ref[:1, :1] + weight_ref[...] * field
    next_ref[...] = partial
    put_ends(partial, odd, own_rows, swap_a_ref, swap_b_ref)


def entries(pairs):
    lane = iota((1, LANES), 1)
    row = jnp.zeros((1, LANES), F32)
    for i, value in pairs:
        row = jnp.where(lane == i, value, row)
    return row


def share(value, norm):
    return jnp.full((1, LANES), value, F32) / jnp.maximum(jnp.full((1, LANES), norm, F32), 1e-30)


def lower_kernel(own_rows, weight_ref, scale_ref, first_ref, second_ref, values0_ref, values1_ref,
                 forces0_ref, forces1_ref, after_ref, own0_ref, own1_ref, turned_ref, numbers_ref):
    del after_ref
    own, weight = own_mask(own_rows), weight_ref[...]
    first, second = jnp.where(own, first_ref[...], 0.0), jnp.where(own, second_ref[...], 0.0)
    norm0 = jnp.sum(first * first)
    theta = share(jnp.sum(first * second), norm0)
    second = second - theta * first
    own0_ref[...], own1_ref[...] = first, second
    scale, part = scale_ref[:1, :1], theta[:, :1]
    values0, forces0 = values0_ref[...], forces0_ref[...]
    values1, forces1 = values1_ref[...] - part * values0, forces1_ref[...] - part * forces0
    turned_ref[...] = values1
    norm1 = jnp.sum(second * second)
    row = entries([
        (0, norm0),
        (1, jnp.sum(first * second)),
        (2, norm1),
        (6, jnp.sum(values0 * forces0) * scale + jnp.sum(weight * first * first)),
        (7, jnp.sum(values0 * forces1) * scale + jnp.sum(weight * first * second)),
        (8, jnp.sum(values1 * forces1) * scale + jnp.sum(weight * second * second)),
        (12, theta),
    ])
    numbers_ref[...] = jnp.concatenate(
        [row, share(1.0, norm0), share(1.0, norm1), jnp.zeros((5, LANES), F32)], axis=0)


def moment_kernel(own_rows, devices, odd_ref, partial_ref, swap_a_in, swap_b_in, weight_ref, scale_ref,
                  connectivity_ref, stiffness_ref, own0_ref, own1_ref, values0_ref, turned_ref, numbers_ref,
                  pick0_ref, pick1_ref, field_ref, values_ref, moments_ref):
    del pick0_ref, pick1_ref
    odd = odd_ref[0] == 1
    field = add_ends(partial_ref[...], odd, own_rows, swap_a_in[...], swap_b_in[...])
    field_ref[...] = field
    weight, scale = weight_ref[...], scale_ref[:1, :1]
    first, second = own0_ref[...], own1_ref[...]
    third = jnp.where(own_mask(own_rows), field, 0.0)
    phi = jnp.sum(first * third) * numbers_ref[1:2]
    psi = jnp.sum(second * third) * numbers_ref[2:3]
    third = third - psi * second - phi * first
    values0, values1 = values0_ref[...], turned_ref[...]
    values2 = jnp.concatenate(gather_corners(field, connectivity_ref[...]), axis=0)
    values_ref[...] = values2
    values2 = values2 - psi[:, :1] * values1 - phi[:, :1] * values0
    forces2 = matvec(stiffness_ref, [values2[c * CORNERS:(c + 1) * CORNERS] for c in range(3)])
    weighted = weight * third
    row = numbers_ref[:1] + entries([
        (3, jnp.sum(first * third)),
        (4, jnp.sum(second * third)),
        (5, jnp.sum(third * third)),
        (9, jnp.sum(values0 * forces2) * scale + jnp.sum(first * weighted)),
        (10, jnp.sum(values1 * forces2) * scale + jnp.sum(second * weighted)),
        (11, jnp.sum(values2 * forces2) * scale + jnp.sum(third * weighted)),
        (13, psi),
        (14, phi),
    ])
    moments_ref[...] = jnp.broadcast_to(row, (devices, LANES))


def step_weights(rows):
    column = [rows[:, i:i + 1] for i in range(15)]
    norms, energies, (theta, psi, phi) = column[:6], column[6:12], column[12:]

    def square(matrix, y):
        total = y[0] * y[0] * matrix[0]
        if len(y) > 1:
            total = total + y[1] * (2.0 * y[0] * matrix[1] + y[1] * matrix[2])
        if len(y) > 2:
            total = total + y[2] * (2.0 * (y[0] * matrix[3] + y[1] * matrix[4]) + y[2] * matrix[5])
        return jnp.sum(total, axis=0, keepdims=True)

    norm0 = jnp.sum(norms[0], axis=0, keepdims=True)
    step0 = norm0 / jnp.sum(energies[0], axis=0, keepdims=True)
    residual = [1.0 - step0 * theta, -step0]
    norm1 = square(norms, residual)
    turn0 = norm1 / norm0
    direction = [residual[0] + turn0, -step0]
    step1 = norm1 / square(energies, direction)
    lead = 1.0 + turn0
    residual = [
        residual[0] - step1 * (lead * theta - step0 * phi),
        -step0 - step1 * (lead - step0 * psi),
        step1 * step0,
    ]
    norm2 = square(norms, residual)
    turn1 = norm2 / norm1
    direction = [residual[0] + turn1 * direction[0], residual[1] - turn1 * step0, residual[2]]
    step2 = norm2 / square(energies, direction)
    return [
        step0 + step1 * lead + step2 * (1.0 + turn1 * lead),
        -step1 * step0 - step2 * (step0 + step1 * lead + turn1 * step0),
        step2 * step1 * step0,
    ]


def pick(values, code_ref, out_ref, blend):
    for start in range(0, code_ref.shape[1], LANES):
        sections = []
        for g in range(GROUPS):
            code = jnp.broadcast_to(code_ref[g:g + 1, start:start + LANES], (CORNERS, LANES))
            low, high = code & 127, code >> 7
            masks = [high == i for i in range(8)]
            for c in range(3):
                total = jnp.zeros((CORNERS, LANES), F32)
                for i in range(8):
                    tile = values[c * CORNERS:(c + 1) * CORNERS, i * LANES:(i + 1) * LANES]
                    total = jnp.where(masks[i], take_lanes(tile, low), total)
                sections.append(total)
        sections.append(jnp.zeros((CORNERS, LANES), F32))
        rows = pl.ds(start, LANES)
        out_ref[rows, :] = blend(jnp.concatenate(sections, axis=0).T, rows)


def pick_kernel(values_ref, code_ref, after_ref, out_ref):
    del after_ref
    pick(values_ref[...], code_ref, out_ref, lambda tile, rows: tile)


def blend_kernel(moments_ref, scale_ref, code_ref, pick0_ref, pick1_ref, values_ref, weights_ref, out_ref):
    weights = step_weights(moments_ref[...])
    weights = [weight * scale_ref[:1, :1] for weight in weights]
    weights_ref[...] = jnp.concatenate([jnp.broadcast_to(weight, (8, LANES)) for weight in weights], axis=0)

    def blend(tile, rows):
        return weights[0] * pick0_ref[rows, :] + weights[1] * pick1_ref[rows, :] + weights[2] * tile

    pick(values_ref[...], code_ref, out_ref, blend)


def motion_kernel(own_rows, rows_ref, place_ref, table_ref, weights_ref, first_ref, second_ref, third_ref,
                  displacement_hbm, out_hbm, displacement_ref, out_ref, sems):
    field = weights_ref[:1] * first_ref[...] + weights_ref[8:9] * second_ref[...] + weights_ref[16:17] * third_ref[...]
    for c in range(3):
        for h in range(own_rows):
            displacement_ref[c:c + 1, h * LANES:(h + 1) * LANES] = field[c * FIELD_ROWS + h:c * FIELD_ROWS + h + 1]
    copies = [pltpu.make_async_copy(displacement_ref, displacement_hbm, sems.at[0])]
    copies[0].start()
    high, low = split(rows_ref[...].T)
    slots, faces = rows_ref.shape[0], place_ref.shape[1]
    place, group = place_ref[0:1], place_ref[1:2]
    found = dot_nn(jnp.concatenate([high, low], axis=0), onehot(iota((slots, faces), 0) == place))
    found = found[:LANES] + found[LANES:]
    owned = jnp.zeros((DOF, faces), F32)
    for g in range(GROUPS):
        owned = jnp.where(group == g, found[g * DOF:(g + 1) * DOF], owned)
    upper = owned.astype(BF16).astype(F32)
    lower = owned - upper
    parts = jnp.concatenate([upper, lower, upper], axis=0).T.astype(BF16)
    table_high, table_low = split(table_ref[...])
    right = jnp.concatenate([table_high, table_high, table_low], axis=0)
    for i, start in enumerate(range(0, faces, WIDE)):
        out_ref[start:start + WIDE, :] = dot_nn(parts[start:start + WIDE], right)
        copy = pltpu.make_async_copy(
            out_ref.at[pl.ds(start, WIDE)], out_hbm.at[pl.ds(start, WIDE)], sems.at[1 + i])
        copy.start()
        copies.append(copy)
    for copy in copies:
        copy.wait()


def call(kernel, outs, args, scalars=0, hbm=(), outs_hbm=(), scratch=(), time=1.0):
    in_specs = []
    for i in range(len(args)):
        if i < scalars:
            in_specs.append(pl.BlockSpec(memory_space=pltpu.SMEM))
        elif i in hbm:
            in_specs.append(pl.BlockSpec(memory_space=pltpu.HBM))
        else:
            in_specs.append(pl.BlockSpec(memory_space=pltpu.VMEM))
    return pl.pallas_call(
        kernel,
        name=getattr(kernel, "func", kernel).__name__,
        out_shape=[jax.ShapeDtypeStruct(shape, dtype) for shape, dtype in outs],
        in_specs=in_specs,
        out_specs=[
            pl.BlockSpec(memory_space=pltpu.HBM if i in outs_hbm else pltpu.VMEM) for i in range(len(outs))
        ],
        scratch_shapes=list(scratch),
        cost_estimate=pl.CostEstimate(flops=int(time * 1e9), transcendentals=0, bytes_accessed=int(time * 1e6)),
        compiler_params=pltpu.CompilerParams(vmem_limit_bytes=VMEM_BYTES),
    )(*[pltpu.with_memory_space_constraint(arg, pltpu.HBM) if i in hbm else arg for i, arg in enumerate(args)])


def shards(pressure, face_owner, face_element, shape_table, stiffness, connectivity, support):
    devices = lax.axis_size(AXES)
    faces = pressure.shape[0]
    elements = stiffness.shape[2]
    nodes = support.shape[1]
    own_rows = nodes // LANES
    capacity = max(2, (5 * faces + 2 * devices - 1) // (2 * devices))
    per = (capacity + GROUPS - 1) // GROUPS
    slots = devices * per
    odd = (lax.axis_index(AXES) % 2).astype(jnp.int32).reshape(1)
    evens = [(i, i + 1) for i in range(0, devices - 1, 2)]
    odds = [(i, i + 1) for i in range(1, devices - 1, 2)]
    pairs_a = evens + [(j, i) for i, j in evens]
    pairs_b = odds + [(j, i) for i, j in odds]

    def swap(a, b):
        return lax.ppermute(a, AXES, pairs_a), lax.ppermute(b, AXES, pairs_b)

    def everywhere(rows):
        return lax.all_to_all(rows, AXES, split_axis=0, concat_axis=0, tiled=True)

    field = ((3 * FIELD_ROWS, LANES), F32)
    values = ((DOF, elements), F32)
    ends = ((8, LANES), F32)
    block = ((slots, LANES), F32)
    sent, place = call(
        functools.partial(send_kernel, devices, per),
        [block, ((8, faces), jnp.int32)],
        (odd, pressure, face_owner.reshape(1, faces), face_element.reshape(1, faces), shape_table, support, stiffness),
        scalars=1,
        hbm=range(1, 7),
        scratch=(
            pltpu.VMEM(pressure.shape, F32),
            pltpu.VMEM((1, faces), jnp.int32),
            pltpu.VMEM((1, faces), jnp.int32),
            pltpu.VMEM(shape_table.shape, F32),
            pltpu.VMEM(support.shape, F32),
            pltpu.VMEM((DOF, elements), F32),
            pltpu.SemaphoreType.DMA((5 + DOF,)),
        ),
    )
    arrived = everywhere(sent)
    partial, end_a, end_b, weight, scale, codes = call(
        functools.partial(load_kernel, devices, per),
        [field, ends, ends, field, ends, ((8, slots), jnp.int32)],
        (odd, arrived, connectivity, support),
        scalars=1,
    )
    stage = (
        functools.partial(product_kernel, own_rows),
        [field, values, values, field, ends, ends],
    )
    end_a, end_b = swap(end_a, end_b)
    first, values0, forces0, partial, end_a, end_b = call(
        *stage, (odd, partial, end_a, end_b, weight, scale, connectivity, stiffness), scalars=1)
    end_a, end_b = swap(end_a, end_b)
    (pick0,) = call(pick_kernel, [block], (values0, codes, end_a), time=0.1)
    second, values1, forces1, partial, end_a, end_b = call(
        *stage, (odd, partial, end_a, end_b, weight, scale, connectivity, stiffness), scalars=1)
    end_a, end_b = swap(end_a, end_b)
    (pick1,) = call(pick_kernel, [block], (values1, codes, end_a), time=0.1)
    own0, own1, turned, numbers = call(
        functools.partial(lower_kernel, own_rows),
        [field, field, values, ends],
        (weight, scale, first, second, values0, values1, forces0, forces1, end_a),
        time=0.1,
    )
    third, values2, moments = call(
        functools.partial(moment_kernel, own_rows, devices),
        [field, values, ((devices, LANES), F32)],
        (odd, partial, end_a, end_b, weight, scale, connectivity, stiffness, own0, own1, values0, turned, numbers,
         pick0, pick1),
        scalars=1,
    )
    moments = everywhere(moments)
    weights, leaving = call(
        blend_kernel,
        [((24, LANES), F32), block],
        (moments, scale, codes, pick0, pick1, values2),
    )
    returned = everywhere(leaving)
    return call(
        functools.partial(motion_kernel, own_rows),
        [((3, nodes), F32), ((faces, LANES), F32)],
        (returned, place, shape_table, weights, first, second, third),
        outs_hbm=(0, 1),
        scratch=(
            pltpu.VMEM((3, nodes), F32),
            pltpu.VMEM((faces, LANES), F32),
            pltpu.SemaphoreType.DMA((1 + faces // WIDE,)),
        ),
    )


def solution(mesh):
    in_specs = (
        P(AXES, None),
        P(AXES, None),
        P(AXES),
        P(),
        P(None, None, AXES),
        P(None, AXES),
        P(None, AXES),
    )
    out_specs = (P(None, AXES), P(AXES, None))
    return jax.shard_map(shards, mesh=mesh, in_specs=in_specs, out_specs=out_specs, check_vma=False)
```

```python
import functools

import jax
import jax.numpy as jnp
from jax import lax
from jax.experimental import pallas as pl
from jax.experimental.pallas import tpu as pltpu
from jax.sharding import PartitionSpec as P

AXES = ("fluid", "solid")
DOF = 24
CORNERS = 8
GROUPS = 5
FIELD_ROWS = 16
LANES = 128
WIDE = 256
VMEM_BYTES = 24 * 1024 * 1024
F32 = jnp.float32
BF16 = jnp.bfloat16


def iota(shape, axis):
    return lax.broadcasted_iota(jnp.int32, shape, axis)


def onehot(mask):
    return jnp.where(mask, 1.0, 0.0).astype(BF16)


def split(value):
    high = value.astype(BF16)
    return high, (value - high.astype(F32)).astype(BF16)


def dot_nt(left, right):
    return lax.dot_general(left, right, (((1,), (1,)), ((), ())), preferred_element_type=F32)


def dot_nn(left, right):
    return lax.dot_general(left, right, (((1,), (0,)), ((), ())), preferred_element_type=F32)


def take_lanes(table, index):
    return jnp.take_along_axis(table, index, axis=1, mode="promise_in_bounds")


def gather_corners(field, connectivity):
    elements = connectivity.shape[1]
    rows = {}
    for c in range(3):
        for h in range(9):
            rows[c, h] = jnp.broadcast_to(field[c * FIELD_ROWS + h:c * FIELD_ROWS + h + 1], (CORNERS, LANES))
    parts = [[], [], []]
    for start in range(0, elements, LANES):
        index = connectivity[:, start:start + LANES]
        low, high = index & 127, index >> 7
        masks = [high == h for h in range(9)]
        for c in range(3):
            total = jnp.zeros((CORNERS, LANES), F32)
            for h in range(9):
                total = jnp.where(masks[h], take_lanes(rows[c, h], low), total)
            parts[c].append(total)
    return [jnp.concatenate(part, axis=1) for part in parts]


def assemble(terms, connectivity, columns_ref=None):
    elements = connectivity.shape[1]
    high, low = connectivity >> 7, connectivity & 127
    upper = terms.astype(BF16).astype(F32)
    lower = terms - upper
    total = jnp.zeros((6 * FIELD_ROWS, LANES), F32)
    for k in range(CORNERS):
        mask = iota((FIELD_ROWS, elements), 0) == high[k:k + 1]
        pieces = [
            jnp.where(mask, part[c * CORNERS + k:c * CORNERS + k + 1], 0.0)
            for part in (upper, lower)
            for c in range(3)
        ]
        left = jnp.concatenate(pieces, axis=0).astype(BF16)
        if columns_ref is None:
            total = total + dot_nt(left, onehot(iota((LANES, elements), 0) == low[k:k + 1]))
        else:
            total = total + dot_nn(left, columns_ref[k])
    return total[:3 * FIELD_ROWS] + total[3 * FIELD_ROWS:]


def columns_kernel(connectivity_ref, after_ref, out_ref):
    del after_ref
    low = connectivity_ref[...] & 127
    for k in range(CORNERS):
        out_ref[k] = jnp.where(iota((LANES, low.shape[1]), 0) == low[k:k + 1], 1.0, 0.0).T.astype(BF16)


def matvec(stiffness, values):
    elements = stiffness.shape[2]
    parts = []
    for start in range(0, elements, 128):
        total = jnp.zeros((DOF, 128), F32)
        for b in range(DOF):
            total = total + stiffness[b, :, start:start + 128] * values[b // 8][b % 8:b % 8 + 1, start:start + 128]
        parts.append(total)
    return jnp.concatenate(parts, axis=1)


def put_ends(partial, odd, own_rows, swap_a_ref, swap_b_ref):
    pad = [jnp.zeros((5, LANES), F32)]
    first = jnp.concatenate([partial[c * FIELD_ROWS:c * FIELD_ROWS + 1] for c in range(3)] + pad, axis=0)
    over = jnp.concatenate(
        [partial[c * FIELD_ROWS + own_rows:c * FIELD_ROWS + own_rows + 1] for c in range(3)] + pad, axis=0)
    swap_a_ref[...] = jnp.where(odd, first, over)
    swap_b_ref[...] = jnp.where(odd, over, first)


def add_ends(partial, odd, own_rows, swap_a, swap_b):
    before = jnp.where(odd, swap_a, swap_b)
    after = jnp.where(odd, swap_b, swap_a)
    pieces = []
    for c in range(3):
        pieces += [
            before[c:c + 1],
            jnp.zeros((own_rows - 1, LANES), F32),
            after[c:c + 1],
            jnp.zeros((FIELD_ROWS - own_rows - 1, LANES), F32),
        ]
    return partial + jnp.concatenate(pieces, axis=0)


def own_mask(own_rows):
    return (iota((3 * FIELD_ROWS, LANES), 0) % FIELD_ROWS) < own_rows


def as_field(rows, own_rows):
    pieces = []
    for c in range(3):
        pieces += [rows[c:c + 1, h * LANES:(h + 1) * LANES] for h in range(own_rows)]
        pieces.append(jnp.zeros((FIELD_ROWS - own_rows, LANES), F32))
    return jnp.concatenate(pieces, axis=0)


def send_kernel(devices, per, odd_ref, pressure_hbm, owner_hbm, element_hbm, table_hbm, support_hbm, stiffness_hbm,
                out_ref, place_ref, pressure_ref, owner_ref, element_ref, table_ref, support_ref, diagonal_ref, sems):
    del odd_ref
    moves = [(owner_hbm, owner_ref), (element_hbm, element_ref), (table_hbm, table_ref), (pressure_hbm, pressure_ref),
             (support_hbm, support_ref)]
    moves += [(stiffness_hbm.at[i, pl.ds(i, 1)], diagonal_ref.at[pl.ds(i, 1)]) for i in range(DOF)]
    copies = [pltpu.make_async_copy(source, target, sems.at[i]) for i, (source, target) in enumerate(moves)]
    for copy in copies:
        copy.start()
    for copy in copies:
        copy.wait()
    faces = pressure_ref.shape[0]
    target = owner_ref[...]
    named = iota((devices, faces), 0) == target
    named16 = onehot(named)
    blocks = range(0, faces, WIDE)
    upto = onehot(iota((WIDE, WIDE), 0) <= iota((WIDE, WIDE), 1))
    counts = dot_nn(jnp.concatenate([named16[:, start:start + WIDE] for start in blocks], axis=0), upto)
    before = jnp.zeros((devices, 1), F32)
    ranks = []
    for i, start in enumerate(blocks):
        count = counts[i * devices:(i + 1) * devices]
        here = jnp.where(named[:, start:start + WIDE], count + before, 0.0)
        ranks.append(jnp.sum(here, axis=0, keepdims=True))
        before = before + count[:, WIDE - 1:]
    rank = jnp.concatenate(ranks, axis=1).astype(jnp.int32) - 1
    group = jnp.zeros_like(rank)
    for i in range(1, GROUPS):
        group = group + (rank >= i * per).astype(jnp.int32)
    place = target * per + rank - group * per
    place_ref[...] = jnp.concatenate([place, group, jnp.zeros((6, faces), jnp.int32)], axis=0)
    chosen = onehot(iota((devices * per, faces), 0) == place)

    pad = jnp.zeros((LANES - GROUPS * DOF, table_ref.shape[1]), F32)
    table_high, table_low = split(jnp.concatenate([table_ref[...]] * GROUPS + [pad], axis=0))
    rows_high, rows_low = split(pressure_ref[...])
    projected = dot_nt(
        jnp.concatenate([table_high, table_low, table_high], axis=1),
        jnp.concatenate([rows_high, rows_high, rows_low], axis=1),
    )
    spread = [jnp.where(group == i, projected[i * DOF:(i + 1) * DOF], 0.0) for i in range(GROUPS)]
    spread.append(jnp.where(iota((8, faces), 0) == group, element_ref[...].astype(F32), 0.0))
    spread_high, spread_low = split(jnp.concatenate(spread, axis=0))
    sent = dot_nt(chosen, jnp.concatenate([spread_high, spread_low], axis=0))

    trace = jnp.sum(diagonal_ref[...]) + jnp.sum(support_ref[...])
    out_ref[...] = jnp.where(iota((devices * per, LANES), 1) == 125, trace, sent[:, :LANES] + sent[:, LANES:])


def load_kernel(devices, per, odd_ref, rows_ref, connectivity_ref, support_ref,
                partial_ref, swap_a_ref, swap_b_ref, weight_ref, scale_ref, code_ref, loads_ref):
    nodes = support_ref.shape[1]
    own_rows = nodes // LANES

    @pl.when(odd_ref[0] >= 0)
    def _():
        rows = rows_ref[...]
        arrived = rows.T
        codes = arrived[GROUPS * DOF:].astype(jnp.int32)
        code_ref[...] = codes
        slots = rows.shape[0]
        total = jnp.zeros((4 * 2 * DOF, WIDE), F32)
        for g in range(GROUPS):
            terms = arrived[g * DOF:(g + 1) * DOF]
            upper = terms.astype(BF16).astype(F32)
            both = jnp.concatenate([upper, terms - upper], axis=0)
            code = codes[g:g + 1]
            left = jnp.concatenate([jnp.where((code >> 8) == i, both, 0.0) for i in range(4)], axis=0).astype(BF16)
            total = total + dot_nt(left, onehot(iota((WIDE, slots), 0) == (code & 255)))
        for i in range(4):
            start = i * 2 * DOF
            loads_ref[:, i * WIDE:(i + 1) * WIDE] = total[start:start + DOF] + total[start + DOF:start + 2 * DOF]

    partial = assemble(loads_ref[...], connectivity_ref[...])
    partial_ref[...] = partial
    put_ends(partial, odd_ref[0] == 1, own_rows, swap_a_ref, swap_b_ref)
    trace = jnp.sum(rows_ref[:, 125:126]) * (1.0 / per)
    inverse = jnp.full((8, LANES), 3.0 * nodes * devices, F32) / jnp.full((8, LANES), trace, F32)
    scale_ref[...] = inverse
    weight_ref[...] = as_field(support_ref[...], own_rows) * inverse[:1, :1]


def product_kernel(own_rows, odd_ref, partial_ref, swap_a_in, swap_b_in, weight_ref, scale_ref, connectivity_ref,
                   stiffness_ref, columns_ref, field_ref, values_ref, forces_ref, next_ref, swap_a_ref, swap_b_ref):
    odd = odd_ref[0] == 1

    @pl.when(odd_ref[0] >= 0)
    def _():
        field = add_ends(partial_ref[...], odd, own_rows, swap_a_in[...], swap_b_in[...])
        field_ref[...] = field
        values = gather_corners(field, connectivity_ref[...])
        values_ref[...] = jnp.concatenate(values, axis=0)
        forces_ref[...] = matvec(stiffness_ref, values)

    partial = assemble(forces_ref[...], connectivity_ref[...], columns_ref)
    partial = partial * scale_ref[:1, :1] + weight_ref[...] * field_ref[...]
    next_ref[...] = partial
    put_ends(partial, odd, own_rows, swap_a_ref, swap_b_ref)


def entries(pairs):
    lane = iota((1, LANES), 1)
    row = jnp.zeros((1, LANES), F32)
    for i, value in pairs:
        row = jnp.where(lane == i, value, row)
    return row


def share(value, norm):
    return jnp.full((1, LANES), value, F32) / jnp.maximum(jnp.full((1, LANES), norm, F32), 1e-30)


def lower_kernel(own_rows, weight_ref, scale_ref, first_ref, second_ref, values0_ref, values1_ref,
                 forces0_ref, forces1_ref, after_ref, own0_ref, own1_ref, turned_ref, numbers_ref):
    del after_ref
    own, weight = own_mask(own_rows), weight_ref[...]
    first, second = jnp.where(own, first_ref[...], 0.0), jnp.where(own, second_ref[...], 0.0)
    norm0 = jnp.sum(first * first)
    theta = share(jnp.sum(first * second), norm0)
    second = second - theta * first
    own0_ref[...], own1_ref[...] = first, second
    scale, part = scale_ref[:1, :1], theta[:, :1]
    values0, forces0 = values0_ref[...], forces0_ref[...]
    values1, forces1 = values1_ref[...] - part * values0, forces1_ref[...] - part * forces0
    turned_ref[...] = values1
    norm1 = jnp.sum(second * second)
    row = entries([
        (0, norm0),
        (1, jnp.sum(first * second)),
        (2, norm1),
        (6, jnp.sum(values0 * forces0) * scale + jnp.sum(weight * first * first)),
        (7, jnp.sum(values0 * forces1) * scale + jnp.sum(weight * first * second)),
        (8, jnp.sum(values1 * forces1) * scale + jnp.sum(weight * second * second)),
        (12, theta),
    ])
    numbers_ref[...] = jnp.concatenate(
        [row, share(1.0, norm0), share(1.0, norm1), jnp.zeros((5, LANES), F32)], axis=0)


def moment_kernel(own_rows, devices, odd_ref, partial_ref, swap_a_in, swap_b_in, weight_ref, scale_ref,
                  connectivity_ref, stiffness_ref, own0_ref, own1_ref, values0_ref, turned_ref, numbers_ref,
                  pick0_ref, pick1_ref, field_ref, values_ref, moments_ref):
    del pick0_ref, pick1_ref
    odd = odd_ref[0] == 1
    field = add_ends(partial_ref[...], odd, own_rows, swap_a_in[...], swap_b_in[...])
    field_ref[...] = field
    weight, scale = weight_ref[...], scale_ref[:1, :1]
    first, second = own0_ref[...], own1_ref[...]
    third = jnp.where(own_mask(own_rows), field, 0.0)
    phi = jnp.sum(first * third) * numbers_ref[1:2]
    psi = jnp.sum(second * third) * numbers_ref[2:3]
    third = third - psi * second - phi * first
    values0, values1 = values0_ref[...], turned_ref[...]
    values2 = jnp.concatenate(gather_corners(field, connectivity_ref[...]), axis=0)
    values_ref[...] = values2
    values2 = values2 - psi[:, :1] * values1 - phi[:, :1] * values0
    forces2 = matvec(stiffness_ref, [values2[c * CORNERS:(c + 1) * CORNERS] for c in range(3)])
    weighted = weight * third
    row = numbers_ref[:1] + entries([
        (3, jnp.sum(first * third)),
        (4, jnp.sum(second * third)),
        (5, jnp.sum(third * third)),
        (9, jnp.sum(values0 * forces2) * scale + jnp.sum(first * weighted)),
        (10, jnp.sum(values1 * forces2) * scale + jnp.sum(second * weighted)),
        (11, jnp.sum(values2 * forces2) * scale + jnp.sum(third * weighted)),
        (13, psi),
        (14, phi),
    ])
    moments_ref[...] = jnp.broadcast_to(row, (devices, LANES))


def step_weights(rows):
    column = [rows[:, i:i + 1] for i in range(15)]
    norms, energies, (theta, psi, phi) = column[:6], column[6:12], column[12:]

    def square(matrix, y):
        total = y[0] * y[0] * matrix[0]
        if len(y) > 1:
            total = total + y[1] * (2.0 * y[0] * matrix[1] + y[1] * matrix[2])
        if len(y) > 2:
            total = total + y[2] * (2.0 * (y[0] * matrix[3] + y[1] * matrix[4]) + y[2] * matrix[5])
        return jnp.sum(total, axis=0, keepdims=True)

    norm0 = jnp.sum(norms[0], axis=0, keepdims=True)
    step0 = norm0 / jnp.sum(energies[0], axis=0, keepdims=True)
    residual = [1.0 - step0 * theta, -step0]
    norm1 = square(norms, residual)
    turn0 = norm1 / norm0
    direction = [residual[0] + turn0, -step0]
    step1 = norm1 / square(energies, direction)
    lead = 1.0 + turn0
    residual = [
        residual[0] - step1 * (lead * theta - step0 * phi),
        -step0 - step1 * (lead - step0 * psi),
        step1 * step0,
    ]
    norm2 = square(norms, residual)
    turn1 = norm2 / norm1
    direction = [residual[0] + turn1 * direction[0], residual[1] - turn1 * step0, residual[2]]
    step2 = norm2 / square(energies, direction)
    return [
        step0 + step1 * lead + step2 * (1.0 + turn1 * lead),
        -step1 * step0 - step2 * (step0 + step1 * lead + turn1 * step0),
        step2 * step1 * step0,
    ]


def pick(values, code_ref, out_ref, blend):
    for start in range(0, code_ref.shape[1], LANES):
        sections = []
        for g in range(GROUPS):
            code = jnp.broadcast_to(code_ref[g:g + 1, start:start + LANES], (CORNERS, LANES))
            low, high = code & 127, code >> 7
            masks = [high == i for i in range(8)]
            for c in range(3):
                total = jnp.zeros((CORNERS, LANES), F32)
                for i in range(8):
                    tile = values[c * CORNERS:(c + 1) * CORNERS, i * LANES:(i + 1) * LANES]
                    total = jnp.where(masks[i], take_lanes(tile, low), total)
                sections.append(total)
        sections.append(jnp.zeros((CORNERS, LANES), F32))
        rows = pl.ds(start, LANES)
        out_ref[rows, :] = blend(jnp.concatenate(sections, axis=0).T, rows)


def pick_kernel(values_ref, code_ref, after_ref, out_ref):
    del after_ref
    pick(values_ref[...], code_ref, out_ref, lambda tile, rows: tile)


def blend_kernel(moments_ref, scale_ref, code_ref, pick0_ref, pick1_ref, values_ref, weights_ref, out_ref):
    weights = step_weights(moments_ref[...])
    weights = [weight * scale_ref[:1, :1] for weight in weights]
    weights_ref[...] = jnp.concatenate([jnp.broadcast_to(weight, (8, LANES)) for weight in weights], axis=0)

    def blend(tile, rows):
        return weights[0] * pick0_ref[rows, :] + weights[1] * pick1_ref[rows, :] + weights[2] * tile

    pick(values_ref[...], code_ref, out_ref, blend)


def motion_kernel(own_rows, rows_ref, place_ref, table_ref, weights_ref, first_ref, second_ref, third_ref,
                  displacement_hbm, out_hbm, displacement_ref, out_ref, sems):
    field = weights_ref[:1] * first_ref[...] + weights_ref[8:9] * second_ref[...] + weights_ref[16:17] * third_ref[...]
    for c in range(3):
        for h in range(own_rows):
            displacement_ref[c:c + 1, h * LANES:(h + 1) * LANES] = field[c * FIELD_ROWS + h:c * FIELD_ROWS + h + 1]
    copies = [pltpu.make_async_copy(displacement_ref, displacement_hbm, sems.at[0])]
    copies[0].start()
    high, low = split(rows_ref[...].T)
    slots, faces = rows_ref.shape[0], place_ref.shape[1]
    place, group = place_ref[0:1], place_ref[1:2]
    found = dot_nn(jnp.concatenate([high, low], axis=0), onehot(iota((slots, faces), 0) == place))
    found = found[:LANES] + found[LANES:]
    owned = jnp.zeros((DOF, faces), F32)
    for g in range(GROUPS):
        owned = jnp.where(group == g, found[g * DOF:(g + 1) * DOF], owned)
    upper = owned.astype(BF16).astype(F32)
    lower = owned - upper
    parts = jnp.concatenate([upper, lower, upper], axis=0).T.astype(BF16)
    table_high, table_low = split(table_ref[...])
    right = jnp.concatenate([table_high, table_high, table_low], axis=0)
    for i, start in enumerate(range(0, faces, WIDE)):
        out_ref[start:start + WIDE, :] = dot_nn(parts[start:start + WIDE], right)
        copy = pltpu.make_async_copy(
            out_ref.at[pl.ds(start, WIDE)], out_hbm.at[pl.ds(start, WIDE)], sems.at[1 + i])
        copy.start()
        copies.append(copy)
    for copy in copies:
        copy.wait()


def call(kernel, outs, args, scalars=0, hbm=(), outs_hbm=(), scratch=(), time=1.0):
    in_specs = []
    for i in range(len(args)):
        if i < scalars:
            in_specs.append(pl.BlockSpec(memory_space=pltpu.SMEM))
        elif i in hbm:
            in_specs.append(pl.BlockSpec(memory_space=pltpu.HBM))
        else:
            in_specs.append(pl.BlockSpec(memory_space=pltpu.VMEM))
    return pl.pallas_call(
        kernel,
        name=getattr(kernel, "func", kernel).__name__,
        out_shape=[jax.ShapeDtypeStruct(shape, dtype) for shape, dtype in outs],
        in_specs=in_specs,
        out_specs=[
            pl.BlockSpec(memory_space=pltpu.HBM if i in outs_hbm else pltpu.VMEM) for i in range(len(outs))
        ],
        scratch_shapes=list(scratch),
        cost_estimate=pl.CostEstimate(flops=int(time * 1e9), transcendentals=0, bytes_accessed=int(time * 1e6)),
        compiler_params=pltpu.CompilerParams(vmem_limit_bytes=VMEM_BYTES),
    )(*[pltpu.with_memory_space_constraint(arg, pltpu.HBM) if i in hbm else arg for i, arg in enumerate(args)])


def shards(pressure, face_owner, face_element, shape_table, stiffness, connectivity, support):
    devices = lax.axis_size(AXES)
    faces = pressure.shape[0]
    elements = stiffness.shape[2]
    nodes = support.shape[1]
    own_rows = nodes // LANES
    capacity = max(2, (5 * faces + 2 * devices - 1) // (2 * devices))
    per = (capacity + GROUPS - 1) // GROUPS
    slots = devices * per
    odd = (lax.axis_index(AXES) % 2).astype(jnp.int32).reshape(1)
    evens = [(i, i + 1) for i in range(0, devices - 1, 2)]
    odds = [(i, i + 1) for i in range(1, devices - 1, 2)]
    pairs_a = evens + [(j, i) for i, j in evens]
    pairs_b = odds + [(j, i) for i, j in odds]

    def swap(a, b):
        return lax.ppermute(a, AXES, pairs_a), lax.ppermute(b, AXES, pairs_b)

    def everywhere(rows):
        return lax.all_to_all(rows, AXES, split_axis=0, concat_axis=0, tiled=True)

    field = ((3 * FIELD_ROWS, LANES), F32)
    values = ((DOF, elements), F32)
    ends = ((8, LANES), F32)
    block = ((slots, LANES), F32)
    sent, place = call(
        functools.partial(send_kernel, devices, per),
        [block, ((8, faces), jnp.int32)],
        (odd, pressure, face_owner.reshape(1, faces), face_element.reshape(1, faces), shape_table, support, stiffness),
        scalars=1,
        hbm=range(1, 7),
        scratch=(
            pltpu.VMEM(pressure.shape, F32),
            pltpu.VMEM((1, faces), jnp.int32),
            pltpu.VMEM((1, faces), jnp.int32),
            pltpu.VMEM(shape_table.shape, F32),
            pltpu.VMEM(support.shape, F32),
            pltpu.VMEM((DOF, elements), F32),
            pltpu.SemaphoreType.DMA((5 + DOF,)),
        ),
    )
    arrived = everywhere(sent)
    partial, end_a, end_b, weight, scale, codes = call(
        functools.partial(load_kernel, devices, per),
        [field, ends, ends, field, ends, ((8, slots), jnp.int32)],
        (odd, arrived, connectivity, support),
        scalars=1,
        scratch=(pltpu.VMEM((DOF, elements), F32),),
    )
    stage = (
        functools.partial(product_kernel, own_rows),
        [field, values, values, field, ends, ends],
    )
    end_a, end_b = swap(end_a, end_b)
    (columns,) = call(
        columns_kernel, [((CORNERS, elements, LANES), BF16)], (connectivity, end_a), time=0.1)
    first, values0, forces0, partial, end_a, end_b = call(
        *stage, (odd, partial, end_a, end_b, weight, scale, connectivity, stiffness, columns), scalars=1)
    end_a, end_b = swap(end_a, end_b)
    (pick0,) = call(pick_kernel, [block], (values0, codes, end_a), time=0.1)
    second, values1, forces1, partial, end_a, end_b = call(
        *stage, (odd, partial, end_a, end_b, weight, scale, connectivity, stiffness, columns), scalars=1)
    end_a, end_b = swap(end_a, end_b)
    (pick1,) = call(pick_kernel, [block], (values1, codes, end_a), time=0.1)
    own0, own1, turned, numbers = call(
        functools.partial(lower_kernel, own_rows),
        [field, field, values, ends],
        (weight, scale, first, second, values0, values1, forces0, forces1, end_a),
        time=0.1,
    )
    third, values2, moments = call(
        functools.partial(moment_kernel, own_rows, devices),
        [field, values, ((devices, LANES), F32)],
        (odd, partial, end_a, end_b, weight, scale, connectivity, stiffness, own0, own1, values0, turned, numbers,
         pick0, pick1),
        scalars=1,
    )
    moments = everywhere(moments)
    weights, leaving = call(
        blend_kernel,
        [((24, LANES), F32), block],
        (moments, scale, codes, pick0, pick1, values2),
    )
    returned = everywhere(leaving)
    return call(
        functools.partial(motion_kernel, own_rows),
        [((3, nodes), F32), ((faces, LANES), F32)],
        (returned, place, shape_table, weights, first, second, third),
        outs_hbm=(0, 1),
        scratch=(
            pltpu.VMEM((3, nodes), F32),
            pltpu.VMEM((faces, LANES), F32),
            pltpu.SemaphoreType.DMA((1 + faces // WIDE,)),
        ),
    )


def solution(mesh):
    in_specs = (
        P(AXES, None),
        P(AXES, None),
        P(AXES),
        P(),
        P(None, None, AXES),
        P(None, AXES),
        P(None, AXES),
    )
    out_specs = (P(None, AXES), P(AXES, None))
    return jax.shard_map(shards, mesh=mesh, in_specs=in_specs, out_specs=out_specs, check_vma=False)
```

```python
import functools

import jax
import jax.numpy as jnp
from jax import lax
from jax.experimental import pallas as pl
from jax.experimental.pallas import tpu as pltpu
from jax.sharding import PartitionSpec as P

AXES = ("fluid", "solid")
DOF = 24
CORNERS = 8
GROUPS = 5
FIELD_ROWS = 16
LANES = 128
WIDE = 256
VMEM_BYTES = 24 * 1024 * 1024
F32 = jnp.float32
BF16 = jnp.bfloat16


def iota(shape, axis):
    return lax.broadcasted_iota(jnp.int32, shape, axis)


def onehot(mask):
    return jnp.where(mask, 1.0, 0.0).astype(BF16)


def split(value):
    high = value.astype(BF16)
    return high, (value - high.astype(F32)).astype(BF16)


def dot_nt(left, right):
    return lax.dot_general(left, right, (((1,), (1,)), ((), ())), preferred_element_type=F32)


def dot_nn(left, right):
    return lax.dot_general(left, right, (((1,), (0,)), ((), ())), preferred_element_type=F32)


def take_lanes(table, index):
    return jnp.take_along_axis(table, index, axis=1, mode="promise_in_bounds")


def gather_corners(field, connectivity):
    elements = connectivity.shape[1]
    rows = {}
    for c in range(3):
        for h in range(9):
            rows[c, h] = jnp.broadcast_to(field[c * FIELD_ROWS + h:c * FIELD_ROWS + h + 1], (CORNERS, LANES))
    parts = [[], [], []]
    for start in range(0, elements, LANES):
        index = connectivity[:, start:start + LANES]
        low, high = index & 127, index >> 7
        masks = [high == h for h in range(9)]
        for c in range(3):
            total = jnp.zeros((CORNERS, LANES), F32)
            for h in range(9):
                total = jnp.where(masks[h], take_lanes(rows[c, h], low), total)
            parts[c].append(total)
    return [jnp.concatenate(part, axis=1) for part in parts]


def assemble(terms, connectivity, columns_ref=None):
    elements = connectivity.shape[1]
    high, low = connectivity >> 7, connectivity & 127
    upper = terms.astype(BF16).astype(F32)
    lower = terms - upper
    total = jnp.zeros((6 * FIELD_ROWS, LANES), F32)
    for k in range(CORNERS):
        mask = iota((FIELD_ROWS, elements), 0) == high[k:k + 1]
        pieces = [
            jnp.where(mask, part[c * CORNERS + k:c * CORNERS + k + 1], 0.0)
            for part in (upper, lower)
            for c in range(3)
        ]
        left = jnp.concatenate(pieces, axis=0).astype(BF16)
        if columns_ref is None:
            total = total + dot_nt(left, onehot(iota((LANES, elements), 0) == low[k:k + 1]))
        else:
            total = total + dot_nn(left, columns_ref[k])
    return total[:3 * FIELD_ROWS] + total[3 * FIELD_ROWS:]


def columns_kernel(connectivity_ref, after_ref, out_ref):
    del after_ref
    low = connectivity_ref[...] & 127
    for k in range(CORNERS):
        out_ref[k] = jnp.where(iota((LANES, low.shape[1]), 0) == low[k:k + 1], 1.0, 0.0).T.astype(BF16)


def matvec(stiffness, values):
    elements = stiffness.shape[2]
    parts = []
    for start in range(0, elements, 128):
        total = jnp.zeros((DOF, 128), F32)
        for b in range(DOF):
            total = total + stiffness[b, :, start:start + 128] * values[b // 8][b % 8:b % 8 + 1, start:start + 128]
        parts.append(total)
    return jnp.concatenate(parts, axis=1)


def put_ends(partial, odd, own_rows, swap_a_ref, swap_b_ref):
    pad = [jnp.zeros((5, LANES), F32)]
    first = jnp.concatenate([partial[c * FIELD_ROWS:c * FIELD_ROWS + 1] for c in range(3)] + pad, axis=0)
    over = jnp.concatenate(
        [partial[c * FIELD_ROWS + own_rows:c * FIELD_ROWS + own_rows + 1] for c in range(3)] + pad, axis=0)
    swap_a_ref[...] = jnp.where(odd, first, over)
    swap_b_ref[...] = jnp.where(odd, over, first)


def add_ends(partial, odd, own_rows, swap_a, swap_b):
    before = jnp.where(odd, swap_a, swap_b)
    after = jnp.where(odd, swap_b, swap_a)
    pieces = []
    for c in range(3):
        pieces += [
            before[c:c + 1],
            jnp.zeros((own_rows - 1, LANES), F32),
            after[c:c + 1],
            jnp.zeros((FIELD_ROWS - own_rows - 1, LANES), F32),
        ]
    return partial + jnp.concatenate(pieces, axis=0)


def own_mask(own_rows):
    return (iota((3 * FIELD_ROWS, LANES), 0) % FIELD_ROWS) < own_rows


def as_field(rows, own_rows):
    pieces = []
    for c in range(3):
        pieces += [rows[c:c + 1, h * LANES:(h + 1) * LANES] for h in range(own_rows)]
        pieces.append(jnp.zeros((FIELD_ROWS - own_rows, LANES), F32))
    return jnp.concatenate(pieces, axis=0)


def send_kernel(devices, per, odd_ref, pressure_hbm, owner_hbm, element_hbm, table_hbm, support_hbm, stiffness_hbm,
                out_ref, place_ref, pressure_ref, owner_ref, element_ref, table_ref, support_ref, diagonal_ref, sems):
    del odd_ref
    moves = [(owner_hbm, owner_ref), (element_hbm, element_ref), (table_hbm, table_ref), (pressure_hbm, pressure_ref),
             (support_hbm, support_ref)]
    moves += [
        (stiffness_hbm.at[c * CORNERS, pl.ds(c * CORNERS, 1)], diagonal_ref.at[pl.ds(c, 1)]) for c in range(3)]
    copies = [pltpu.make_async_copy(source, target, sems.at[i]) for i, (source, target) in enumerate(moves)]
    for copy in copies:
        copy.start()
    for copy in copies:
        copy.wait()
    faces = pressure_ref.shape[0]
    target = owner_ref[...]
    named = iota((devices, faces), 0) == target
    named16 = onehot(named)
    blocks = range(0, faces, WIDE)
    upto = onehot(iota((WIDE, WIDE), 0) <= iota((WIDE, WIDE), 1))
    counts = dot_nn(jnp.concatenate([named16[:, start:start + WIDE] for start in blocks], axis=0), upto)
    before = jnp.zeros((devices, 1), F32)
    ranks = []
    for i, start in enumerate(blocks):
        count = counts[i * devices:(i + 1) * devices]
        here = jnp.where(named[:, start:start + WIDE], count + before, 0.0)
        ranks.append(jnp.sum(here, axis=0, keepdims=True))
        before = before + count[:, WIDE - 1:]
    rank = jnp.concatenate(ranks, axis=1).astype(jnp.int32) - 1
    group = jnp.zeros_like(rank)
    for i in range(1, GROUPS):
        group = group + (rank >= i * per).astype(jnp.int32)
    place = target * per + rank - group * per
    place_ref[...] = jnp.concatenate([place, group, jnp.zeros((6, faces), jnp.int32)], axis=0)
    chosen = onehot(iota((devices * per, faces), 0) == place)

    pad = jnp.zeros((LANES - GROUPS * DOF, table_ref.shape[1]), F32)
    table_high, table_low = split(jnp.concatenate([table_ref[...]] * GROUPS + [pad], axis=0))
    rows_high, rows_low = split(pressure_ref[...])
    projected = dot_nt(
        jnp.concatenate([table_high, table_low, table_high], axis=1),
        jnp.concatenate([rows_high, rows_high, rows_low], axis=1),
    )
    spread = [jnp.where(group == i, projected[i * DOF:(i + 1) * DOF], 0.0) for i in range(GROUPS)]
    spread.append(jnp.where(iota((8, faces), 0) == group, element_ref[...].astype(F32), 0.0))
    spread_high, spread_low = split(jnp.concatenate(spread, axis=0))
    sent = dot_nt(chosen, jnp.concatenate([spread_high, spread_low], axis=0))

    trace = CORNERS * jnp.sum(diagonal_ref[...]) + jnp.sum(support_ref[...])
    out_ref[...] = jnp.where(iota((devices * per, LANES), 1) == 125, trace, sent[:, :LANES] + sent[:, LANES:])


def load_kernel(devices, per, odd_ref, rows_ref, connectivity_ref, support_ref,
                partial_ref, swap_a_ref, swap_b_ref, weight_ref, scale_ref, code_ref, loads_ref):
    nodes = support_ref.shape[1]
    own_rows = nodes // LANES

    @pl.when(odd_ref[0] >= 0)
    def _():
        rows = rows_ref[...]
        arrived = rows.T
        codes = arrived[GROUPS * DOF:].astype(jnp.int32)
        code_ref[...] = codes
        slots = rows.shape[0]
        total = jnp.zeros((4 * 2 * DOF, WIDE), F32)
        for g in range(GROUPS):
            terms = arrived[g * DOF:(g + 1) * DOF]
            upper = terms.astype(BF16).astype(F32)
            both = jnp.concatenate([upper, terms - upper], axis=0)
            code = codes[g:g + 1]
            left = jnp.concatenate([jnp.where((code >> 8) == i, both, 0.0) for i in range(4)], axis=0).astype(BF16)
            total = total + dot_nt(left, onehot(iota((WIDE, slots), 0) == (code & 255)))
        for i in range(4):
            start = i * 2 * DOF
            loads_ref[:, i * WIDE:(i + 1) * WIDE] = total[start:start + DOF] + total[start + DOF:start + 2 * DOF]

    partial = assemble(loads_ref[...], connectivity_ref[...])
    partial_ref[...] = partial
    put_ends(partial, odd_ref[0] == 1, own_rows, swap_a_ref, swap_b_ref)
    trace = jnp.sum(rows_ref[:, 125:126]) * (1.0 / per)
    inverse = jnp.full((8, LANES), 3.0 * nodes * devices, F32) / jnp.full((8, LANES), trace, F32)
    scale_ref[...] = inverse
    weight_ref[...] = as_field(support_ref[...], own_rows) * inverse[:1, :1]


def product_kernel(own_rows, odd_ref, partial_ref, swap_a_in, swap_b_in, weight_ref, scale_ref, connectivity_ref,
                   stiffness_ref, columns_ref, field_ref, values_ref, forces_ref, next_ref, swap_a_ref, swap_b_ref):
    odd = odd_ref[0] == 1

    @pl.when(odd_ref[0] >= 0)
    def _():
        field = add_ends(partial_ref[...], odd, own_rows, swap_a_in[...], swap_b_in[...])
        field_ref[...] = field
        values = gather_corners(field, connectivity_ref[...])
        values_ref[...] = jnp.concatenate(values, axis=0)
        forces_ref[...] = matvec(stiffness_ref, values)

    partial = assemble(forces_ref[...], connectivity_ref[...], columns_ref)
    partial = partial * scale_ref[:1, :1] + weight_ref[...] * field_ref[...]
    next_ref[...] = partial
    put_ends(partial, odd, own_rows, swap_a_ref, swap_b_ref)


def entries(pairs):
    lane = iota((1, LANES), 1)
    row = jnp.zeros((1, LANES), F32)
    for i, value in pairs:
        row = jnp.where(lane == i, value, row)
    return row


def share(value, norm):
    return jnp.full((1, LANES), value, F32) / jnp.maximum(jnp.full((1, LANES), norm, F32), 1e-30)


def lower_kernel(own_rows, weight_ref, scale_ref, first_ref, second_ref, values0_ref, values1_ref,
                 forces0_ref, forces1_ref, after_ref, own0_ref, own1_ref, turned_ref, numbers_ref):
    del after_ref
    own, weight = own_mask(own_rows), weight_ref[...]
    first, second = jnp.where(own, first_ref[...], 0.0), jnp.where(own, second_ref[...], 0.0)
    norm0 = jnp.sum(first * first)
    theta = share(jnp.sum(first * second), norm0)
    second = second - theta * first
    own0_ref[...], own1_ref[...] = first, second
    scale, part = scale_ref[:1, :1], theta[:, :1]
    values0, forces0 = values0_ref[...], forces0_ref[...]
    values1, forces1 = values1_ref[...] - part * values0, forces1_ref[...] - part * forces0
    turned_ref[...] = values1
    norm1 = jnp.sum(second * second)
    row = entries([
        (0, norm0),
        (1, jnp.sum(first * second)),
        (2, norm1),
        (6, jnp.sum(values0 * forces0) * scale + jnp.sum(weight * first * first)),
        (7, jnp.sum(values0 * forces1) * scale + jnp.sum(weight * first * second)),
        (8, jnp.sum(values1 * forces1) * scale + jnp.sum(weight * second * second)),
        (12, theta),
    ])
    numbers_ref[...] = jnp.concatenate(
        [row, share(1.0, norm0), share(1.0, norm1), jnp.zeros((5, LANES), F32)], axis=0)


def moment_kernel(own_rows, devices, odd_ref, partial_ref, swap_a_in, swap_b_in, weight_ref, scale_ref,
                  connectivity_ref, stiffness_ref, own0_ref, own1_ref, values0_ref, turned_ref, numbers_ref,
                  pick0_ref, pick1_ref, field_ref, values_ref, moments_ref):
    del pick0_ref, pick1_ref
    odd = odd_ref[0] == 1
    field = add_ends(partial_ref[...], odd, own_rows, swap_a_in[...], swap_b_in[...])
    field_ref[...] = field
    weight, scale = weight_ref[...], scale_ref[:1, :1]
    first, second = own0_ref[...], own1_ref[...]
    third = jnp.where(own_mask(own_rows), field, 0.0)
    phi = jnp.sum(first * third) * numbers_ref[1:2]
    psi = jnp.sum(second * third) * numbers_ref[2:3]
    third = third - psi * second - phi * first
    values0, values1 = values0_ref[...], turned_ref[...]
    values2 = jnp.concatenate(gather_corners(field, connectivity_ref[...]), axis=0)
    values_ref[...] = values2
    values2 = values2 - psi[:, :1] * values1 - phi[:, :1] * values0
    forces2 = matvec(stiffness_ref, [values2[c * CORNERS:(c + 1) * CORNERS] for c in range(3)])
    weighted = weight * third
    row = numbers_ref[:1] + entries([
        (3, jnp.sum(first * third)),
        (4, jnp.sum(second * third)),
        (5, jnp.sum(third * third)),
        (9, jnp.sum(values0 * forces2) * scale + jnp.sum(first * weighted)),
        (10, jnp.sum(values1 * forces2) * scale + jnp.sum(second * weighted)),
        (11, jnp.sum(values2 * forces2) * scale + jnp.sum(third * weighted)),
        (13, psi),
        (14, phi),
    ])
    moments_ref[...] = jnp.broadcast_to(row, (devices, LANES))


def step_weights(rows):
    column = [rows[:, i:i + 1] for i in range(15)]
    norms, energies, (theta, psi, phi) = column[:6], column[6:12], column[12:]

    def square(matrix, y):
        total = y[0] * y[0] * matrix[0]
        if len(y) > 1:
            total = total + y[1] * (2.0 * y[0] * matrix[1] + y[1] * matrix[2])
        if len(y) > 2:
            total = total + y[2] * (2.0 * (y[0] * matrix[3] + y[1] * matrix[4]) + y[2] * matrix[5])
        return jnp.sum(total, axis=0, keepdims=True)

    norm0 = jnp.sum(norms[0], axis=0, keepdims=True)
    step0 = norm0 / jnp.sum(energies[0], axis=0, keepdims=True)
    residual = [1.0 - step0 * theta, -step0]
    norm1 = square(norms, residual)
    turn0 = norm1 / norm0
    direction = [residual[0] + turn0, -step0]
    step1 = norm1 / square(energies, direction)
    lead = 1.0 + turn0
    residual = [
        residual[0] - step1 * (lead * theta - step0 * phi),
        -step0 - step1 * (lead - step0 * psi),
        step1 * step0,
    ]
    norm2 = square(norms, residual)
    turn1 = norm2 / norm1
    direction = [residual[0] + turn1 * direction[0], residual[1] - turn1 * step0, residual[2]]
    step2 = norm2 / square(energies, direction)
    return [
        step0 + step1 * lead + step2 * (1.0 + turn1 * lead),
        -step1 * step0 - step2 * (step0 + step1 * lead + turn1 * step0),
        step2 * step1 * step0,
    ]


def pick(values, code_ref, out_ref, blend):
    for start in range(0, code_ref.shape[1], LANES):
        sections = []
        for g in range(GROUPS):
            code = jnp.broadcast_to(code_ref[g:g + 1, start:start + LANES], (CORNERS, LANES))
            low, high = code & 127, code >> 7
            masks = [high == i for i in range(8)]
            for c in range(3):
                total = jnp.zeros((CORNERS, LANES), F32)
                for i in range(8):
                    tile = values[c * CORNERS:(c + 1) * CORNERS, i * LANES:(i + 1) * LANES]
                    total = jnp.where(masks[i], take_lanes(tile, low), total)
                sections.append(total)
        sections.append(jnp.zeros((CORNERS, LANES), F32))
        rows = pl.ds(start, LANES)
        out_ref[rows, :] = blend(jnp.concatenate(sections, axis=0).T, rows)


def pick_kernel(values_ref, code_ref, after_ref, out_ref):
    del after_ref
    pick(values_ref[...], code_ref, out_ref, lambda tile, rows: tile)


def blend_kernel(moments_ref, scale_ref, code_ref, pick0_ref, pick1_ref, values_ref, weights_ref, out_ref):
    weights = step_weights(moments_ref[...])
    weights = [weight * scale_ref[:1, :1] for weight in weights]
    weights_ref[...] = jnp.concatenate([jnp.broadcast_to(weight, (8, LANES)) for weight in weights], axis=0)

    def blend(tile, rows):
        return weights[0] * pick0_ref[rows, :] + weights[1] * pick1_ref[rows, :] + weights[2] * tile

    pick(values_ref[...], code_ref, out_ref, blend)


def motion_kernel(own_rows, rows_ref, place_ref, table_ref, weights_ref, first_ref, second_ref, third_ref,
                  displacement_hbm, out_hbm, displacement_ref, out_ref, sems):
    field = weights_ref[:1] * first_ref[...] + weights_ref[8:9] * second_ref[...] + weights_ref[16:17] * third_ref[...]
    for c in range(3):
        for h in range(own_rows):
            displacement_ref[c:c + 1, h * LANES:(h + 1) * LANES] = field[c * FIELD_ROWS + h:c * FIELD_ROWS + h + 1]
    copies = [pltpu.make_async_copy(displacement_ref, displacement_hbm, sems.at[0])]
    copies[0].start()
    high, low = split(rows_ref[...].T)
    slots, faces = rows_ref.shape[0], place_ref.shape[1]
    place, group = place_ref[0:1], place_ref[1:2]
    found = dot_nn(jnp.concatenate([high, low], axis=0), onehot(iota((slots, faces), 0) == place))
    found = found[:LANES] + found[LANES:]
    owned = jnp.zeros((DOF, faces), F32)
    for g in range(GROUPS):
        owned = jnp.where(group == g, found[g * DOF:(g + 1) * DOF], owned)
    upper = owned.astype(BF16).astype(F32)
    lower = owned - upper
    parts = jnp.concatenate([upper, lower, upper], axis=0).T.astype(BF16)
    table_high, table_low = split(table_ref[...])
    right = jnp.concatenate([table_high, table_high, table_low], axis=0)
    for i, start in enumerate(range(0, faces, WIDE)):
        out_ref[start:start + WIDE, :] = dot_nn(parts[start:start + WIDE], right)
        copy = pltpu.make_async_copy(
            out_ref.at[pl.ds(start, WIDE)], out_hbm.at[pl.ds(start, WIDE)], sems.at[1 + i])
        copy.start()
        copies.append(copy)
    for copy in copies:
        copy.wait()


def call(kernel, outs, args, scalars=0, hbm=(), outs_hbm=(), scratch=(), time=1.0):
    in_specs = []
    for i in range(len(args)):
        if i < scalars:
            in_specs.append(pl.BlockSpec(memory_space=pltpu.SMEM))
        elif i in hbm:
            in_specs.append(pl.BlockSpec(memory_space=pltpu.HBM))
        else:
            in_specs.append(pl.BlockSpec(memory_space=pltpu.VMEM))
    return pl.pallas_call(
        kernel,
        name=getattr(kernel, "func", kernel).__name__,
        out_shape=[jax.ShapeDtypeStruct(shape, dtype) for shape, dtype in outs],
        in_specs=in_specs,
        out_specs=[
            pl.BlockSpec(memory_space=pltpu.HBM if i in outs_hbm else pltpu.VMEM) for i in range(len(outs))
        ],
        scratch_shapes=list(scratch),
        cost_estimate=pl.CostEstimate(flops=int(time * 1e9), transcendentals=0, bytes_accessed=int(time * 1e6)),
        compiler_params=pltpu.CompilerParams(vmem_limit_bytes=VMEM_BYTES),
    )(*[pltpu.with_memory_space_constraint(arg, pltpu.HBM) if i in hbm else arg for i, arg in enumerate(args)])


def shards(pressure, face_owner, face_element, shape_table, stiffness, connectivity, support):
    devices = lax.axis_size(AXES)
    faces = pressure.shape[0]
    elements = stiffness.shape[2]
    nodes = support.shape[1]
    own_rows = nodes // LANES
    capacity = max(2, (5 * faces + 2 * devices - 1) // (2 * devices))
    per = (capacity + GROUPS - 1) // GROUPS
    slots = devices * per
    odd = (lax.axis_index(AXES) % 2).astype(jnp.int32).reshape(1)
    evens = [(i, i + 1) for i in range(0, devices - 1, 2)]
    odds = [(i, i + 1) for i in range(1, devices - 1, 2)]
    pairs_a = evens + [(j, i) for i, j in evens]
    pairs_b = odds + [(j, i) for i, j in odds]

    def swap(a, b):
        return lax.ppermute(a, AXES, pairs_a), lax.ppermute(b, AXES, pairs_b)

    def everywhere(rows):
        return lax.all_to_all(rows, AXES, split_axis=0, concat_axis=0, tiled=True)

    field = ((3 * FIELD_ROWS, LANES), F32)
    values = ((DOF, elements), F32)
    ends = ((8, LANES), F32)
    block = ((slots, LANES), F32)
    sent, place = call(
        functools.partial(send_kernel, devices, per),
        [block, ((8, faces), jnp.int32)],
        (odd, pressure, face_owner.reshape(1, faces), face_element.reshape(1, faces), shape_table, support, stiffness),
        scalars=1,
        hbm=range(1, 7),
        scratch=(
            pltpu.VMEM(pressure.shape, F32),
            pltpu.VMEM((1, faces), jnp.int32),
            pltpu.VMEM((1, faces), jnp.int32),
            pltpu.VMEM(shape_table.shape, F32),
            pltpu.VMEM(support.shape, F32),
            pltpu.VMEM((3, elements), F32),
            pltpu.SemaphoreType.DMA((8,)),
        ),
    )
    arrived = everywhere(sent)
    partial, end_a, end_b, weight, scale, codes = call(
        functools.partial(load_kernel, devices, per),
        [field, ends, ends, field, ends, ((8, slots), jnp.int32)],
        (odd, arrived, connectivity, support),
        scalars=1,
        scratch=(pltpu.VMEM((DOF, elements), F32),),
    )
    stage = (
        functools.partial(product_kernel, own_rows),
        [field, values, values, field, ends, ends],
    )
    end_a, end_b = swap(end_a, end_b)
    (columns,) = call(
        columns_kernel, [((CORNERS, elements, LANES), BF16)], (connectivity, end_a), time=0.1)
    first, values0, forces0, partial, end_a, end_b = call(
        *stage, (odd, partial, end_a, end_b, weight, scale, connectivity, stiffness, columns), scalars=1)
    end_a, end_b = swap(end_a, end_b)
    (pick0,) = call(pick_kernel, [block], (values0, codes, end_a), time=0.1)
    second, values1, forces1, partial, end_a, end_b = call(
        *stage, (odd, partial, end_a, end_b, weight, scale, connectivity, stiffness, columns), scalars=1)
    end_a, end_b = swap(end_a, end_b)
    (pick1,) = call(pick_kernel, [block], (values1, codes, end_a), time=0.1)
    own0, own1, turned, numbers = call(
        functools.partial(lower_kernel, own_rows),
        [field, field, values, ends],
        (weight, scale, first, second, values0, values1, forces0, forces1, end_a),
        time=0.1,
    )
    third, values2, moments = call(
        functools.partial(moment_kernel, own_rows, devices),
        [field, values, ((devices, LANES), F32)],
        (odd, partial, end_a, end_b, weight, scale, connectivity, stiffness, own0, own1, values0, turned, numbers,
         pick0, pick1),
        scalars=1,
    )
    moments = everywhere(moments)
    weights, leaving = call(
        blend_kernel,
        [((24, LANES), F32), block],
        (moments, scale, codes, pick0, pick1, values2),
    )
    returned = everywhere(leaving)
    return call(
        functools.partial(motion_kernel, own_rows),
        [((3, nodes), F32), ((faces, LANES), F32)],
        (returned, place, shape_table, weights, first, second, third),
        outs_hbm=(0, 1),
        scratch=(
            pltpu.VMEM((3, nodes), F32),
            pltpu.VMEM((faces, LANES), F32),
            pltpu.SemaphoreType.DMA((1 + faces // WIDE,)),
        ),
    )


def solution(mesh):
    in_specs = (
        P(AXES, None),
        P(AXES, None),
        P(AXES),
        P(),
        P(None, None, AXES),
        P(None, AXES),
        P(None, AXES),
    )
    out_specs = (P(None, AXES), P(AXES, None))
    return jax.shard_map(shards, mesh=mesh, in_specs=in_specs, out_specs=out_specs, check_vma=False)
```

```python
import functools

import jax
import jax.numpy as jnp
from jax import lax
from jax.experimental import pallas as pl
from jax.experimental.pallas import tpu as pltpu
from jax.sharding import PartitionSpec as P

AXES = ("fluid", "solid")
DOF = 24
CORNERS = 8
GROUPS = 5
FIELD_ROWS = 16
LANES = 128
WIDE = 256
VMEM_BYTES = 24 * 1024 * 1024
F32 = jnp.float32
BF16 = jnp.bfloat16


def iota(shape, axis):
    return lax.broadcasted_iota(jnp.int32, shape, axis)


def onehot(mask):
    return jnp.where(mask, 1.0, 0.0).astype(BF16)


def split(value):
    high = value.astype(BF16)
    return high, (value - high.astype(F32)).astype(BF16)


def dot_nt(left, right):
    return lax.dot_general(left, right, (((1,), (1,)), ((), ())), preferred_element_type=F32)


def dot_nn(left, right):
    return lax.dot_general(left, right, (((1,), (0,)), ((), ())), preferred_element_type=F32)


def take_lanes(table, index):
    return jnp.take_along_axis(table, index, axis=1, mode="promise_in_bounds")


def gather_corners(field, connectivity):
    elements = connectivity.shape[1]
    rows = {}
    for c in range(3):
        for h in range(9):
            rows[c, h] = jnp.broadcast_to(field[c * FIELD_ROWS + h:c * FIELD_ROWS + h + 1], (CORNERS, LANES))
    parts = [[], [], []]
    for start in range(0, elements, LANES):
        index = connectivity[:, start:start + LANES]
        low, high = index & 127, index >> 7
        masks = [high == h for h in range(9)]
        for c in range(3):
            total = jnp.zeros((CORNERS, LANES), F32)
            for h in range(9):
                total = jnp.where(masks[h], take_lanes(rows[c, h], low), total)
            parts[c].append(total)
    return [jnp.concatenate(part, axis=1) for part in parts]


def assemble(terms, connectivity, columns_ref=None):
    elements = connectivity.shape[1]
    high, low = connectivity >> 7, connectivity & 127
    upper = terms.astype(BF16).astype(F32)
    lower = terms - upper
    total = jnp.zeros((6 * FIELD_ROWS, LANES), F32)
    for k in range(CORNERS):
        mask = iota((FIELD_ROWS, elements), 0) == high[k:k + 1]
        pieces = [
            jnp.where(mask, part[c * CORNERS + k:c * CORNERS + k + 1], 0.0)
            for part in (upper, lower)
            for c in range(3)
        ]
        left = jnp.concatenate(pieces, axis=0).astype(BF16)
        if columns_ref is None:
            total = total + dot_nt(left, onehot(iota((LANES, elements), 0) == low[k:k + 1]))
        else:
            total = total + dot_nn(left, columns_ref[k])
    return total[:3 * FIELD_ROWS] + total[3 * FIELD_ROWS:]


def columns_kernel(connectivity_ref, after_ref, out_ref):
    del after_ref
    low = connectivity_ref[...] & 127
    for k in range(CORNERS):
        out_ref[k] = jnp.where(iota((LANES, low.shape[1]), 0) == low[k:k + 1], 1.0, 0.0).T.astype(BF16)


def matvec(stiffness, values):
    elements = stiffness.shape[2]
    parts = []
    for start in range(0, elements, 128):
        total = jnp.zeros((DOF, 128), F32)
        for b in range(DOF):
            total = total + stiffness[b, :, start:start + 128] * values[b // 8][b % 8:b % 8 + 1, start:start + 128]
        parts.append(total)
    return jnp.concatenate(parts, axis=1)


def put_ends(partial, odd, own_rows, swap_a_ref, swap_b_ref):
    pad = [jnp.zeros((5, LANES), F32)]
    first = jnp.concatenate([partial[c * FIELD_ROWS:c * FIELD_ROWS + 1] for c in range(3)] + pad, axis=0)
    over = jnp.concatenate(
        [partial[c * FIELD_ROWS + own_rows:c * FIELD_ROWS + own_rows + 1] for c in range(3)] + pad, axis=0)
    swap_a_ref[...] = jnp.where(odd, first, over)
    swap_b_ref[...] = jnp.where(odd, over, first)


def add_ends(partial, odd, own_rows, swap_a, swap_b):
    before = jnp.where(odd, swap_a, swap_b)
    after = jnp.where(odd, swap_b, swap_a)
    pieces = []
    for c in range(3):
        pieces += [
            before[c:c + 1],
            jnp.zeros((own_rows - 1, LANES), F32),
            after[c:c + 1],
            jnp.zeros((FIELD_ROWS - own_rows - 1, LANES), F32),
        ]
    return partial + jnp.concatenate(pieces, axis=0)


def own_mask(own_rows):
    return (iota((3 * FIELD_ROWS, LANES), 0) % FIELD_ROWS) < own_rows


def as_field(rows, own_rows):
    pieces = []
    for c in range(3):
        pieces += [rows[c:c + 1, h * LANES:(h + 1) * LANES] for h in range(own_rows)]
        pieces.append(jnp.zeros((FIELD_ROWS - own_rows, LANES), F32))
    return jnp.concatenate(pieces, axis=0)


def send_kernel(devices, per, odd_ref, pressure_hbm, owner_hbm, element_hbm, table_hbm, support_hbm, stiffness_hbm,
                out_ref, place_ref, pressure_ref, owner_ref, element_ref, table_ref, support_ref, diagonal_ref, sems):
    del odd_ref
    moves = [(owner_hbm, owner_ref), (element_hbm, element_ref), (table_hbm, table_ref), (pressure_hbm, pressure_ref),
             (support_hbm, support_ref)]
    copies = [pltpu.make_async_copy(source, target, sems.at[i]) for i, (source, target) in enumerate(moves)]
    for copy in copies:
        copy.start()
    for i in range(DOF):
        pltpu.make_async_copy(
            stiffness_hbm.at[i, pl.ds(i, 1)], diagonal_ref.at[pl.ds(i, 1)], sems.at[len(moves)]).start()
    for copy in copies:
        copy.wait()
    pltpu.make_async_copy(stiffness_hbm.at[0], diagonal_ref, sems.at[len(moves)]).wait()
    faces = pressure_ref.shape[0]
    target = owner_ref[...]
    named = iota((devices, faces), 0) == target
    named16 = onehot(named)
    blocks = range(0, faces, WIDE)
    upto = onehot(iota((WIDE, WIDE), 0) <= iota((WIDE, WIDE), 1))
    counts = dot_nn(jnp.concatenate([named16[:, start:start + WIDE] for start in blocks], axis=0), upto)
    before = jnp.zeros((devices, 1), F32)
    ranks = []
    for i, start in enumerate(blocks):
        count = counts[i * devices:(i + 1) * devices]
        here = jnp.where(named[:, start:start + WIDE], count + before, 0.0)
        ranks.append(jnp.sum(here, axis=0, keepdims=True))
        before = before + count[:, WIDE - 1:]
    rank = jnp.concatenate(ranks, axis=1).astype(jnp.int32) - 1
    group = jnp.zeros_like(rank)
    for i in range(1, GROUPS):
        group = group + (rank >= i * per).astype(jnp.int32)
    place = target * per + rank - group * per
    place_ref[...] = jnp.concatenate([place, group, jnp.zeros((6, faces), jnp.int32)], axis=0)
    chosen = onehot(iota((devices * per, faces), 0) == place)

    pad = jnp.zeros((LANES - GROUPS * DOF, table_ref.shape[1]), F32)
    table_high, table_low = split(jnp.concatenate([table_ref[...]] * GROUPS + [pad], axis=0))
    rows_high, rows_low = split(pressure_ref[...])
    projected = dot_nt(
        jnp.concatenate([table_high, table_low, table_high], axis=1),
        jnp.concatenate([rows_high, rows_high, rows_low], axis=1),
    )
    spread = [jnp.where(group == i, projected[i * DOF:(i + 1) * DOF], 0.0) for i in range(GROUPS)]
    spread.append(jnp.where(iota((8, faces), 0) == group, element_ref[...].astype(F32), 0.0))
    spread_high, spread_low = split(jnp.concatenate(spread, axis=0))
    sent = dot_nt(chosen, jnp.concatenate([spread_high, spread_low], axis=0))

    trace = jnp.sum(diagonal_ref[...]) + jnp.sum(support_ref[...])
    out_ref[...] = jnp.where(iota((devices * per, LANES), 1) == 125, trace, sent[:, :LANES] + sent[:, LANES:])


def load_kernel(devices, per, odd_ref, rows_ref, connectivity_ref, support_ref,
                partial_ref, swap_a_ref, swap_b_ref, weight_ref, scale_ref, code_ref, loads_ref):
    nodes = support_ref.shape[1]
    own_rows = nodes // LANES

    @pl.when(odd_ref[0] >= 0)
    def _():
        rows = rows_ref[...]
        arrived = rows.T
        codes = arrived[GROUPS * DOF:].astype(jnp.int32)
        code_ref[...] = codes
        slots = rows.shape[0]
        total = jnp.zeros((4 * 2 * DOF, WIDE), F32)
        for g in range(GROUPS):
            terms = arrived[g * DOF:(g + 1) * DOF]
            upper = terms.astype(BF16).astype(F32)
            both = jnp.concatenate([upper, terms - upper], axis=0)
            code = codes[g:g + 1]
            left = jnp.concatenate([jnp.where((code >> 8) == i, both, 0.0) for i in range(4)], axis=0).astype(BF16)
            total = total + dot_nt(left, onehot(iota((WIDE, slots), 0) == (code & 255)))
        for i in range(4):
            start = i * 2 * DOF
            loads_ref[:, i * WIDE:(i + 1) * WIDE] = total[start:start + DOF] + total[start + DOF:start + 2 * DOF]

    partial = assemble(loads_ref[...], connectivity_ref[...])
    partial_ref[...] = partial
    put_ends(partial, odd_ref[0] == 1, own_rows, swap_a_ref, swap_b_ref)
    trace = jnp.sum(rows_ref[:, 125:126]) * (1.0 / per)
    inverse = jnp.full((8, LANES), 3.0 * nodes * devices, F32) / jnp.full((8, LANES), trace, F32)
    scale_ref[...] = inverse
    weight_ref[...] = as_field(support_ref[...], own_rows) * inverse[:1, :1]


def product_kernel(own_rows, odd_ref, partial_ref, swap_a_in, swap_b_in, weight_ref, scale_ref, connectivity_ref,
                   stiffness_ref, columns_ref, field_ref, values_ref, forces_ref, next_ref, swap_a_ref, swap_b_ref):
    odd = odd_ref[0] == 1

    @pl.when(odd_ref[0] >= 0)
    def _():
        field = add_ends(partial_ref[...], odd, own_rows, swap_a_in[...], swap_b_in[...])
        field_ref[...] = field
        values = gather_corners(field, connectivity_ref[...])
        values_ref[...] = jnp.concatenate(values, axis=0)
        forces_ref[...] = matvec(stiffness_ref, values)

    partial = assemble(forces_ref[...], connectivity_ref[...], columns_ref)
    partial = partial * scale_ref[:1, :1] + weight_ref[...] * field_ref[...]
    next_ref[...] = partial
    put_ends(partial, odd, own_rows, swap_a_ref, swap_b_ref)


def entries(pairs):
    lane = iota((1, LANES), 1)
    row = jnp.zeros((1, LANES), F32)
    for i, value in pairs:
        row = jnp.where(lane == i, value, row)
    return row


def share(value, norm):
    return jnp.full((1, LANES), value, F32) / jnp.maximum(jnp.full((1, LANES), norm, F32), 1e-30)


def lower_kernel(own_rows, weight_ref, scale_ref, first_ref, second_ref, values0_ref, values1_ref,
                 forces0_ref, forces1_ref, after_ref, own0_ref, own1_ref, turned_ref, numbers_ref):
    del after_ref
    own, weight = own_mask(own_rows), weight_ref[...]
    first, second = jnp.where(own, first_ref[...], 0.0), jnp.where(own, second_ref[...], 0.0)
    norm0 = jnp.sum(first * first)
    theta = share(jnp.sum(first * second), norm0)
    second = second - theta * first
    own0_ref[...], own1_ref[...] = first, second
    scale, part = scale_ref[:1, :1], theta[:, :1]
    values0, forces0 = values0_ref[...], forces0_ref[...]
    values1, forces1 = values1_ref[...] - part * values0, forces1_ref[...] - part * forces0
    turned_ref[...] = values1
    norm1 = jnp.sum(second * second)
    row = entries([
        (0, norm0),
        (1, jnp.sum(first * second)),
        (2, norm1),
        (6, jnp.sum(values0 * forces0) * scale + jnp.sum(weight * first * first)),
        (7, jnp.sum(values0 * forces1) * scale + jnp.sum(weight * first * second)),
        (8, jnp.sum(values1 * forces1) * scale + jnp.sum(weight * second * second)),
        (12, theta),
    ])
    numbers_ref[...] = jnp.concatenate(
        [row, share(1.0, norm0), share(1.0, norm1), jnp.zeros((5, LANES), F32)], axis=0)


def moment_kernel(own_rows, devices, odd_ref, partial_ref, swap_a_in, swap_b_in, weight_ref, scale_ref,
                  connectivity_ref, stiffness_ref, own0_ref, own1_ref, values0_ref, turned_ref, numbers_ref,
                  pick0_ref, pick1_ref, field_ref, values_ref, moments_ref):
    del pick0_ref, pick1_ref
    odd = odd_ref[0] == 1
    field = add_ends(partial_ref[...], odd, own_rows, swap_a_in[...], swap_b_in[...])
    field_ref[...] = field
    weight, scale = weight_ref[...], scale_ref[:1, :1]
    first, second = own0_ref[...], own1_ref[...]
    third = jnp.where(own_mask(own_rows), field, 0.0)
    phi = jnp.sum(first * third) * numbers_ref[1:2]
    psi = jnp.sum(second * third) * numbers_ref[2:3]
    third = third - psi * second - phi * first
    values0, values1 = values0_ref[...], turned_ref[...]
    values2 = jnp.concatenate(gather_corners(field, connectivity_ref[...]), axis=0)
    values_ref[...] = values2
    values2 = values2 - psi[:, :1] * values1 - phi[:, :1] * values0
    forces2 = matvec(stiffness_ref, [values2[c * CORNERS:(c + 1) * CORNERS] for c in range(3)])
    weighted = weight * third
    row = numbers_ref[:1] + entries([
        (3, jnp.sum(first * third)),
        (4, jnp.sum(second * third)),
        (5, jnp.sum(third * third)),
        (9, jnp.sum(values0 * forces2) * scale + jnp.sum(first * weighted)),
        (10, jnp.sum(values1 * forces2) * scale + jnp.sum(second * weighted)),
        (11, jnp.sum(values2 * forces2) * scale + jnp.sum(third * weighted)),
        (13, psi),
        (14, phi),
    ])
    moments_ref[...] = jnp.broadcast_to(row, (devices, LANES))


def step_weights(rows):
    column = [rows[:, i:i + 1] for i in range(15)]
    norms, energies, (theta, psi, phi) = column[:6], column[6:12], column[12:]

    def square(matrix, y):
        total = y[0] * y[0] * matrix[0]
        if len(y) > 1:
            total = total + y[1] * (2.0 * y[0] * matrix[1] + y[1] * matrix[2])
        if len(y) > 2:
            total = total + y[2] * (2.0 * (y[0] * matrix[3] + y[1] * matrix[4]) + y[2] * matrix[5])
        return jnp.sum(total, axis=0, keepdims=True)

    norm0 = jnp.sum(norms[0], axis=0, keepdims=True)
    step0 = norm0 / jnp.sum(energies[0], axis=0, keepdims=True)
    residual = [1.0 - step0 * theta, -step0]
    norm1 = square(norms, residual)
    turn0 = norm1 / norm0
    direction = [residual[0] + turn0, -step0]
    step1 = norm1 / square(energies, direction)
    lead = 1.0 + turn0
    residual = [
        residual[0] - step1 * (lead * theta - step0 * phi),
        -step0 - step1 * (lead - step0 * psi),
        step1 * step0,
    ]
    norm2 = square(norms, residual)
    turn1 = norm2 / norm1
    direction = [residual[0] + turn1 * direction[0], residual[1] - turn1 * step0, residual[2]]
    step2 = norm2 / square(energies, direction)
    return [
        step0 + step1 * lead + step2 * (1.0 + turn1 * lead),
        -step1 * step0 - step2 * (step0 + step1 * lead + turn1 * step0),
        step2 * step1 * step0,
    ]


def pick(values, code_ref, out_ref, blend):
    for start in range(0, code_ref.shape[1], LANES):
        sections = []
        for g in range(GROUPS):
            code = jnp.broadcast_to(code_ref[g:g + 1, start:start + LANES], (CORNERS, LANES))
            low, high = code & 127, code >> 7
            masks = [high == i for i in range(8)]
            for c in range(3):
                total = jnp.zeros((CORNERS, LANES), F32)
                for i in range(8):
                    tile = values[c * CORNERS:(c + 1) * CORNERS, i * LANES:(i + 1) * LANES]
                    total = jnp.where(masks[i], take_lanes(tile, low), total)
                sections.append(total)
        sections.append(jnp.zeros((CORNERS, LANES), F32))
        rows = pl.ds(start, LANES)
        out_ref[rows, :] = blend(jnp.concatenate(sections, axis=0).T, rows)


def pick_kernel(values_ref, code_ref, after_ref, out_ref):
    del after_ref
    pick(values_ref[...], code_ref, out_ref, lambda tile, rows: tile)


def blend_kernel(moments_ref, scale_ref, code_ref, pick0_ref, pick1_ref, values_ref, weights_ref, out_ref):
    weights = step_weights(moments_ref[...])
    weights = [weight * scale_ref[:1, :1] for weight in weights]
    weights_ref[...] = jnp.concatenate([jnp.broadcast_to(weight, (8, LANES)) for weight in weights], axis=0)

    def blend(tile, rows):
        return weights[0] * pick0_ref[rows, :] + weights[1] * pick1_ref[rows, :] + weights[2] * tile

    pick(values_ref[...], code_ref, out_ref, blend)


def motion_kernel(own_rows, rows_ref, place_ref, table_ref, weights_ref, first_ref, second_ref, third_ref,
                  displacement_hbm, out_hbm, displacement_ref, out_ref, sems):
    field = weights_ref[:1] * first_ref[...] + weights_ref[8:9] * second_ref[...] + weights_ref[16:17] * third_ref[...]
    for c in range(3):
        for h in range(own_rows):
            displacement_ref[c:c + 1, h * LANES:(h + 1) * LANES] = field[c * FIELD_ROWS + h:c * FIELD_ROWS + h + 1]
    copies = [pltpu.make_async_copy(displacement_ref, displacement_hbm, sems.at[0])]
    copies[0].start()
    high, low = split(rows_ref[...].T)
    slots, faces = rows_ref.shape[0], place_ref.shape[1]
    place, group = place_ref[0:1], place_ref[1:2]
    found = dot_nn(jnp.concatenate([high, low], axis=0), onehot(iota((slots, faces), 0) == place))
    found = found[:LANES] + found[LANES:]
    owned = jnp.zeros((DOF, faces), F32)
    for g in range(GROUPS):
        owned = jnp.where(group == g, found[g * DOF:(g + 1) * DOF], owned)
    upper = owned.astype(BF16).astype(F32)
    lower = owned - upper
    parts = jnp.concatenate([upper, lower, upper], axis=0).T.astype(BF16)
    table_high, table_low = split(table_ref[...])
    right = jnp.concatenate([table_high, table_high, table_low], axis=0)
    for i, start in enumerate(range(0, faces, WIDE)):
        out_ref[start:start + WIDE, :] = dot_nn(parts[start:start + WIDE], right)
        copy = pltpu.make_async_copy(
            out_ref.at[pl.ds(start, WIDE)], out_hbm.at[pl.ds(start, WIDE)], sems.at[1 + i])
        copy.start()
        copies.append(copy)
    for copy in copies:
        copy.wait()


def call(kernel, outs, args, scalars=0, hbm=(), outs_hbm=(), scratch=(), time=1.0):
    in_specs = []
    for i in range(len(args)):
        if i < scalars:
            in_specs.append(pl.BlockSpec(memory_space=pltpu.SMEM))
        elif i in hbm:
            in_specs.append(pl.BlockSpec(memory_space=pltpu.HBM))
        else:
            in_specs.append(pl.BlockSpec(memory_space=pltpu.VMEM))
    return pl.pallas_call(
        kernel,
        name=getattr(kernel, "func", kernel).__name__,
        out_shape=[jax.ShapeDtypeStruct(shape, dtype) for shape, dtype in outs],
        in_specs=in_specs,
        out_specs=[
            pl.BlockSpec(memory_space=pltpu.HBM if i in outs_hbm else pltpu.VMEM) for i in range(len(outs))
        ],
        scratch_shapes=list(scratch),
        cost_estimate=pl.CostEstimate(flops=int(time * 1e9), transcendentals=0, bytes_accessed=int(time * 1e6)),
        compiler_params=pltpu.CompilerParams(vmem_limit_bytes=VMEM_BYTES),
    )(*[pltpu.with_memory_space_constraint(arg, pltpu.HBM) if i in hbm else arg for i, arg in enumerate(args)])


def shards(pressure, face_owner, face_element, shape_table, stiffness, connectivity, support):
    devices = lax.axis_size(AXES)
    faces = pressure.shape[0]
    elements = stiffness.shape[2]
    nodes = support.shape[1]
    own_rows = nodes // LANES
    capacity = max(2, (5 * faces + 2 * devices - 1) // (2 * devices))
    per = (capacity + GROUPS - 1) // GROUPS
    slots = devices * per
    odd = (lax.axis_index(AXES) % 2).astype(jnp.int32).reshape(1)
    evens = [(i, i + 1) for i in range(0, devices - 1, 2)]
    odds = [(i, i + 1) for i in range(1, devices - 1, 2)]
    pairs_a = evens + [(j, i) for i, j in evens]
    pairs_b = odds + [(j, i) for i, j in odds]

    def swap(a, b):
        return lax.ppermute(a, AXES, pairs_a), lax.ppermute(b, AXES, pairs_b)

    def everywhere(rows):
        return lax.all_to_all(rows, AXES, split_axis=0, concat_axis=0, tiled=True)

    field = ((3 * FIELD_ROWS, LANES), F32)
    values = ((DOF, elements), F32)
    ends = ((8, LANES), F32)
    block = ((slots, LANES), F32)
    sent, place = call(
        functools.partial(send_kernel, devices, per),
        [block, ((8, faces), jnp.int32)],
        (odd, pressure, face_owner.reshape(1, faces), face_element.reshape(1, faces), shape_table, support, stiffness),
        scalars=1,
        hbm=range(1, 7),
        scratch=(
            pltpu.VMEM(pressure.shape, F32),
            pltpu.VMEM((1, faces), jnp.int32),
            pltpu.VMEM((1, faces), jnp.int32),
            pltpu.VMEM(shape_table.shape, F32),
            pltpu.VMEM(support.shape, F32),
            pltpu.VMEM((DOF, elements), F32),
            pltpu.SemaphoreType.DMA((6,)),
        ),
    )
    arrived = everywhere(sent)
    partial, end_a, end_b, weight, scale, codes = call(
        functools.partial(load_kernel, devices, per),
        [field, ends, ends, field, ends, ((8, slots), jnp.int32)],
        (odd, arrived, connectivity, support),
        scalars=1,
        scratch=(pltpu.VMEM((DOF, elements), F32),),
    )
    stage = (
        functools.partial(product_kernel, own_rows),
        [field, values, values, field, ends, ends],
    )
    end_a, end_b = swap(end_a, end_b)
    (columns,) = call(
        columns_kernel, [((CORNERS, elements, LANES), BF16)], (connectivity, end_a), time=0.1)
    first, values0, forces0, partial, end_a, end_b = call(
        *stage, (odd, partial, end_a, end_b, weight, scale, connectivity, stiffness, columns), scalars=1)
    end_a, end_b = swap(end_a, end_b)
    (pick0,) = call(pick_kernel, [block], (values0, codes, end_a), time=0.1)
    second, values1, forces1, partial, end_a, end_b = call(
        *stage, (odd, partial, end_a, end_b, weight, scale, connectivity, stiffness, columns), scalars=1)
    end_a, end_b = swap(end_a, end_b)
    (pick1,) = call(pick_kernel, [block], (values1, codes, end_a), time=0.1)
    own0, own1, turned, numbers = call(
        functools.partial(lower_kernel, own_rows),
        [field, field, values, ends],
        (weight, scale, first, second, values0, values1, forces0, forces1, end_a),
        time=0.1,
    )
    third, values2, moments = call(
        functools.partial(moment_kernel, own_rows, devices),
        [field, values, ((devices, LANES), F32)],
        (odd, partial, end_a, end_b, weight, scale, connectivity, stiffness, own0, own1, values0, turned, numbers,
         pick0, pick1),
        scalars=1,
    )
    moments = everywhere(moments)
    weights, leaving = call(
        blend_kernel,
        [((24, LANES), F32), block],
        (moments, scale, codes, pick0, pick1, values2),
    )
    returned = everywhere(leaving)
    return call(
        functools.partial(motion_kernel, own_rows),
        [((3, nodes), F32), ((faces, LANES), F32)],
        (returned, place, shape_table, weights, first, second, third),
        outs_hbm=(0, 1),
        scratch=(
            pltpu.VMEM((3, nodes), F32),
            pltpu.VMEM((faces, LANES), F32),
            pltpu.SemaphoreType.DMA((1 + faces // WIDE,)),
        ),
    )


def solution(mesh):
    in_specs = (
        P(AXES, None),
        P(AXES, None),
        P(AXES),
        P(),
        P(None, None, AXES),
        P(None, AXES),
        P(None, AXES),
    )
    out_specs = (P(None, AXES), P(AXES, None))
    return jax.shard_map(shards, mesh=mesh, in_specs=in_specs, out_specs=out_specs, check_vma=False)
```

```python
import functools

import jax
import jax.numpy as jnp
from jax import lax
from jax.experimental import pallas as pl
from jax.experimental.pallas import tpu as pltpu
from jax.sharding import PartitionSpec as P

AXES = ("fluid", "solid")
DOF = 24
CORNERS = 8
GROUPS = 5
FIELD_ROWS = 16
LANES = 128
WIDE = 256
VMEM_BYTES = 24 * 1024 * 1024
F32 = jnp.float32
BF16 = jnp.bfloat16


def iota(shape, axis):
    return lax.broadcasted_iota(jnp.int32, shape, axis)


def onehot(mask):
    return jnp.where(mask, 1.0, 0.0).astype(BF16)


def split(value):
    high = value.astype(BF16)
    return high, (value - high.astype(F32)).astype(BF16)


def dot_nt(left, right):
    return lax.dot_general(left, right, (((1,), (1,)), ((), ())), preferred_element_type=F32)


def dot_nn(left, right):
    return lax.dot_general(left, right, (((1,), (0,)), ((), ())), preferred_element_type=F32)


def take_lanes(table, index):
    return jnp.take_along_axis(table, index, axis=1, mode="promise_in_bounds")


def gather_corners(field, connectivity, blocks, known=None):
    elements = connectivity.shape[1]
    rows = {}
    for c in range(3):
        for h in blocks:
            rows[c, h] = jnp.broadcast_to(field[c * FIELD_ROWS + h:c * FIELD_ROWS + h + 1], (CORNERS, LANES))
    parts = [[], [], []]
    for start in range(0, elements, LANES):
        index = connectivity[:, start:start + LANES]
        low, high = index & 127, index >> 7
        masks = {h: high == h for h in blocks}
        for c in range(3):
            if known is None:
                total = jnp.zeros((CORNERS, LANES), F32)
            else:
                total = known[c * CORNERS:(c + 1) * CORNERS, start:start + LANES]
            for h in blocks:
                total = jnp.where(masks[h], take_lanes(rows[c, h], low), total)
            parts[c].append(total)
    return [jnp.concatenate(part, axis=1) for part in parts]


def assemble(terms, connectivity, columns_ref=None):
    elements = connectivity.shape[1]
    high, low = connectivity >> 7, connectivity & 127
    upper = terms.astype(BF16).astype(F32)
    lower = terms - upper
    total = jnp.zeros((6 * FIELD_ROWS, LANES), F32)
    for k in range(CORNERS):
        mask = iota((FIELD_ROWS, elements), 0) == high[k:k + 1]
        pieces = [
            jnp.where(mask, part[c * CORNERS + k:c * CORNERS + k + 1], 0.0)
            for part in (upper, lower)
            for c in range(3)
        ]
        left = jnp.concatenate(pieces, axis=0).astype(BF16)
        if columns_ref is None:
            total = total + dot_nt(left, onehot(iota((LANES, elements), 0) == low[k:k + 1]))
        else:
            total = total + dot_nn(left, columns_ref[k])
    return total[:3 * FIELD_ROWS] + total[3 * FIELD_ROWS:]


def columns_kernel(connectivity_ref, after_ref, out_ref):
    del after_ref
    low = connectivity_ref[...] & 127
    for k in range(CORNERS):
        out_ref[k] = jnp.where(iota((LANES, low.shape[1]), 0) == low[k:k + 1], 1.0, 0.0).T.astype(BF16)


def matvec(stiffness, values):
    elements = stiffness.shape[2]
    parts = []
    for start in range(0, elements, 128):
        total = jnp.zeros((DOF, 128), F32)
        for b in range(DOF):
            total = total + stiffness[b, :, start:start + 128] * values[b // 8][b % 8:b % 8 + 1, start:start + 128]
        parts.append(total)
    return jnp.concatenate(parts, axis=1)


def put_ends(partial, odd, own_rows, swap_a_ref, swap_b_ref):
    pad = [jnp.zeros((5, LANES), F32)]
    first = jnp.concatenate([partial[c * FIELD_ROWS:c * FIELD_ROWS + 1] for c in range(3)] + pad, axis=0)
    over = jnp.concatenate(
        [partial[c * FIELD_ROWS + own_rows:c * FIELD_ROWS + own_rows + 1] for c in range(3)] + pad, axis=0)
    swap_a_ref[...] = jnp.where(odd, first, over)
    swap_b_ref[...] = jnp.where(odd, over, first)


def add_ends(partial, odd, own_rows, swap_a, swap_b):
    before = jnp.where(odd, swap_a, swap_b)
    after = jnp.where(odd, swap_b, swap_a)
    pieces = []
    for c in range(3):
        pieces += [
            before[c:c + 1],
            jnp.zeros((own_rows - 1, LANES), F32),
            after[c:c + 1],
            jnp.zeros((FIELD_ROWS - own_rows - 1, LANES), F32),
        ]
    return partial + jnp.concatenate(pieces, axis=0)


def own_mask(own_rows):
    return (iota((3 * FIELD_ROWS, LANES), 0) % FIELD_ROWS) < own_rows


def as_field(rows, own_rows):
    pieces = []
    for c in range(3):
        pieces += [rows[c:c + 1, h * LANES:(h + 1) * LANES] for h in range(own_rows)]
        pieces.append(jnp.zeros((FIELD_ROWS - own_rows, LANES), F32))
    return jnp.concatenate(pieces, axis=0)


def send_kernel(devices, per, odd_ref, pressure_hbm, owner_hbm, element_hbm, table_hbm, support_hbm, stiffness_hbm,
                out_ref, place_ref, pressure_ref, owner_ref, element_ref, table_ref, support_ref, diagonal_ref, sems):
    del odd_ref
    moves = [(owner_hbm, owner_ref), (element_hbm, element_ref), (table_hbm, table_ref), (pressure_hbm, pressure_ref),
             (support_hbm, support_ref)]
    copies = [pltpu.make_async_copy(source, target, sems.at[i]) for i, (source, target) in enumerate(moves)]
    for copy in copies:
        copy.start()
    for i in range(DOF):
        pltpu.make_async_copy(
            stiffness_hbm.at[i, pl.ds(i, 1)], diagonal_ref.at[pl.ds(i, 1)], sems.at[len(moves)]).start()
    for copy in copies:
        copy.wait()
    pltpu.make_async_copy(stiffness_hbm.at[0], diagonal_ref, sems.at[len(moves)]).wait()
    faces = pressure_ref.shape[0]
    target = owner_ref[...]
    named = iota((devices, faces), 0) == target
    named16 = onehot(named)
    blocks = range(0, faces, WIDE)
    upto = onehot(iota((WIDE, WIDE), 0) <= iota((WIDE, WIDE), 1))
    counts = dot_nn(jnp.concatenate([named16[:, start:start + WIDE] for start in blocks], axis=0), upto)
    before = jnp.zeros((devices, 1), F32)
    ranks = []
    for i, start in enumerate(blocks):
        count = counts[i * devices:(i + 1) * devices]
        here = jnp.where(named[:, start:start + WIDE], count + before, 0.0)
        ranks.append(jnp.sum(here, axis=0, keepdims=True))
        before = before + count[:, WIDE - 1:]
    rank = jnp.concatenate(ranks, axis=1).astype(jnp.int32) - 1
    group = jnp.zeros_like(rank)
    for i in range(1, GROUPS):
        group = group + (rank >= i * per).astype(jnp.int32)
    place = target * per + rank - group * per
    place_ref[...] = jnp.concatenate([place, group, jnp.zeros((6, faces), jnp.int32)], axis=0)
    chosen = onehot(iota((devices * per, faces), 0) == place)

    pad = jnp.zeros((LANES - GROUPS * DOF, table_ref.shape[1]), F32)
    table_high, table_low = split(jnp.concatenate([table_ref[...]] * GROUPS + [pad], axis=0))
    rows_high, rows_low = split(pressure_ref[...])
    projected = dot_nt(
        jnp.concatenate([table_high, table_low, table_high], axis=1),
        jnp.concatenate([rows_high, rows_high, rows_low], axis=1),
    )
    spread = [jnp.where(group == i, projected[i * DOF:(i + 1) * DOF], 0.0) for i in range(GROUPS)]
    spread.append(jnp.where(iota((8, faces), 0) == group, element_ref[...].astype(F32), 0.0))
    spread_high, spread_low = split(jnp.concatenate(spread, axis=0))
    sent = dot_nt(chosen, jnp.concatenate([spread_high, spread_low], axis=0))

    trace = jnp.sum(diagonal_ref[...]) + jnp.sum(support_ref[...])
    out_ref[...] = jnp.where(iota((devices * per, LANES), 1) == 125, trace, sent[:, :LANES] + sent[:, LANES:])


def load_kernel(devices, per, odd_ref, rows_ref, connectivity_ref, support_ref,
                partial_ref, swap_a_ref, swap_b_ref, weight_ref, scale_ref, code_ref, loads_ref):
    nodes = support_ref.shape[1]
    own_rows = nodes // LANES

    @pl.when(odd_ref[0] >= 0)
    def _():
        rows = rows_ref[...]
        arrived = rows.T
        codes = arrived[GROUPS * DOF:].astype(jnp.int32)
        code_ref[...] = codes
        slots = rows.shape[0]
        total = jnp.zeros((4 * 2 * DOF, WIDE), F32)
        for g in range(GROUPS):
            terms = arrived[g * DOF:(g + 1) * DOF]
            upper = terms.astype(BF16).astype(F32)
            both = jnp.concatenate([upper, terms - upper], axis=0)
            code = codes[g:g + 1]
            left = jnp.concatenate([jnp.where((code >> 8) == i, both, 0.0) for i in range(4)], axis=0).astype(BF16)
            total = total + dot_nt(left, onehot(iota((WIDE, slots), 0) == (code & 255)))
        for i in range(4):
            start = i * 2 * DOF
            loads_ref[:, i * WIDE:(i + 1) * WIDE] = total[start:start + DOF] + total[start + DOF:start + 2 * DOF]

    partial = assemble(loads_ref[...], connectivity_ref[...])
    partial_ref[...] = partial
    put_ends(partial, odd_ref[0] == 1, own_rows, swap_a_ref, swap_b_ref)
    trace = jnp.sum(rows_ref[:, 125:126]) * (1.0 / per)
    inverse = jnp.full((8, LANES), 3.0 * nodes * devices, F32) / jnp.full((8, LANES), trace, F32)
    scale_ref[...] = inverse
    weight_ref[...] = as_field(support_ref[...], own_rows) * inverse[:1, :1]


def inner_kernel(own_rows, partial_ref, connectivity_ref, after_ref, out_ref):
    del after_ref
    out_ref[...] = jnp.concatenate(
        gather_corners(partial_ref[...], connectivity_ref[...], range(1, own_rows)), axis=0)


def product_kernel(own_rows, odd_ref, partial_ref, swap_a_in, swap_b_in, weight_ref, scale_ref, connectivity_ref,
                   stiffness_ref, columns_ref, inner_ref, field_ref, values_ref, forces_ref, next_ref, swap_a_ref, swap_b_ref):
    odd = odd_ref[0] == 1

    @pl.when(odd_ref[0] >= 0)
    def _():
        field = add_ends(partial_ref[...], odd, own_rows, swap_a_in[...], swap_b_in[...])
        field_ref[...] = field
        values = gather_corners(field, connectivity_ref[...], (0, own_rows), inner_ref)
        values_ref[...] = jnp.concatenate(values, axis=0)
        forces_ref[...] = matvec(stiffness_ref, values)

    partial = assemble(forces_ref[...], connectivity_ref[...], columns_ref)
    partial = partial * scale_ref[:1, :1] + weight_ref[...] * field_ref[...]
    next_ref[...] = partial
    put_ends(partial, odd, own_rows, swap_a_ref, swap_b_ref)


def entries(pairs):
    lane = iota((1, LANES), 1)
    row = jnp.zeros((1, LANES), F32)
    for i, value in pairs:
        row = jnp.where(lane == i, value, row)
    return row


def share(value, norm):
    return jnp.full((1, LANES), value, F32) / jnp.maximum(jnp.full((1, LANES), norm, F32), 1e-30)


def lower_kernel(own_rows, weight_ref, scale_ref, first_ref, second_ref, values0_ref, values1_ref,
                 forces0_ref, forces1_ref, after_ref, own0_ref, own1_ref, turned_ref, numbers_ref):
    del after_ref
    own, weight = own_mask(own_rows), weight_ref[...]
    first, second = jnp.where(own, first_ref[...], 0.0), jnp.where(own, second_ref[...], 0.0)
    norm0 = jnp.sum(first * first)
    theta = share(jnp.sum(first * second), norm0)
    second = second - theta * first
    own0_ref[...], own1_ref[...] = first, second
    scale, part = scale_ref[:1, :1], theta[:, :1]
    values0, forces0 = values0_ref[...], forces0_ref[...]
    values1, forces1 = values1_ref[...] - part * values0, forces1_ref[...] - part * forces0
    turned_ref[...] = values1
    norm1 = jnp.sum(second * second)
    row = entries([
        (0, norm0),
        (1, jnp.sum(first * second)),
        (2, norm1),
        (6, jnp.sum(values0 * forces0) * scale + jnp.sum(weight * first * first)),
        (7, jnp.sum(values0 * forces1) * scale + jnp.sum(weight * first * second)),
        (8, jnp.sum(values1 * forces1) * scale + jnp.sum(weight * second * second)),
        (12, theta),
    ])
    numbers_ref[...] = jnp.concatenate(
        [row, share(1.0, norm0), share(1.0, norm1), jnp.zeros((5, LANES), F32)], axis=0)


def moment_kernel(own_rows, devices, odd_ref, partial_ref, swap_a_in, swap_b_in, weight_ref, scale_ref,
                  connectivity_ref, stiffness_ref, own0_ref, own1_ref, values0_ref, turned_ref, numbers_ref, inner_ref,
                  pick0_ref, pick1_ref, field_ref, values_ref, moments_ref):
    del pick0_ref, pick1_ref
    odd = odd_ref[0] == 1
    field = add_ends(partial_ref[...], odd, own_rows, swap_a_in[...], swap_b_in[...])
    field_ref[...] = field
    weight, scale = weight_ref[...], scale_ref[:1, :1]
    first, second = own0_ref[...], own1_ref[...]
    third = jnp.where(own_mask(own_rows), field, 0.0)
    phi = jnp.sum(first * third) * numbers_ref[1:2]
    psi = jnp.sum(second * third) * numbers_ref[2:3]
    third = third - psi * second - phi * first
    values0, values1 = values0_ref[...], turned_ref[...]
    values2 = jnp.concatenate(gather_corners(field, connectivity_ref[...], (0, own_rows), inner_ref), axis=0)
    values_ref[...] = values2
    values2 = values2 - psi[:, :1] * values1 - phi[:, :1] * values0
    forces2 = matvec(stiffness_ref, [values2[c * CORNERS:(c + 1) * CORNERS] for c in range(3)])
    weighted = weight * third
    row = numbers_ref[:1] + entries([
        (3, jnp.sum(first * third)),
        (4, jnp.sum(second * third)),
        (5, jnp.sum(third * third)),
        (9, jnp.sum(values0 * forces2) * scale + jnp.sum(first * weighted)),
        (10, jnp.sum(values1 * forces2) * scale + jnp.sum(second * weighted)),
        (11, jnp.sum(values2 * forces2) * scale + jnp.sum(third * weighted)),
        (13, psi),
        (14, phi),
    ])
    moments_ref[...] = jnp.broadcast_to(row, (devices, LANES))


def step_weights(rows):
    column = [rows[:, i:i + 1] for i in range(15)]
    norms, energies, (theta, psi, phi) = column[:6], column[6:12], column[12:]

    def square(matrix, y):
        total = y[0] * y[0] * matrix[0]
        if len(y) > 1:
            total = total + y[1] * (2.0 * y[0] * matrix[1] + y[1] * matrix[2])
        if len(y) > 2:
            total = total + y[2] * (2.0 * (y[0] * matrix[3] + y[1] * matrix[4]) + y[2] * matrix[5])
        return jnp.sum(total, axis=0, keepdims=True)

    norm0 = jnp.sum(norms[0], axis=0, keepdims=True)
    step0 = norm0 / jnp.sum(energies[0], axis=0, keepdims=True)
    residual = [1.0 - step0 * theta, -step0]
    norm1 = square(norms, residual)
    turn0 = norm1 / norm0
    direction = [residual[0] + turn0, -step0]
    step1 = norm1 / square(energies, direction)
    lead = 1.0 + turn0
    residual = [
        residual[0] - step1 * (lead * theta - step0 * phi),
        -step0 - step1 * (lead - step0 * psi),
        step1 * step0,
    ]
    norm2 = square(norms, residual)
    turn1 = norm2 / norm1
    direction = [residual[0] + turn1 * direction[0], residual[1] - turn1 * step0, residual[2]]
    step2 = norm2 / square(energies, direction)
    return [
        step0 + step1 * lead + step2 * (1.0 + turn1 * lead),
        -step1 * step0 - step2 * (step0 + step1 * lead + turn1 * step0),
        step2 * step1 * step0,
    ]


def pick(values, code_ref, out_ref, blend):
    for start in range(0, code_ref.shape[1], LANES):
        sections = []
        for g in range(GROUPS):
            code = jnp.broadcast_to(code_ref[g:g + 1, start:start + LANES], (CORNERS, LANES))
            low, high = code & 127, code >> 7
            masks = [high == i for i in range(8)]
            for c in range(3):
                total = jnp.zeros((CORNERS, LANES), F32)
                for i in range(8):
                    tile = values[c * CORNERS:(c + 1) * CORNERS, i * LANES:(i + 1) * LANES]
                    total = jnp.where(masks[i], take_lanes(tile, low), total)
                sections.append(total)
        sections.append(jnp.zeros((CORNERS, LANES), F32))
        rows = pl.ds(start, LANES)
        out_ref[rows, :] = blend(jnp.concatenate(sections, axis=0).T, rows)


def pick_kernel(values_ref, code_ref, after_ref, out_ref):
    del after_ref
    pick(values_ref[...], code_ref, out_ref, lambda tile, rows: tile)


def blend_kernel(moments_ref, scale_ref, code_ref, pick0_ref, pick1_ref, values_ref, weights_ref, out_ref):
    weights = step_weights(moments_ref[...])
    weights = [weight * scale_ref[:1, :1] for weight in weights]
    weights_ref[...] = jnp.concatenate([jnp.broadcast_to(weight, (8, LANES)) for weight in weights], axis=0)

    def blend(tile, rows):
        return weights[0] * pick0_ref[rows, :] + weights[1] * pick1_ref[rows, :] + weights[2] * tile

    pick(values_ref[...], code_ref, out_ref, blend)


def motion_kernel(own_rows, rows_ref, place_ref, table_ref, weights_ref, first_ref, second_ref, third_ref,
                  displacement_hbm, out_hbm, displacement_ref, out_ref, sems):
    field = weights_ref[:1] * first_ref[...] + weights_ref[8:9] * second_ref[...] + weights_ref[16:17] * third_ref[...]
    for c in range(3):
        for h in range(own_rows):
            displacement_ref[c:c + 1, h * LANES:(h + 1) * LANES] = field[c * FIELD_ROWS + h:c * FIELD_ROWS + h + 1]
    copies = [pltpu.make_async_copy(displacement_ref, displacement_hbm, sems.at[0])]
    copies[0].start()
    high, low = split(rows_ref[...].T)
    slots, faces = rows_ref.shape[0], place_ref.shape[1]
    place, group = place_ref[0:1], place_ref[1:2]
    found = dot_nn(jnp.concatenate([high, low], axis=0), onehot(iota((slots, faces), 0) == place))
    found = found[:LANES] + found[LANES:]
    owned = jnp.zeros((DOF, faces), F32)
    for g in range(GROUPS):
        owned = jnp.where(group == g, found[g * DOF:(g + 1) * DOF], owned)
    upper = owned.astype(BF16).astype(F32)
    lower = owned - upper
    parts = jnp.concatenate([upper, lower, upper], axis=0).T.astype(BF16)
    table_high, table_low = split(table_ref[...])
    right = jnp.concatenate([table_high, table_high, table_low], axis=0)
    for i, start in enumerate(range(0, faces, WIDE)):
        out_ref[start:start + WIDE, :] = dot_nn(parts[start:start + WIDE], right)
        copy = pltpu.make_async_copy(
            out_ref.at[pl.ds(start, WIDE)], out_hbm.at[pl.ds(start, WIDE)], sems.at[1 + i])
        copy.start()
        copies.append(copy)
    for copy in copies:
        copy.wait()


def call(kernel, outs, args, scalars=0, hbm=(), outs_hbm=(), scratch=(), time=1.0):
    in_specs = []
    for i in range(len(args)):
        if i < scalars:
            in_specs.append(pl.BlockSpec(memory_space=pltpu.SMEM))
        elif i in hbm:
            in_specs.append(pl.BlockSpec(memory_space=pltpu.HBM))
        else:
            in_specs.append(pl.BlockSpec(memory_space=pltpu.VMEM))
    return pl.pallas_call(
        kernel,
        name=getattr(kernel, "func", kernel).__name__,
        out_shape=[jax.ShapeDtypeStruct(shape, dtype) for shape, dtype in outs],
        in_specs=in_specs,
        out_specs=[
            pl.BlockSpec(memory_space=pltpu.HBM if i in outs_hbm else pltpu.VMEM) for i in range(len(outs))
        ],
        scratch_shapes=list(scratch),
        cost_estimate=pl.CostEstimate(flops=int(time * 1e9), transcendentals=0, bytes_accessed=int(time * 1e6)),
        compiler_params=pltpu.CompilerParams(vmem_limit_bytes=VMEM_BYTES),
    )(*[pltpu.with_memory_space_constraint(arg, pltpu.HBM) if i in hbm else arg for i, arg in enumerate(args)])


def shards(pressure, face_owner, face_element, shape_table, stiffness, connectivity, support):
    devices = lax.axis_size(AXES)
    faces = pressure.shape[0]
    elements = stiffness.shape[2]
    nodes = support.shape[1]
    own_rows = nodes // LANES
    capacity = max(2, (5 * faces + 2 * devices - 1) // (2 * devices))
    per = (capacity + GROUPS - 1) // GROUPS
    slots = devices * per
    odd = (lax.axis_index(AXES) % 2).astype(jnp.int32).reshape(1)
    evens = [(i, i + 1) for i in range(0, devices - 1, 2)]
    odds = [(i, i + 1) for i in range(1, devices - 1, 2)]
    pairs_a = evens + [(j, i) for i, j in evens]
    pairs_b = odds + [(j, i) for i, j in odds]

    def swap(a, b):
        return lax.ppermute(a, AXES, pairs_a), lax.ppermute(b, AXES, pairs_b)

    def everywhere(rows):
        return lax.all_to_all(rows, AXES, split_axis=0, concat_axis=0, tiled=True)

    field = ((3 * FIELD_ROWS, LANES), F32)
    values = ((DOF, elements), F32)
    ends = ((8, LANES), F32)
    block = ((slots, LANES), F32)
    sent, place = call(
        functools.partial(send_kernel, devices, per),
        [block, ((8, faces), jnp.int32)],
        (odd, pressure, face_owner.reshape(1, faces), face_element.reshape(1, faces), shape_table, support, stiffness),
        scalars=1,
        hbm=range(1, 7),
        scratch=(
            pltpu.VMEM(pressure.shape, F32),
            pltpu.VMEM((1, faces), jnp.int32),
            pltpu.VMEM((1, faces), jnp.int32),
            pltpu.VMEM(shape_table.shape, F32),
            pltpu.VMEM(support.shape, F32),
            pltpu.VMEM((DOF, elements), F32),
            pltpu.SemaphoreType.DMA((6,)),
        ),
    )
    arrived = everywhere(sent)
    partial, end_a, end_b, weight, scale, codes = call(
        functools.partial(load_kernel, devices, per),
        [field, ends, ends, field, ends, ((8, slots), jnp.int32)],
        (odd, arrived, connectivity, support),
        scalars=1,
        scratch=(pltpu.VMEM((DOF, elements), F32),),
    )
    stage = (
        functools.partial(product_kernel, own_rows),
        [field, values, values, field, ends, ends],
    )
    end_a, end_b = swap(end_a, end_b)
    (inner,) = call(
        functools.partial(inner_kernel, own_rows), [values], (partial, connectivity, end_a), time=0.1)
    (columns,) = call(
        columns_kernel, [((CORNERS, elements, LANES), BF16)], (connectivity, end_a), time=0.1)
    first, values0, forces0, partial, end_a, end_b = call(
        *stage, (odd, partial, end_a, end_b, weight, scale, connectivity, stiffness, columns, inner), scalars=1)
    end_a, end_b = swap(end_a, end_b)
    (inner,) = call(
        functools.partial(inner_kernel, own_rows), [values], (partial, connectivity, end_a), time=0.1)
    (pick0,) = call(pick_kernel, [block], (values0, codes, end_a), time=0.1)
    second, values1, forces1, partial, end_a, end_b = call(
        *stage, (odd, partial, end_a, end_b, weight, scale, connectivity, stiffness, columns, inner), scalars=1)
    end_a, end_b = swap(end_a, end_b)
    (inner,) = call(
        functools.partial(inner_kernel, own_rows), [values], (partial, connectivity, end_a), time=0.1)
    (pick1,) = call(pick_kernel, [block], (values1, codes, end_a), time=0.1)
    own0, own1, turned, numbers = call(
        functools.partial(lower_kernel, own_rows),
        [field, field, values, ends],
        (weight, scale, first, second, values0, values1, forces0, forces1, end_a),
        time=0.1,
    )
    third, values2, moments = call(
        functools.partial(moment_kernel, own_rows, devices),
        [field, values, ((devices, LANES), F32)],
        (odd, partial, end_a, end_b, weight, scale, connectivity, stiffness, own0, own1, values0, turned, numbers, inner,
         pick0, pick1),
        scalars=1,
    )
    moments = everywhere(moments)
    weights, leaving = call(
        blend_kernel,
        [((24, LANES), F32), block],
        (moments, scale, codes, pick0, pick1, values2),
    )
    returned = everywhere(leaving)
    return call(
        functools.partial(motion_kernel, own_rows),
        [((3, nodes), F32), ((faces, LANES), F32)],
        (returned, place, shape_table, weights, first, second, third),
        outs_hbm=(0, 1),
        scratch=(
            pltpu.VMEM((3, nodes), F32),
            pltpu.VMEM((faces, LANES), F32),
            pltpu.SemaphoreType.DMA((1 + faces // WIDE,)),
        ),
    )


def solution(mesh):
    in_specs = (
        P(AXES, None),
        P(AXES, None),
        P(AXES),
        P(),
        P(None, None, AXES),
        P(None, AXES),
        P(None, AXES),
    )
    out_specs = (P(None, AXES), P(AXES, None))
    return jax.shard_map(shards, mesh=mesh, in_specs=in_specs, out_specs=out_specs, check_vma=False)
```

```python
import functools

import jax
import jax.numpy as jnp
from jax import lax
from jax.experimental import pallas as pl
from jax.experimental.pallas import tpu as pltpu
from jax.sharding import PartitionSpec as P

AXES = ("fluid", "solid")
DOF = 24
CORNERS = 8
GROUPS = 5
FIELD_ROWS = 16
LANES = 128
WIDE = 256
SPOTS = 3
VMEM_BYTES = 24 * 1024 * 1024
F32 = jnp.float32
BF16 = jnp.bfloat16


def iota(shape, axis):
    return lax.broadcasted_iota(jnp.int32, shape, axis)


def onehot(mask):
    return jnp.where(mask, 1.0, 0.0).astype(BF16)


def split(value):
    high = value.astype(BF16)
    return high, (value - high.astype(F32)).astype(BF16)


def dot_nt(left, right):
    return lax.dot_general(left, right, (((1,), (1,)), ((), ())), preferred_element_type=F32)


def dot_nn(left, right):
    return lax.dot_general(left, right, (((1,), (0,)), ((), ())), preferred_element_type=F32)


def take_lanes(table, index):
    return jnp.take_along_axis(table, index, axis=1, mode="promise_in_bounds")


def gather_corners(field, connectivity, blocks, known=None):
    elements = connectivity.shape[1]
    rows = {}
    for c in range(3):
        for h in blocks:
            rows[c, h] = jnp.broadcast_to(field[c * FIELD_ROWS + h:c * FIELD_ROWS + h + 1], (CORNERS, LANES))
    parts = [[], [], []]
    for start in range(0, elements, LANES):
        index = connectivity[:, start:start + LANES]
        low, high = index & 127, index >> 7
        masks = {h: high == h for h in blocks}
        for c in range(3):
            if known is None:
                total = jnp.zeros((CORNERS, LANES), F32)
            else:
                total = known[c * CORNERS:(c + 1) * CORNERS, start:start + LANES]
            for h in blocks:
                total = jnp.where(masks[h], take_lanes(rows[c, h], low), total)
            parts[c].append(total)
    return [jnp.concatenate(part, axis=1) for part in parts]


def assemble(terms, connectivity, columns_ref=None):
    elements = connectivity.shape[1]
    high, low = connectivity >> 7, connectivity & 127
    upper = terms.astype(BF16).astype(F32)
    lower = terms - upper
    total = jnp.zeros((6 * FIELD_ROWS, LANES), F32)
    for k in range(CORNERS):
        mask = iota((FIELD_ROWS, elements), 0) == high[k:k + 1]
        pieces = [
            jnp.where(mask, part[c * CORNERS + k:c * CORNERS + k + 1], 0.0)
            for part in (upper, lower)
            for c in range(3)
        ]
        left = jnp.concatenate(pieces, axis=0).astype(BF16)
        if columns_ref is None:
            total = total + dot_nt(left, onehot(iota((LANES, elements), 0) == low[k:k + 1]))
        else:
            total = total + dot_nn(left, columns_ref[k])
    return total[:3 * FIELD_ROWS] + total[3 * FIELD_ROWS:]


def columns_kernel(connectivity_ref, after_ref, out_ref):
    del after_ref
    low = connectivity_ref[...] & 127
    for k in range(CORNERS):
        out_ref[k] = jnp.where(iota((LANES, low.shape[1]), 0) == low[k:k + 1], 1.0, 0.0).T.astype(BF16)


def matvec(stiffness, values):
    elements = stiffness.shape[2]
    parts = []
    for start in range(0, elements, 128):
        total = jnp.zeros((DOF, 128), F32)
        for b in range(DOF):
            total = total + stiffness[b, :, start:start + 128] * values[b // 8][b % 8:b % 8 + 1, start:start + 128]
        parts.append(total)
    return jnp.concatenate(parts, axis=1)


def put_ends(partial, odd, own_rows, swap_a_ref, swap_b_ref):
    pad = [jnp.zeros((5, LANES), F32)]
    first = jnp.concatenate([partial[c * FIELD_ROWS:c * FIELD_ROWS + 1] for c in range(3)] + pad, axis=0)
    over = jnp.concatenate(
        [partial[c * FIELD_ROWS + own_rows:c * FIELD_ROWS + own_rows + 1] for c in range(3)] + pad, axis=0)
    swap_a_ref[...] = jnp.where(odd, first, over)
    swap_b_ref[...] = jnp.where(odd, over, first)


def add_ends(partial, odd, own_rows, swap_a, swap_b):
    before = jnp.where(odd, swap_a, swap_b)
    after = jnp.where(odd, swap_b, swap_a)
    pieces = []
    for c in range(3):
        pieces += [
            before[c:c + 1],
            jnp.zeros((own_rows - 1, LANES), F32),
            after[c:c + 1],
            jnp.zeros((FIELD_ROWS - own_rows - 1, LANES), F32),
        ]
    return partial + jnp.concatenate(pieces, axis=0)


def own_mask(own_rows):
    return (iota((3 * FIELD_ROWS, LANES), 0) % FIELD_ROWS) < own_rows


def as_field(rows, own_rows):
    pieces = []
    for c in range(3):
        pieces += [rows[c:c + 1, h * LANES:(h + 1) * LANES] for h in range(own_rows)]
        pieces.append(jnp.zeros((FIELD_ROWS - own_rows, LANES), F32))
    return jnp.concatenate(pieces, axis=0)


def send_kernel(devices, per, odd_ref, pressure_hbm, owner_hbm, element_hbm, table_hbm, support_hbm, stiffness_hbm,
                out_ref, place_ref, pressure_ref, owner_ref, element_ref, table_ref, support_ref, diagonal_ref, sems):
    del odd_ref
    moves = [(owner_hbm, owner_ref), (element_hbm, element_ref), (table_hbm, table_ref), (pressure_hbm, pressure_ref),
             (support_hbm, support_ref)]
    copies = [pltpu.make_async_copy(source, target, sems.at[i]) for i, (source, target) in enumerate(moves)]
    for copy in copies:
        copy.start()
    for i in range(DOF):
        pltpu.make_async_copy(
            stiffness_hbm.at[i, pl.ds(i, 1)], diagonal_ref.at[pl.ds(i, 1)], sems.at[len(moves)]).start()
    for copy in copies:
        copy.wait()
    pltpu.make_async_copy(stiffness_hbm.at[0], diagonal_ref, sems.at[len(moves)]).wait()
    faces = pressure_ref.shape[0]
    target = owner_ref[...]
    named = iota((devices, faces), 0) == target
    named16 = onehot(named)
    blocks = range(0, faces, WIDE)
    upto = onehot(iota((WIDE, WIDE), 0) <= iota((WIDE, WIDE), 1))
    counts = dot_nn(jnp.concatenate([named16[:, start:start + WIDE] for start in blocks], axis=0), upto)
    before = jnp.zeros((devices, 1), F32)
    ranks = []
    for i, start in enumerate(blocks):
        count = counts[i * devices:(i + 1) * devices]
        here = jnp.where(named[:, start:start + WIDE], count + before, 0.0)
        ranks.append(jnp.sum(here, axis=0, keepdims=True))
        before = before + count[:, WIDE - 1:]
    rank = jnp.concatenate(ranks, axis=1).astype(jnp.int32) - 1
    group = jnp.zeros_like(rank)
    for i in range(1, GROUPS):
        group = group + (rank >= i * per).astype(jnp.int32)
    place = target * per + rank - group * per
    place_ref[...] = jnp.concatenate([place, group, jnp.zeros((6, faces), jnp.int32)], axis=0)
    chosen = onehot(iota((devices * per, faces), 0) == place)

    pad = jnp.zeros((LANES - GROUPS * DOF, table_ref.shape[1]), F32)
    table_high, table_low = split(jnp.concatenate([table_ref[...]] * GROUPS + [pad], axis=0))
    rows_high, rows_low = split(pressure_ref[...])
    projected = dot_nt(
        jnp.concatenate([table_high, table_low, table_high], axis=1),
        jnp.concatenate([rows_high, rows_high, rows_low], axis=1),
    )
    spread = [jnp.where(group == i, projected[i * DOF:(i + 1) * DOF], 0.0) for i in range(GROUPS)]
    spread.append(jnp.where(iota((8, faces), 0) == group, element_ref[...].astype(F32), 0.0))
    spread_high, spread_low = split(jnp.concatenate(spread, axis=0))
    sent = dot_nt(chosen, jnp.concatenate([spread_high, spread_low], axis=0))

    trace = jnp.sum(diagonal_ref[...]) + jnp.sum(support_ref[...])
    out_ref[...] = jnp.where(iota((devices * per, LANES), 1) == 125, trace, sent[:, :LANES] + sent[:, LANES:])


def load_kernel(devices, per, odd_ref, rows_ref, connectivity_ref, support_ref,
                partial_ref, swap_a_ref, swap_b_ref, weight_ref, scale_ref, code_ref, loads_ref):
    nodes = support_ref.shape[1]
    own_rows = nodes // LANES

    @pl.when(odd_ref[0] >= 0)
    def _():
        rows = rows_ref[...]
        arrived = rows.T
        codes = arrived[GROUPS * DOF:].astype(jnp.int32)
        code_ref[...] = codes
        slots = rows.shape[0]
        total = jnp.zeros((4 * 2 * DOF, WIDE), F32)
        for g in range(GROUPS):
            terms = arrived[g * DOF:(g + 1) * DOF]
            upper = terms.astype(BF16).astype(F32)
            both = jnp.concatenate([upper, terms - upper], axis=0)
            code = codes[g:g + 1]
            left = jnp.concatenate([jnp.where((code >> 8) == i, both, 0.0) for i in range(4)], axis=0).astype(BF16)
            total = total + dot_nt(left, onehot(iota((WIDE, slots), 0) == (code & 255)))
        for i in range(4):
            start = i * 2 * DOF
            loads_ref[:, i * WIDE:(i + 1) * WIDE] = total[start:start + DOF] + total[start + DOF:start + 2 * DOF]

    partial = assemble(loads_ref[...], connectivity_ref[...])
    partial_ref[...] = partial
    put_ends(partial, odd_ref[0] == 1, own_rows, swap_a_ref, swap_b_ref)
    trace = jnp.sum(rows_ref[:, 125:126]) * (1.0 / per)
    inverse = jnp.full((8, LANES), 3.0 * nodes * devices, F32) / jnp.full((8, LANES), trace, F32)
    scale_ref[...] = inverse
    weight_ref[...] = as_field(support_ref[...], own_rows) * inverse[:1, :1]


def inner_kernel(own_rows, partial_ref, connectivity_ref, after_ref, out_ref):
    del after_ref
    out_ref[...] = jnp.concatenate(
        gather_corners(partial_ref[...], connectivity_ref[...], range(1, own_rows)), axis=0)


def product_kernel(own_rows, odd_ref, partial_ref, swap_a_in, swap_b_in, weight_ref, scale_ref, connectivity_ref,
                   stiffness_ref, columns_ref, inner_ref, after_ref, field_ref, values_ref, forces_ref, next_ref, swap_a_ref, swap_b_ref):
    del after_ref
    odd = odd_ref[0] == 1

    @pl.when(odd_ref[0] >= 0)
    def _():
        field = add_ends(partial_ref[...], odd, own_rows, swap_a_in[...], swap_b_in[...])
        field_ref[...] = field
        values = gather_corners(field, connectivity_ref[...], (0, own_rows), inner_ref)
        values_ref[...] = jnp.concatenate(values, axis=0)
        forces_ref[...] = matvec(stiffness_ref, values)

    partial = assemble(forces_ref[...], connectivity_ref[...], columns_ref)
    partial = partial * scale_ref[:1, :1] + weight_ref[...] * field_ref[...]
    next_ref[...] = partial
    put_ends(partial, odd, own_rows, swap_a_ref, swap_b_ref)


def entries(pairs):
    lane = iota((1, LANES), 1)
    row = jnp.zeros((1, LANES), F32)
    for i, value in pairs:
        row = jnp.where(lane == i, value, row)
    return row


def share(value, norm):
    return jnp.full((1, LANES), value, F32) / jnp.maximum(jnp.full((1, LANES), norm, F32), 1e-30)


def lower_kernel(own_rows, weight_ref, scale_ref, first_ref, second_ref, values0_ref, values1_ref,
                 forces0_ref, forces1_ref, after_ref, own0_ref, own1_ref, turned_ref, numbers_ref):
    del after_ref
    own, weight = own_mask(own_rows), weight_ref[...]
    first, second = jnp.where(own, first_ref[...], 0.0), jnp.where(own, second_ref[...], 0.0)
    norm0 = jnp.sum(first * first)
    theta = share(jnp.sum(first * second), norm0)
    second = second - theta * first
    own0_ref[...], own1_ref[...] = first, second
    scale, part = scale_ref[:1, :1], theta[:, :1]
    values0, forces0 = values0_ref[...], forces0_ref[...]
    values1, forces1 = values1_ref[...] - part * values0, forces1_ref[...] - part * forces0
    turned_ref[...] = values1
    norm1 = jnp.sum(second * second)
    row = entries([
        (0, norm0),
        (1, jnp.sum(first * second)),
        (2, norm1),
        (6, jnp.sum(values0 * forces0) * scale + jnp.sum(weight * first * first)),
        (7, jnp.sum(values0 * forces1) * scale + jnp.sum(weight * first * second)),
        (8, jnp.sum(values1 * forces1) * scale + jnp.sum(weight * second * second)),
        (12, theta),
    ])
    numbers_ref[...] = jnp.concatenate(
        [row, share(1.0, norm0), share(1.0, norm1), jnp.zeros((5, LANES), F32)], axis=0)


def moment_kernel(own_rows, devices, odd_ref, partial_ref, swap_a_in, swap_b_in, weight_ref, scale_ref,
                  connectivity_ref, stiffness_ref, own0_ref, own1_ref, values0_ref, turned_ref, numbers_ref, inner_ref,
                  pick0_ref, pick1_ref, field_ref, values_ref, moments_ref):
    del pick0_ref, pick1_ref
    odd = odd_ref[0] == 1
    field = add_ends(partial_ref[...], odd, own_rows, swap_a_in[...], swap_b_in[...])
    field_ref[...] = field
    weight, scale = weight_ref[...], scale_ref[:1, :1]
    first, second = own0_ref[...], own1_ref[...]
    third = jnp.where(own_mask(own_rows), field, 0.0)
    phi = jnp.sum(first * third) * numbers_ref[1:2]
    psi = jnp.sum(second * third) * numbers_ref[2:3]
    third = third - psi * second - phi * first
    values0, values1 = values0_ref[...], turned_ref[...]
    values2 = jnp.concatenate(gather_corners(field, connectivity_ref[...], (0, own_rows), inner_ref), axis=0)
    values_ref[...] = values2
    values2 = values2 - psi[:, :1] * values1 - phi[:, :1] * values0
    forces2 = matvec(stiffness_ref, [values2[c * CORNERS:(c + 1) * CORNERS] for c in range(3)])
    weighted = weight * third
    row = numbers_ref[:1] + entries([
        (3, jnp.sum(first * third)),
        (4, jnp.sum(second * third)),
        (5, jnp.sum(third * third)),
        (9, jnp.sum(values0 * forces2) * scale + jnp.sum(first * weighted)),
        (10, jnp.sum(values1 * forces2) * scale + jnp.sum(second * weighted)),
        (11, jnp.sum(values2 * forces2) * scale + jnp.sum(third * weighted)),
        (13, psi),
        (14, phi),
    ])
    moments_ref[...] = jnp.broadcast_to(row, (devices, LANES))


def step_weights(rows):
    column = [rows[:, i:i + 1] for i in range(15)]
    norms, energies, (theta, psi, phi) = column[:6], column[6:12], column[12:]

    def square(matrix, y):
        total = y[0] * y[0] * matrix[0]
        if len(y) > 1:
            total = total + y[1] * (2.0 * y[0] * matrix[1] + y[1] * matrix[2])
        if len(y) > 2:
            total = total + y[2] * (2.0 * (y[0] * matrix[3] + y[1] * matrix[4]) + y[2] * matrix[5])
        return jnp.sum(total, axis=0, keepdims=True)

    norm0 = jnp.sum(norms[0], axis=0, keepdims=True)
    step0 = norm0 / jnp.sum(energies[0], axis=0, keepdims=True)
    residual = [1.0 - step0 * theta, -step0]
    norm1 = square(norms, residual)
    turn0 = norm1 / norm0
    direction = [residual[0] + turn0, -step0]
    step1 = norm1 / square(energies, direction)
    lead = 1.0 + turn0
    residual = [
        residual[0] - step1 * (lead * theta - step0 * phi),
        -step0 - step1 * (lead - step0 * psi),
        step1 * step0,
    ]
    norm2 = square(norms, residual)
    turn1 = norm2 / norm1
    direction = [residual[0] + turn1 * direction[0], residual[1] - turn1 * step0, residual[2]]
    step2 = norm2 / square(energies, direction)
    return [
        step0 + step1 * lead + step2 * (1.0 + turn1 * lead),
        -step1 * step0 - step2 * (step0 + step1 * lead + turn1 * step0),
        step2 * step1 * step0,
    ]


def spots_kernel(code_ref, after_ref, out_ref):
    del after_ref
    for i in range(out_ref.shape[0]):
        code = code_ref[GROUPS - out_ref.shape[0] + i:GROUPS - out_ref.shape[0] + i + 1]
        out_ref[i] = onehot(iota(out_ref.shape[1:], 0) == (code & 255))


def pick(values, code_ref, out_ref, blend, spots_ref=None):
    gathered, found = GROUPS, {}
    if spots_ref is not None:
        gathered = GROUPS - spots_ref.shape[0]
        halves = split(values)
        stack = jnp.concatenate(
            [half[:, i * WIDE:(i + 1) * WIDE] for i in range(values.shape[1] // WIDE) for half in halves], axis=0)
        for g in range(gathered, GROUPS):
            product = dot_nn(stack, spots_ref[g - gathered])
            high = code_ref[g:g + 1] >> 8
            total = jnp.zeros((DOF, code_ref.shape[1]), F32)
            for i in range(values.shape[1] // WIDE):
                part = product[i * 2 * DOF:i * 2 * DOF + DOF] + product[i * 2 * DOF + DOF:(i + 1) * 2 * DOF]
                total = jnp.where(high == i, part, total)
            found[g] = total
    for start in range(0, code_ref.shape[1], LANES):
        sections = []
        for g in range(GROUPS):
            if g >= gathered:
                sections.append(found[g][:, start:start + LANES])
                continue
            code = jnp.broadcast_to(code_ref[g:g + 1, start:start + LANES], (CORNERS, LANES))
            low, high = code & 127, code >> 7
            masks = [high == i for i in range(8)]
            for c in range(3):
                total = jnp.zeros((CORNERS, LANES), F32)
                for i in range(8):
                    tile = values[c * CORNERS:(c + 1) * CORNERS, i * LANES:(i + 1) * LANES]
                    total = jnp.where(masks[i], take_lanes(tile, low), total)
                sections.append(total)
        sections.append(jnp.zeros((CORNERS, LANES), F32))
        rows = pl.ds(start, LANES)
        out_ref[rows, :] = blend(jnp.concatenate(sections, axis=0).T, rows)


def pick_kernel(values_ref, code_ref, after_ref, out_ref):
    del after_ref
    pick(values_ref[...], code_ref, out_ref, lambda tile, rows: tile)


def blend_kernel(moments_ref, scale_ref, code_ref, spots_ref, pick0_ref, pick1_ref, values_ref,
                 weights_ref, out_ref):
    weights = step_weights(moments_ref[...])
    weights = [weight * scale_ref[:1, :1] for weight in weights]
    weights_ref[...] = jnp.concatenate([jnp.broadcast_to(weight, (8, LANES)) for weight in weights], axis=0)

    def blend(tile, rows):
        return weights[0] * pick0_ref[rows, :] + weights[1] * pick1_ref[rows, :] + weights[2] * tile

    pick(values_ref[...], code_ref, out_ref, blend, spots_ref)


def motion_kernel(own_rows, rows_ref, place_ref, table_ref, weights_ref, first_ref, second_ref, third_ref,
                  displacement_hbm, out_hbm, displacement_ref, out_ref, sems):
    field = weights_ref[:1] * first_ref[...] + weights_ref[8:9] * second_ref[...] + weights_ref[16:17] * third_ref[...]
    for c in range(3):
        for h in range(own_rows):
            displacement_ref[c:c + 1, h * LANES:(h + 1) * LANES] = field[c * FIELD_ROWS + h:c * FIELD_ROWS + h + 1]
    copies = [pltpu.make_async_copy(displacement_ref, displacement_hbm, sems.at[0])]
    copies[0].start()
    high, low = split(rows_ref[...].T)
    slots, faces = rows_ref.shape[0], place_ref.shape[1]
    place, group = place_ref[0:1], place_ref[1:2]
    found = dot_nn(jnp.concatenate([high, low], axis=0), onehot(iota((slots, faces), 0) == place))
    found = found[:LANES] + found[LANES:]
    owned = jnp.zeros((DOF, faces), F32)
    for g in range(GROUPS):
        owned = jnp.where(group == g, found[g * DOF:(g + 1) * DOF], owned)
    upper = owned.astype(BF16).astype(F32)
    lower = owned - upper
    parts = jnp.concatenate([upper, lower, upper], axis=0).T.astype(BF16)
    table_high, table_low = split(table_ref[...])
    right = jnp.concatenate([table_high, table_high, table_low], axis=0)
    for i, start in enumerate(range(0, faces, WIDE)):
        out_ref[start:start + WIDE, :] = dot_nn(parts[start:start + WIDE], right)
        copy = pltpu.make_async_copy(
            out_ref.at[pl.ds(start, WIDE)], out_hbm.at[pl.ds(start, WIDE)], sems.at[1 + i])
        copy.start()
        copies.append(copy)
    for copy in copies:
        copy.wait()


def call(kernel, outs, args, scalars=0, hbm=(), outs_hbm=(), scratch=(), time=1.0):
    in_specs = []
    for i in range(len(args)):
        if i < scalars:
            in_specs.append(pl.BlockSpec(memory_space=pltpu.SMEM))
        elif i in hbm:
            in_specs.append(pl.BlockSpec(memory_space=pltpu.HBM))
        else:
            in_specs.append(pl.BlockSpec(memory_space=pltpu.VMEM))
    return pl.pallas_call(
        kernel,
        name=getattr(kernel, "func", kernel).__name__,
        out_shape=[jax.ShapeDtypeStruct(shape, dtype) for shape, dtype in outs],
        in_specs=in_specs,
        out_specs=[
            pl.BlockSpec(memory_space=pltpu.HBM if i in outs_hbm else pltpu.VMEM) for i in range(len(outs))
        ],
        scratch_shapes=list(scratch),
        cost_estimate=pl.CostEstimate(flops=int(time * 1e9), transcendentals=0, bytes_accessed=int(time * 1e6)),
        compiler_params=pltpu.CompilerParams(vmem_limit_bytes=VMEM_BYTES),
    )(*[pltpu.with_memory_space_constraint(arg, pltpu.HBM) if i in hbm else arg for i, arg in enumerate(args)])


def shards(pressure, face_owner, face_element, shape_table, stiffness, connectivity, support):
    devices = lax.axis_size(AXES)
    faces = pressure.shape[0]
    elements = stiffness.shape[2]
    nodes = support.shape[1]
    own_rows = nodes // LANES
    capacity = max(2, (5 * faces + 2 * devices - 1) // (2 * devices))
    per = (capacity + GROUPS - 1) // GROUPS
    slots = devices * per
    odd = (lax.axis_index(AXES) % 2).astype(jnp.int32).reshape(1)
    evens = [(i, i + 1) for i in range(0, devices - 1, 2)]
    odds = [(i, i + 1) for i in range(1, devices - 1, 2)]
    pairs_a = evens + [(j, i) for i, j in evens]
    pairs_b = odds + [(j, i) for i, j in odds]

    def swap(a, b):
        return lax.ppermute(a, AXES, pairs_a), lax.ppermute(b, AXES, pairs_b)

    def everywhere(rows):
        return lax.all_to_all(rows, AXES, split_axis=0, concat_axis=0, tiled=True)

    field = ((3 * FIELD_ROWS, LANES), F32)
    values = ((DOF, elements), F32)
    ends = ((8, LANES), F32)
    block = ((slots, LANES), F32)
    sent, place = call(
        functools.partial(send_kernel, devices, per),
        [block, ((8, faces), jnp.int32)],
        (odd, pressure, face_owner.reshape(1, faces), face_element.reshape(1, faces), shape_table, support, stiffness),
        scalars=1,
        hbm=range(1, 7),
        scratch=(
            pltpu.VMEM(pressure.shape, F32),
            pltpu.VMEM((1, faces), jnp.int32),
            pltpu.VMEM((1, faces), jnp.int32),
            pltpu.VMEM(shape_table.shape, F32),
            pltpu.VMEM(support.shape, F32),
            pltpu.VMEM((DOF, elements), F32),
            pltpu.SemaphoreType.DMA((6,)),
        ),
    )
    arrived = everywhere(sent)
    partial, end_a, end_b, weight, scale, codes = call(
        functools.partial(load_kernel, devices, per),
        [field, ends, ends, field, ends, ((8, slots), jnp.int32)],
        (odd, arrived, connectivity, support),
        scalars=1,
        scratch=(pltpu.VMEM((DOF, elements), F32),),
    )
    stage = (
        functools.partial(product_kernel, own_rows),
        [field, values, values, field, ends, ends],
    )
    end_a, end_b = swap(end_a, end_b)
    (inner,) = call(
        functools.partial(inner_kernel, own_rows), [values], (partial, connectivity, end_a), time=0.1)
    (columns,) = call(
        columns_kernel, [((CORNERS, elements, LANES), BF16)], (connectivity, end_a), time=0.1)
    first, values0, forces0, partial, end_a, end_b = call(
        *stage, (odd, partial, end_a, end_b, weight, scale, connectivity, stiffness, columns, inner, weight), scalars=1)
    end_a, end_b = swap(end_a, end_b)
    (inner,) = call(
        functools.partial(inner_kernel, own_rows), [values], (partial, connectivity, end_a), time=0.1)
    (spots,) = call(spots_kernel, [((SPOTS, WIDE, slots), BF16)], (codes, end_a), time=0.1)
    (pick0,) = call(pick_kernel, [block], (values0, codes, end_a), time=0.1)
    second, values1, forces1, partial, end_a, end_b = call(
        *stage, (odd, partial, end_a, end_b, weight, scale, connectivity, stiffness, columns, inner, spots), scalars=1)
    end_a, end_b = swap(end_a, end_b)
    (inner,) = call(
        functools.partial(inner_kernel, own_rows), [values], (partial, connectivity, end_a), time=0.1)
    (pick1,) = call(pick_kernel, [block], (values1, codes, end_a), time=0.1)
    own0, own1, turned, numbers = call(
        functools.partial(lower_kernel, own_rows),
        [field, field, values, ends],
        (weight, scale, first, second, values0, values1, forces0, forces1, end_a),
        time=0.1,
    )
    third, values2, moments = call(
        functools.partial(moment_kernel, own_rows, devices),
        [field, values, ((devices, LANES), F32)],
        (odd, partial, end_a, end_b, weight, scale, connectivity, stiffness, own0, own1, values0, turned, numbers, inner,
         pick0, pick1),
        scalars=1,
    )
    moments = everywhere(moments)
    weights, leaving = call(
        blend_kernel,
        [((24, LANES), F32), block],
        (moments, scale, codes, spots, pick0, pick1, values2),
    )
    returned = everywhere(leaving)
    return call(
        functools.partial(motion_kernel, own_rows),
        [((3, nodes), F32), ((faces, LANES), F32)],
        (returned, place, shape_table, weights, first, second, third),
        outs_hbm=(0, 1),
        scratch=(
            pltpu.VMEM((3, nodes), F32),
            pltpu.VMEM((faces, LANES), F32),
            pltpu.SemaphoreType.DMA((1 + faces // WIDE,)),
        ),
    )


def solution(mesh):
    in_specs = (
        P(AXES, None),
        P(AXES, None),
        P(AXES),
        P(),
        P(None, None, AXES),
        P(None, AXES),
        P(None, AXES),
    )
    out_specs = (P(None, AXES), P(AXES, None))
    return jax.shard_map(shards, mesh=mesh, in_specs=in_specs, out_specs=out_specs, check_vma=False)
```
